32 devices in a mesh: rep: 16 (over z, x, core), exp: 2 (over y).
Axes of the slice: x: 2, y: 2, z: 4, core: 2. Of those that a mesh axis runs over, the one named last changes fastest.
Arguments:
- tokens: bfloat16 [25216, 384], P(('rep', 'exp')), may hold values from -6 to 6
- routes: int32 [25216, 2], P(('rep', 'exp')), may hold values from 0 to 7, all different within a row; in each aligned block of 788 rows (0 to 787, 788 to 1575, ...) at most 394 rows name the same one
- norm_gains: float32 [4, 384], replicated, may hold values from 0.25 to 1.75
- attn_qkv: bfloat16 [2, 384, 1152], replicated, may hold values from -0.3125 to 0.3125
- attn_out: bfloat16 [2, 384, 384], replicated, may hold values from -1.75 to 1.75
- mlp_in: bfloat16 [384, 1536], replicated, may hold values from -0.3125 to 0.3125
- mlp_out: bfloat16 [1536, 384], replicated, may hold values from -0.3125 to 0.3125
- router: bfloat16 [384, 8], replicated, may hold values from -0.21875 to 0.21875
- experts_in: bfloat16 [8, 384, 1536], P('exp'), may hold values from -0.3125 to 0.3125
- experts_out: bfloat16 [8, 1536, 384], P('exp'), may hold values from -0.3125 to 0.3125
- cotangent: bfloat16 [25216, 384], P(('rep', 'exp')), may hold values from -6 to 6
Outputs:
- activations: bfloat16 [25216, 384], P(('rep', 'exp'))
- input_grad: float32 [25216, 384], P(('rep', 'exp'))
- qkv_grad: float32 [2, 384, 1152], replicated
- proj_grad: float32 [2, 384, 384], replicated
- gain_grad: float32 [4, 384], replicated
- mlp_in_grad: float32 [384, 1536], replicated
- mlp_out_grad: float32 [1536, 384], replicated
- router_grad: float32 [384, 8], replicated
- experts_in_grad: float32 [8, 384, 1536], P('exp', None, 'rep')
- experts_out_grad: float32 [8, 1536, 384], P('exp', 'rep')
The draws below stay inside these ranges and needn't reach their ends.
Inputs may be any that keep to these rules, and one draw needn't show every extreme that they name: `routes`: each row names 2 different experts; of the 788 rows of one device no expert is named by more than 394 rows, and in every draw some expert is named by exactly 394 rows of some device.
All inputs are finite; a program needn't handle non-finite values.
Results may differ from the reference program's by a relative error of at most 0.025.
Values may be sent and summed in bfloat16 or wider, within the bound.
A program may use at most 320 MiB of HBM per device.

```python
import math
import jax
import jax.numpy as jnp
import numpy as np
from jax import lax

D = 384
HEADS = 6
FF = 1536
PATCHES = 197
TOP = 2
EXPERTS = 8
TOK_DEV = 788
TOKENS = 25216
CAP = 394


def block_scale(key, shape, split, low, largest):
    level = 1.0
    for position, blocks in split:
        draws = jax.random.uniform(jax.random.fold_in(jax.random.fold_in(key, 6), position), (blocks,), jnp.float32, low / len(split), largest / len(split))
        level = level * jnp.repeat(jnp.exp(draws), shape[position] // blocks).reshape((-1,) + (1,) * (len(shape) - 1 - position))
    return level


def deal_out(key, own, number, rows, amount, top, limit, skew):
    ranking = jax.random.permutation(key, amount)
    heavy_load, ordinary = portions_of(amount, rows * top, limit, skew, True), portions_of(amount, rows * top, limit, skew, False)
    places = jnp.arange(amount)

    def named(sizes, offset_by):
        used = int((sizes > 0).sum())
        fixed = max(1, used // 4)
        moved = fixed + (places - fixed + offset_by * (used - fixed)) % max(1, amount - fixed)
        return jnp.zeros((amount,), jnp.int32).at[ranking[jnp.where(places < fixed, places, moved)]].set(jnp.asarray(sizes, jnp.int32))

    sizes = jnp.where(number % 4 == 0, named(heavy_load, number // 4), named(ordinary, number - number // 4 - 1))
    mixed = jax.random.permutation(jax.random.fold_in(own, 3), amount)
    source_of, receiver = mixed[0:amount // 2 * 2:2], mixed[1:amount // 2 * 2:2]
    room = jnp.minimum(sizes[source_of] - 1, limit - sizes[receiver]) // 2
    room = jnp.where((source_of == ranking[0]) | (receiver == ranking[0]) | (sizes[receiver] == 0), 0, jnp.maximum(room, 0))
    moved = jax.random.randint(jax.random.fold_in(own, 4), (amount // 2,), 0, 1 << 20) % (room + 1)
    sizes = sizes.at[source_of].add(-moved).at[receiver].add(moved)
    items = jnp.searchsorted(jnp.cumsum(sizes), jnp.arange(rows * top), side="right").astype(jnp.int32)
    listing = items.reshape(top, rows).T
    listing = listing[jax.random.permutation(jax.random.fold_in(own, 1), rows)]
    offset_by = jax.random.randint(jax.random.fold_in(own, 2), (rows, 1), 0, top)
    return jnp.take_along_axis(listing, (jnp.arange(top)[None, :] + offset_by) % top, axis=1)


def portions_of(number_of, total, most, lean, full):
    weights = [(1 << 20) // math.isqrt(grade ** lean) + 1 for grade in range(1, number_of + 1)]
    largest = most if full else min(most, max(-(-total // number_of), total * weights[0] // sum(weights)))
    least = 1 if total - largest >= number_of - 1 else 0
    holding, spare = [largest] + [least] * (number_of - 1), total - largest - least * (number_of - 1)
    while spare > 0:
        candidates = [i for i in range(1, number_of) if holding[i] < largest] or [i for i in range(1, number_of) if holding[i] < most]
        pool, left = sum([weights[i] for i in candidates]), spare
        for i in candidates:
            addition = min(most - holding[i], max(1, left * weights[i] // pool), spare)
            holding[i] = holding[i] + addition
            spare = spare - addition
    return np.array(holding)


def normal_values(rng, shape, scale, reach, split=(), kind=jnp.bfloat16):
    entries = scale * jax.random.normal(rng, shape, jnp.float32)
    if split:
        entries = entries * block_scale(rng, shape, split, -0.22, 0.18)
    return jnp.clip(entries, -reach, reach).astype(kind)


def setup_inputs(seed: int = 0) -> dict:
    key_list = jax.random.split(jax.random.key(seed), 12)
    tokens = normal_values(key_list[0], (TOKENS, D), 1.0, 6.0, ((0, 32),))
    routes_keys = jax.random.split(jax.random.fold_in(key_list[1], 1), TOKENS // TOK_DEV)
    routes_turns = jax.random.permutation(jax.random.fold_in(key_list[1], 3), TOKENS // TOK_DEV)
    routes = jax.vmap(lambda own, number: deal_out(jax.random.fold_in(key_list[1], 2), own, number, TOK_DEV, EXPERTS, TOP, CAP, 1))(routes_keys, routes_turns).reshape((TOKENS, TOP))
    norm_gains = jnp.clip(1.0 + 0.15 * jax.random.normal(key_list[2], (4, D), jnp.float32), 0.25, 1.75)
    attn_qkv = normal_values(key_list[3], (2, D, 3 * D), D ** -0.5, 0.3125)
    attn_out = normal_values(key_list[4], (2, D, D), (D // 32) ** -0.5, 1.75)
    mlp_in = normal_values(key_list[5], (D, FF), D ** -0.5, 0.3125)
    mlp_out = normal_values(key_list[6], (FF, D), (FF // 4) ** -0.5, 0.3125)
    router = normal_values(key_list[7], (D, EXPERTS), (2 * D) ** -0.5, 0.21875)
    experts_in = normal_values(key_list[8], (EXPERTS, D, FF), D ** -0.5, 0.3125, ((0, 2),))
    experts_out = normal_values(key_list[9], (EXPERTS, FF, D), (FF // 4) ** -0.5, 0.3125, ((0, 2),))
    cotangent = normal_values(key_list[10], (TOKENS, D), 1.0, 6.0, ((0, 32),))
    return {"tokens": tokens, "routes": routes, "norm_gains": norm_gains, "attn_qkv": attn_qkv, "attn_out": attn_out, "mlp_in": mlp_in, "mlp_out": mlp_out, "router": router, "experts_in": experts_in, "experts_out": experts_out, "cotangent": cotangent}


@jax.custom_vjp
def low(v):
    return lax.optimization_barrier(v.astype(jnp.bfloat16)).astype(jnp.float32)

@jax.custom_vjp
def low_back(v):
    return v

def low_keep(v):
    return (low(v), None)

def low_pass(kept, grad):
    return (grad,)

def back_keep(v):
    return (v, None)

def back_low(kept, grad):
    return (low(grad),)
low.defvjp(low_keep, low_pass)
low_back.defvjp(back_keep, back_low)
highest = lax.Precision.HIGHEST
eps_norm = 1e-06

def matmul(left, right):
    return jnp.dot(left, right, precision=highest)

def layer_norm(values, norm_gain):
    centred = values - lax.optimization_barrier(jnp.mean(values, axis=-1, keepdims=True))
    spread = lax.optimization_barrier(jnp.mean(centred * centred, axis=-1, keepdims=True))
    return centred * lax.rsqrt(spread + eps_norm) * norm_gain

def slot_positions(routes):
    flat_routes = routes.reshape(-1)
    onehot = (flat_routes[:, None] == jnp.arange(EXPERTS, dtype=jnp.int32)[None, :]).astype(jnp.int32)
    before = jnp.cumsum(onehot, axis=0, dtype=jnp.int32) - onehot
    slot_index = lax.optimization_barrier(jnp.sum(before * onehot, axis=1, dtype=jnp.int32))
    return flat_routes * CAP + slot_index

def attention(values, norm_gain, w_qkv, w_out):
    row_count, model_width = values.shape
    head_size = model_width // HEADS
    normed = low(layer_norm(values, norm_gain))
    qkv_rows = low(low_back(matmul(normed, w_qkv)))
    heads_view = qkv_rows.reshape(row_count // PATCHES, PATCHES, 3, HEADS, head_size)
    scores = jnp.einsum('iqhc,ikhc->ihqk', heads_view[:, :, 0], heads_view[:, :, 1], precision=highest)
    scores = low_back(scores * head_size ** (-0.5))
    soft_weights = low(jax.nn.softmax(scores, axis=-1))
    mixed_heads = jnp.einsum('ihqk,ikhc->iqhc', soft_weights, heads_view[:, :, 2], precision=highest)
    mixed_heads = low(low_back(mixed_heads.reshape(row_count, model_width)))
    return values + low_back(matmul(mixed_heads, w_out))

def feed_forward(values, norm_gain, w_in, w_out):
    normed = low(layer_norm(values, norm_gain))
    hidden = low_back(matmul(normed, w_in))
    activated = low(jax.nn.gelu(hidden, approximate=False))
    return values + low_back(matmul(activated, w_out))

def experts_layer(values, routes, norm_gain, router, w_in, w_out):
    model_width = values.shape[1]
    normed = low(layer_norm(values, norm_gain))
    logits = low_back(matmul(normed, router))
    picked = jnp.take_along_axis(logits, routes, axis=1)
    gate_weights = jax.nn.softmax(picked, axis=-1)
    positions = slot_positions(routes)
    pair_rows = low_back(jnp.repeat(normed, TOP, axis=0))
    buffer = jnp.zeros((EXPERTS * CAP, model_width), normed.dtype).at[positions].set(pair_rows)
    buffer = buffer.reshape(EXPERTS, CAP, model_width)
    hidden = low_back(jnp.einsum('ecd,edf->ecf', buffer, w_in, precision=highest))
    activated = low(jax.nn.gelu(hidden, approximate=False))
    expert_out = low(low_back(jnp.einsum('ecf,efd->ecd', activated, w_out, precision=highest)))
    pair_out = expert_out.reshape(EXPERTS * CAP, model_width)[positions].reshape(-1, TOP, model_width)
    return values + lax.optimization_barrier(jnp.sum(gate_weights[:, :, None] * pair_out, axis=1))

def device_block(values, routes, params):
    norm_gains, attn_qkv, attn_out, mlp_in, mlp_out, router, experts_in, experts_out = params
    current = attention(values, norm_gains[0], attn_qkv[0], attn_out[0])
    current = feed_forward(current, norm_gains[1], mlp_in, mlp_out)
    current = attention(current, norm_gains[2], attn_qkv[1], attn_out[1])
    return experts_layer(current, routes, norm_gains[3], router, experts_in, experts_out)

def reference(tokens, routes, norm_gains, attn_qkv, attn_out, mlp_in, mlp_out, router, experts_in, experts_out, cotangent):
    params = tuple((weight.astype(jnp.float32) for weight in (norm_gains, attn_qkv, attn_out, mlp_in, mlp_out, router, experts_in, experts_out)))
    blocks = TOKENS // TOK_DEV
    route_blocks = routes.reshape(blocks, TOK_DEV, TOP)

    def forward(values, weights):

        def block_step(block_pair):
            return device_block(block_pair[0], block_pair[1], weights)
        result = lax.map(jax.checkpoint(block_step), (values.reshape(blocks, TOK_DEV, D), route_blocks))
        return result.reshape(TOKENS, D)
    output, pullback = jax.vjp(forward, tokens.astype(jnp.float32), params)
    input_grad, grads = pullback(cotangent.astype(jnp.float32))
    gain_grad, qkv_grad, proj_grad, mlp_in_grad, mlp_out_grad, router_grad, experts_in_grad, experts_out_grad = grads
    return (output.astype(jnp.bfloat16), input_grad, qkv_grad, proj_grad, gain_grad, mlp_in_grad, mlp_out_grad, router_grad, experts_in_grad, experts_out_grad)
```

```python
import functools

import jax
import jax.numpy as jnp
from jax import lax
from jax.experimental import pallas as pl
from jax.experimental.pallas import tpu as pltpu
from jax.sharding import PartitionSpec as P

F32 = jnp.float32
BF = jnp.bfloat16
HEADS = 6
PATCHES = 197
ROWS = 208
EPS = 1e-6
TILE = 128
CHUNK = 1024
D = 384
FF = 1536
VMEM = pl.BlockSpec(memory_space=pltpu.VMEM)


def dot(a, b):
    return lax.dot_general(a, b, (((1,), (0,)), ((), ())), preferred_element_type=F32)


def dot_t(a, b):
    return lax.dot_general(a, b, (((1,), (1,)), ((), ())), preferred_element_type=F32)


def t_dot(a, b):
    return lax.dot_general(a, b, (((0,), (0,)), ((), ())), preferred_element_type=F32)


def norm_parts(x):
    centred = x - jnp.mean(x, axis=-1, keepdims=True)
    rstd = lax.rsqrt(jnp.mean(centred * centred, axis=-1, keepdims=True) + EPS)
    return centred * rstd, rstd


def norm_back(grad, x, gain):
    xh, rstd = norm_parts(x)
    dxh = grad * gain
    inner = dxh - jnp.mean(dxh, axis=-1, keepdims=True)
    return rstd * (inner - xh * jnp.mean(dxh * xh, axis=-1, keepdims=True)), grad * xh


def gelu_parts(h):
    t = 1.0 / (1.0 + (0.3275911 * 0.7071067811865476) * jnp.abs(h))
    e = jnp.exp(-0.5 * h * h)
    poly = t * (
        0.254829592
        + t * (-0.284496736 + t * (1.421413741 + t * (-1.453152027 + t * 1.061405429)))
    )
    tail = 0.5 * poly * e
    phi = jnp.where(h >= 0, 1.0 - tail, tail)
    return h * phi, phi + h * (0.3989422804014327 * e)


def lane_low(rows):
    return lax.broadcasted_iota(jnp.int32, (rows, 128), 1) < 64


def fwd_kernel(
    x_ref, gains, wqkv, wo, win, wout,
    x1_ref, x2_ref, x3_ref, qkv1_ref, qkv2_ref, o1_ref, o2_ref, p1_ref, p2_ref, u_ref, gp_ref, c_ref,
):
    ib = x_ref.shape[0]
    m = ib * ROWS
    lo = lane_low(ROWS)
    valid = lax.broadcasted_iota(jnp.int32, (ROWS, ROWS), 1) < PATCHES

    def attend(x, layer, gain, qkv_ref, o_ref, p_ref):
        a = (norm_parts(x)[0] * gain).astype(BF)
        qkv_ref[...] = dot(a, wqkv[layer]).astype(BF).reshape(ib, ROWS, 3 * D)
        for i in range(ib):
            for pair in range(HEADS // 2):
                at = 128 * pair
                q = qkv_ref[i, :, at : at + 128] * BF(0.125)
                k = qkv_ref[i, :, D + at : D + at + 128]
                w = qkv_ref[i, :, 2 * D + at : 2 * D + at + 128]
                mixed = []
                for h in range(2):
                    qm = jnp.where(lo if h == 0 else ~lo, q, BF(0))
                    s = jnp.where(valid, dot_t(qm, k), -1e30)
                    s = jnp.exp(s - jnp.max(s, axis=-1, keepdims=True))
                    p = (s * (1.0 / jnp.sum(s, axis=-1, keepdims=True))).astype(BF)
                    p_ref[i, 2 * pair + h] = p
                    mixed.append(dot(p, w))
                o_ref[i, :, at : at + 128] = jnp.where(lo, mixed[0], mixed[1]).astype(BF)
        return x + dot(o_ref[...].reshape(m, D), wo[layer])

    x0 = x_ref[...].astype(F32).reshape(m, D)
    x1 = attend(x0, 0, gains[0:1], qkv1_ref, o1_ref, p1_ref)
    x1_ref[...] = x1.reshape(ib, ROWS, D)
    b = (norm_parts(x1)[0] * gains[1:2]).astype(BF)
    x2 = x1
    for f in range(0, FF, 512):
        u, gp = gelu_parts(dot(b, win[:, f : f + 512]))
        u = u.astype(BF)
        u_ref[:, :, f : f + 512] = u.reshape(ib, ROWS, 512)
        gp_ref[:, :, f : f + 512] = gp.astype(BF).reshape(ib, ROWS, 512)
        x2 = x2 + dot(u, wout[f : f + 512])
    x2_ref[...] = x2.reshape(ib, ROWS, D)
    x3 = attend(x2, 1, gains[2:3], qkv2_ref, o2_ref, p2_ref)
    x3_ref[...] = x3.reshape(ib, ROWS, D)
    c_ref[...] = (norm_parts(x3)[0] * gains[3:4]).astype(BF).reshape(ib, ROWS, D)


def dense_forward(x, gains, wqkv, wo, win, wout):
    n = x.shape[0]
    ib = 2 if n % 2 == 0 else 1

    def out(*shape, dtype=BF):
        return jax.ShapeDtypeStruct((n,) + shape, dtype)

    def block(shape):
        return pl.BlockSpec((ib,) + tuple(shape[1:]), lambda i: (i,) + (0,) * (len(shape) - 1))

    outs = [out(ROWS, D, dtype=F32)] * 3 + [out(ROWS, 3 * D)] * 2 + [out(ROWS, D)] * 2
    outs += [out(HEADS, ROWS, ROWS)] * 2 + [out(ROWS, FF)] * 2 + [out(ROWS, D)]
    return pl.pallas_call(
        fwd_kernel,
        grid=(n // ib,),
        out_shape=outs,
        in_specs=[block(x.shape)] + [VMEM] * 5,
        out_specs=[block(o.shape) for o in outs],
        compiler_params=pltpu.CompilerParams(vmem_limit_bytes=60 << 20),
        name="dense_forward",
    )(x, gains, wqkv, wo, win, wout)


def gate_rows(router_t, c, routes):
    logits = dot_t(router_t, c)
    expert = lax.broadcasted_iota(jnp.int32, logits.shape, 0)
    first, second = expert == routes[0:1], expert == routes[1:2]
    diff = jnp.sum(jnp.where(first, logits, 0.0) - jnp.where(second, logits, 0.0), axis=0, keepdims=True)
    return 1.0 / (1.0 + jnp.exp(-diff)), 1.0 / (1.0 + jnp.exp(diff)), first, second


def experts_kernel(groups, local, exp_axis, *refs):
    c_refs, g_refs, r_refs = refs[:groups], refs[groups : 2 * groups], refs[2 * groups : 3 * groups]
    router_t, win, wout = refs[3 * groups : 3 * groups + 3]
    outs = refs[3 * groups + 3 :]
    eg_ref, y_refs, d_refs, delta_refs = outs[0], outs[1 : groups + 1], outs[groups + 1 : 2 * groups + 1], outs[2 * groups + 1 : 3 * groups + 1]
    ci, g4, rows, cols, slots, acc_out, acc_in, u_scr, gp_scr, back, counts = outs[3 * groups + 1 :]
    n_tok = c_refs[0].shape[0]
    total = groups * n_tok
    step = pl.program_id(0)
    first_expert = lax.axis_index(exp_axis) * local

    @pl.when(step == 0)
    def _():
        for s in range(groups):
            at = s * n_tok
            ci[at : at + n_tok, 0:D] = c_refs[s][...]
            g4[at : at + n_tok] = g_refs[s][...]
        routes = jnp.concatenate([r[0:2] for r in r_refs], axis=1)
        g0, g1, _, _ = gate_rows(router_t[...], ci[:, 0:D], routes)
        mine = first_expert + lax.broadcasted_iota(jnp.int32, (8, total), 0)
        inside = lax.broadcasted_iota(jnp.int32, (8, total), 0) < local
        is0, is1 = (mine == routes[0:1]) & inside, (mine == routes[1:2]) & inside
        member = jnp.where(is0 | is1, 1.0, 0.0)
        lane = lax.broadcasted_iota(jnp.int32, (8, total), 1)
        upto = member
        shift = 1
        while shift < total:
            upto = upto + jnp.where(lane >= shift, pltpu.roll(upto, shift, 1), 0.0)
            shift *= 2
        position = jnp.where(member > 0, upto - 1.0, -1.0)
        rows[0:8] = position
        base = jnp.int32(0)
        starts = []
        for e in range(local):
            n = jnp.sum(member[e : e + 1]).astype(jnp.int32)
            tiles = (n + TILE - 1) // TILE
            counts[e] = tiles
            counts[8 + e] = base
            starts.append((base * TILE).astype(F32))
            base = base + tiles
        counts[16] = base
        start = jnp.zeros((8, total), F32)
        expert_row = lax.broadcasted_iota(jnp.int32, (8, total), 0)
        for e in range(local):
            start = jnp.where(expert_row == e, starts[e], start)
        slot = start + position
        slot0 = jnp.sum(jnp.where(is0, slot + 1.0, 0.0), axis=0, keepdims=True) - 1.0
        slot1 = jnp.sum(jnp.where(is1, slot + 1.0, 0.0), axis=0, keepdims=True) - 1.0
        gates = jnp.where(is0, g0, jnp.where(is1, g1, 0.0))
        sign = jnp.where(is0, 1.0, jnp.where(is1, -1.0, 0.0))
        slot_rows = jnp.where(expert_row == 0, slot0, jnp.where(expert_row == 1, slot1, 0.0))
        stacked = jnp.concatenate([gates, sign, slot_rows, jnp.zeros((104, total), F32)], axis=0)
        lane128 = lax.broadcasted_iota(jnp.int32, (128, 128), 1)
        for at in range(0, total, 128):
            col = stacked[:, at : at + 128].T
            cols[at : at + 128] = col
            low = col - col.astype(BF).astype(F32)
            info = jnp.where(lane128 < 16, col, jnp.where(lane128 < 24, pltpu.roll(low, 16, 1), 0.0))
            ci[at : at + 128, D : D + 128] = info.astype(BF)

    acc_out[...] = jnp.zeros_like(acc_out)
    acc_in[...] = jnp.zeros_like(acc_in)
    position = rows[pl.ds(step, 1)]
    lane = lax.broadcasted_iota(jnp.int32, (TILE, 128), 1)

    def tile(j, _):
        slot = (j * TILE + lax.broadcasted_iota(jnp.int32, (TILE, total), 0)).astype(F32)
        pick = jnp.where(position == slot, 1.0, 0.0).astype(BF)
        xi = dot(pick, ci[...])
        g4r = dot(pick, g4[...])
        x = xi[:, 0:D].astype(BF)
        info = xi[:, D : D + 128]
        gate = jnp.sum(jnp.where((lane == step) | (lane == step + 16), info, 0.0), axis=-1, keepdims=True)
        sign = jnp.sum(jnp.where(lane == step + 8, info, 0.0), axis=-1, keepdims=True)
        dy = (gate * g4r).astype(BF)
        for f in range(0, FF, 512):
            u, gp = gelu_parts(dot(x, win[0, :, f : f + 512]))
            u_scr[:, f : f + 512] = u.astype(BF)
            gp_scr[:, f : f + 512] = gp.astype(BF)
        ey = dot(u_scr[...], wout[0]).astype(BF).astype(F32)
        dg = sign * jnp.sum(g4r * ey, axis=-1, keepdims=True)
        acc_out[...] += t_dot(u_scr[...], dy)
        for f in range(0, FF, 512):
            du = dot_t(dy, wout[0, f : f + 512])
            gp_scr[:, f : f + 512] = (du * gp_scr[:, f : f + 512].astype(F32)).astype(BF)
        dcp = dot_t(gp_scr[...], win[0])
        acc_in[...] += t_dot(gp_scr[...], x)
        at = pl.multiple_of((counts[8 + step] + j) * TILE, TILE)
        slots[pl.ds(at, TILE), 0:D] = (gate * ey).astype(BF)
        slots[pl.ds(at, TILE), D : 2 * D] = dcp.astype(BF)
        low = dg - dg.astype(BF).astype(F32)
        slots[pl.ds(at, TILE), 2 * D : 2 * D + 128] = jnp.where(lane == 0, dg, jnp.where(lane == 1, low, 0.0)).astype(BF)
        return 0

    lax.fori_loop(0, counts[step], tile, 0)
    eg_ref[0, 0] = acc_in[...].astype(BF)
    eg_ref[0, 1] = acc_out[...].astype(BF)

    @pl.when(step == local - 1)
    def _():
        used = counts[16]
        chunks = (used * TILE + CHUNK - 1) // CHUNK

        def clear(j, _):
            at = pl.multiple_of(j * TILE, TILE)
            slots[pl.ds(at, TILE)] = jnp.zeros((TILE, 2 * D + 128), BF)
            return 0

        lax.fori_loop(used, chunks * (CHUNK // TILE), clear, 0)
        lane_chunk = lax.broadcasted_iota(jnp.int32, (ROWS, CHUNK), 1)

        for s in range(groups):
            for b in range(n_tok // ROWS):
                at = s * n_tok + b * ROWS
                slot0, slot1 = cols[at : at + ROWS, 16:17], cols[at : at + ROWS, 17:18]
                back[...] = jnp.zeros_like(back)

                def gather(j, _):
                    slot = (j * CHUNK + lane_chunk).astype(F32)
                    pick = jnp.where((slot0 == slot) | (slot1 == slot), 1.0, 0.0).astype(BF)
                    back[...] += dot(pick, slots[pl.ds(pl.multiple_of(j * CHUNK, CHUNK), CHUNK)])
                    return 0

                lax.fori_loop(0, chunks, gather, 0)
                y_refs[s][b * ROWS : (b + 1) * ROWS] = back[:, 0:D].astype(BF)
                d_refs[s][b * ROWS : (b + 1) * ROWS] = back[:, D : 2 * D].astype(BF)
                cols[at : at + ROWS] = back[:, 2 * D : 2 * D + 128]
        for at in range(0, total, 128):
            rows[:, at : at + 128] = cols[at : at + 128].T[0:8]
        for s in range(groups):
            delta_refs[s][...] = rows[:, s * n_tok : (s + 1) * n_tok]


def experts_all(cs, gs, rs, router_t, win, wout, slots_most):
    groups = len(cs)
    local = win.shape[0]
    n_tok = cs[0].shape[0]
    total = groups * n_tok
    room = -(-(slots_most + local * TILE) // CHUNK) * CHUNK

    def full(shape):
        return pl.BlockSpec(tuple(shape), lambda i: (0,) * len(shape))

    outs = [jax.ShapeDtypeStruct((local, 2, FF, D), BF)]
    outs += [jax.ShapeDtypeStruct((n_tok, D), BF)] * (2 * groups)
    outs += [jax.ShapeDtypeStruct((8, n_tok), F32)] * groups
    result = pl.pallas_call(
        functools.partial(experts_kernel, groups, local, "exp"),
        grid=(local,),
        out_shape=outs,
        in_specs=[VMEM] * (3 * groups + 1)
        + [pl.BlockSpec((1, D, FF), lambda i: (i, 0, 0)), pl.BlockSpec((1, FF, D), lambda i: (i, 0, 0))],
        out_specs=[pl.BlockSpec((1, 2, FF, D), lambda i: (i, 0, 0, 0))] + [full(o.shape) for o in outs[1:]],
        scratch_shapes=[
            pltpu.VMEM((total, D + 128), BF),
            pltpu.VMEM((total, D), BF),
            pltpu.VMEM((8, total), F32),
            pltpu.VMEM((total, 128), F32),
            pltpu.VMEM((room, 2 * D + 128), BF),
            pltpu.VMEM((FF, D), F32),
            pltpu.VMEM((FF, D), F32),
            pltpu.VMEM((TILE, FF), BF),
            pltpu.VMEM((TILE, FF), BF),
            pltpu.VMEM((ROWS, 2 * D + 128), F32),
            pltpu.SMEM((24,), jnp.int32),
        ],
        compiler_params=pltpu.CompilerParams(vmem_limit_bytes=60 << 20),
        name="experts",
    )(*cs, *gs, *rs, router_t, win, wout)
    return result[0], result[1 : groups + 1], result[groups + 1 : 2 * groups + 1], result[2 * groups + 1 :]


def bwd_kernel(groups, n_in, *refs):
    ins, outs, scr = refs[:n_in], refs[n_in : n_in + 10], refs[n_in + 10 :]
    (gains, wqkv, wo, win, wout, router_t, x0, x1, x2, x3, qkv1, qkv2, o1, o2, p1, p2, u, gp, c, cot, routes) = ins[:21]
    y_refs, d_refs, delta_refs = ins[21 : 21 + groups], ins[21 + groups : 21 + 2 * groups], ins[21 + 2 * groups :]
    act, gin, dqkv_a, dqkv_b, dproj_a, dproj_b, dgain, dwin, dwout, drouter = outs
    gv, a_scr, dbr_scr, big = scr
    images = x0.shape[0]
    m = images * ROWS
    lo = lane_low(ROWS)

    g0, g1, first, second = gate_rows(router_t[...], c[...].reshape(m, D), routes[...])
    delta = delta_refs[0][0:1] + delta_refs[0][1:2]
    for r in delta_refs[1:]:
        delta = delta + (r[0:1] + r[1:2])
    dl = g0 * g1 * delta
    dlog = jnp.where(first, dl, jnp.where(second, -dl, 0.0)).astype(BF)
    drouter[...] = dot(dlog, c[...].reshape(m, D))
    gv[...] = t_dot(dlog, router_t[...]).reshape(images, ROWS, D)

    def open_image(i, total):
        y = y_refs[0][i].astype(F32)
        dc = gv[i] + d_refs[0][i].astype(F32)
        for k in range(1, groups):
            y = y + y_refs[k][i].astype(F32)
            dc = dc + d_refs[k][i].astype(F32)
        act[i] = (x3[i] + y).astype(BF)
        dx, by_gain = norm_back(dc, x3[i], gains[3:4])
        gv[i] = cot[i].astype(F32) + dx
        return total + jnp.sum(by_gain, axis=0, keepdims=True)

    dgain[3:4] = lax.fori_loop(0, images, open_image, jnp.zeros((1, D), F32))

    def attend_back(layer, gain_row, x, qkv, o, p, dqkv_out, dproj_out, last):
        gain = gains[gain_row : gain_row + 1]

        def image(i, _):
            a_scr[i] = (norm_parts(x[i].astype(F32))[0] * gain).astype(BF)
            dbr = gv[i].astype(BF)
            dbr_scr[i] = dbr
            do = dot_t(dbr, wo[layer])
            dod = do.astype(BF).astype(F32) * o[i].astype(F32)
            do = do.astype(BF)
            for pair in range(HEADS // 2):
                at = 128 * pair
                q = qkv[i, :, at : at + 128] * BF(0.125)
                k = qkv[i, :, D + at : D + at + 128]
                w = qkv[i, :, 2 * D + at : 2 * D + at + 128]
                dqs, dk, dw = [], 0.0, 0.0
                for h in range(2):
                    mask = lo if h == 0 else ~lo
                    dom = jnp.where(mask, do[:, at : at + 128], BF(0))
                    inner = jnp.sum(jnp.where(mask, dod[:, at : at + 128], 0.0), axis=-1, keepdims=True)
                    ph = p[i, 2 * pair + h]
                    ds = (ph.astype(F32) * (dot_t(dom, w) - inner)).astype(BF)
                    dw = dw + t_dot(ph, dom)
                    dqs.append(dot(ds, k))
                    dk = dk + t_dot(ds, jnp.where(mask, q, BF(0)))
                big[i, :, at : at + 128] = (jnp.where(lo, dqs[0], dqs[1]) * 0.125).astype(BF)
                big[i, :, D + at : D + at + 128] = dk.astype(BF)
                big[i, :, 2 * D + at : 2 * D + at + 128] = dw.astype(BF)
            return 0

        lax.fori_loop(0, images, image, 0)
        dproj_out[...] = t_dot(o[...].reshape(m, D), dbr_scr[...].reshape(m, D)).astype(BF)
        a_all = a_scr[...].reshape(m, D)
        for f in range(0, 3 * D, D):
            dqkv_out[:, f : f + D] = t_dot(a_all, big[:, :, f : f + D].reshape(m, D)).astype(BF)

        def close(i, total):
            da = dot_t(big[i, :, 0 : 3 * D], wqkv[layer])
            dx, by_gain = norm_back(da, x[i].astype(F32), gain)
            new = gv[i] + dx
            if last:
                gin[i] = new
            else:
                gv[i] = new
            return total + jnp.sum(by_gain, axis=0, keepdims=True)

        dgain[gain_row : gain_row + 1] = lax.fori_loop(0, images, close, jnp.zeros((1, D), F32))

    attend_back(1, 2, x2, qkv2, o2, p2, dqkv_b, dproj_b, False)

    def mlp_image(i, _):
        a_scr[i] = (norm_parts(x1[i])[0] * gains[1:2]).astype(BF)
        dm = gv[i].astype(BF)
        dbr_scr[i] = dm
        for f in range(0, FF, 512):
            big[i, :, f : f + 512] = (dot_t(dm, wout[f : f + 512]) * gp[i, :, f : f + 512].astype(F32)).astype(BF)
        return 0

    lax.fori_loop(0, images, mlp_image, 0)
    dm_all = dbr_scr[...].reshape(m, D)
    b_all = a_scr[...].reshape(m, D)
    for f in range(0, FF, 512):
        dwout[f : f + 512] = t_dot(u[:, :, f : f + 512].reshape(m, 512), dm_all).astype(BF)
        dwin[:, f : f + 512] = t_dot(b_all, big[:, :, f : f + 512].reshape(m, 512)).astype(BF)

    def mlp_close(i, total):
        db = dot_t(big[i], win[...])
        dx, by_gain = norm_back(db, x1[i], gains[1:2])
        gv[i] = gv[i] + dx
        return total + jnp.sum(by_gain, axis=0, keepdims=True)

    dgain[1:2] = lax.fori_loop(0, images, mlp_close, jnp.zeros((1, D), F32))

    attend_back(0, 0, x0, qkv1, o1, p1, dqkv_a, dproj_a, True)


def dense_backward(weights, saved, cot, routes, ys, ds, deltas):
    groups = len(ys)
    images = saved[0].shape[0]
    experts = weights[-1].shape[0]
    ins = list(weights) + list(saved) + [cot, routes] + list(ys) + list(ds) + list(deltas)
    outs = [
        jax.ShapeDtypeStruct((images, ROWS, D), BF),
        jax.ShapeDtypeStruct((images, ROWS, D), F32),
        jax.ShapeDtypeStruct((D, 3 * D), BF),
        jax.ShapeDtypeStruct((D, 3 * D), BF),
        jax.ShapeDtypeStruct((D, D), BF),
        jax.ShapeDtypeStruct((D, D), BF),
        jax.ShapeDtypeStruct((4, D), F32),
        jax.ShapeDtypeStruct((D, FF), BF),
        jax.ShapeDtypeStruct((FF, D), BF),
        jax.ShapeDtypeStruct((experts, D), F32),
    ]
    return pl.pallas_call(
        functools.partial(bwd_kernel, groups, len(ins)),
        out_shape=outs,
        in_specs=[VMEM] * len(ins),
        out_specs=[VMEM] * len(outs),
        scratch_shapes=[
            pltpu.VMEM((images, ROWS, D), F32),
            pltpu.VMEM((images, ROWS, D), BF),
            pltpu.VMEM((images, ROWS, D), BF),
            pltpu.VMEM((images, ROWS, FF), BF),
        ],
        compiler_params=pltpu.CompilerParams(vmem_limit_bytes=60 << 20),
        name="dense_backward",
    )(*ins)


def from_peer(array, groups, shift):
    return lax.ppermute(array, "exp", [(i, (i + shift) % groups) for i in range(groups)])


def pad_images(rows, value=0):
    rows = rows.reshape(-1, PATCHES, rows.shape[-1])
    return jnp.pad(rows, ((0, 0), (0, ROWS - PATCHES), (0, 0)), constant_values=value)


def shards(
    tokens, routes, norm_gains, attn_qkv, attn_out, mlp_in, mlp_out, router, experts_in, experts_out, cotangent
):
    row_count = tokens.shape[0]
    groups = lax.axis_size("exp")
    local = experts_in.shape[0]
    choices = routes.shape[1]
    capacity = 2 * choices * row_count // (local * groups)
    images = row_count // PATCHES
    n_tok = images * ROWS
    x0, cot = pad_images(tokens), pad_images(cotangent)
    routes_t = pad_images(routes, -1).reshape(n_tok, choices).T
    routes_t = jnp.pad(routes_t, ((0, 8 - choices), (0, 0)), constant_values=-1)
    router_t = router.T
    flat = cot.reshape(n_tok, D)
    gs = [flat] + [from_peer(flat, groups, k) for k in range(1, groups)]
    rs = [routes_t] + [from_peer(routes_t, groups, k) for k in range(1, groups)]
    x1, x2, x3, qkv1, qkv2, o1, o2, p1, p2, u, gp, c = dense_forward(
        x0, norm_gains, attn_qkv, attn_out, mlp_in, mlp_out
    )
    c_flat = c.reshape(n_tok, D)
    cs = [c_flat] + [from_peer(c_flat, groups, k) for k in range(1, groups)]
    eg, ys, ds, deltas = experts_all(cs, gs, rs, router_t, experts_in, experts_out, local * capacity * groups)

    def back(parts):
        return [parts[0]] + [from_peer(parts[k], groups, groups - k) for k in range(1, groups)]

    ds, deltas, ys = back(ds), back(deltas), back(ys)
    ys = [y.reshape(images, ROWS, D) for y in ys]
    ds = [d.reshape(images, ROWS, D) for d in ds]
    rep = lax.axis_size("rep")
    eg = lax.psum_scatter(eg, "rep", scatter_dimension=2, tiled=True)
    act, gin, dqkv_a, dqkv_b, dproj_a, dproj_b, dgain, dwin, dwout, drouter = dense_backward(
        (norm_gains, attn_qkv, attn_out, mlp_in, mlp_out, router_t),
        (x0, x1, x2, x3, qkv1, qkv2, o1, o2, p1, p2, u, gp, c),
        cot, routes_t, ys, ds, deltas,
    )
    dqkv_a, dqkv_b, dproj_a, dproj_b, dwin, dwout, dgain, drouter = lax.psum(
        (dqkv_a, dqkv_b, dproj_a, dproj_b, dwin, dwout, dgain, drouter), ("rep", "exp")
    )
    return (
        act[:, :PATCHES].reshape(row_count, D),
        gin[:, :PATCHES].reshape(row_count, D),
        jnp.stack([dqkv_a, dqkv_b]).astype(F32),
        jnp.stack([dproj_a, dproj_b]).astype(F32),
        dgain,
        dwin.astype(F32),
        dwout.astype(F32),
        drouter.T,
        jnp.swapaxes(eg[:, 0], 1, 2).astype(F32),
        eg[:, 1].astype(F32),
    )


def solution(mesh):
    rows = P(("rep", "exp"), None)
    return jax.shard_map(
        shards,
        mesh=mesh,
        in_specs=(rows, rows, P(), P(), P(), P(), P(), P(), P("exp", None, None), P("exp", None, None), rows),
        out_specs=(rows, rows, P(), P(), P(), P(), P(), P(), P("exp", None, "rep"), P("exp", "rep", None)),
        check_vma=False,
    )
```

```python
import functools
import math

import jax
import jax.numpy as jnp
from jax import lax
from jax.experimental import pallas as pl
from jax.experimental.pallas import tpu as pltpu
from jax.sharding import PartitionSpec as P

F32 = jnp.float32
BF = jnp.bfloat16
HEADS = 6
PATCHES = 197
ROWS = 208
EPS = 1e-6
TILE = 128
CHUNK = 1024
D = 384
FF = 1536
VMEM = pl.BlockSpec(memory_space=pltpu.VMEM)


def dot(a, b):
    return lax.dot_general(a, b, (((1,), (0,)), ((), ())), preferred_element_type=F32)


def dot_t(a, b):
    return lax.dot_general(a, b, (((1,), (1,)), ((), ())), preferred_element_type=F32)


def t_dot(a, b):
    return lax.dot_general(a, b, (((0,), (0,)), ((), ())), preferred_element_type=F32)


def norm_parts(x):
    centred = x - jnp.mean(x, axis=-1, keepdims=True)
    rstd = lax.rsqrt(jnp.mean(centred * centred, axis=-1, keepdims=True) + EPS)
    return centred * rstd, rstd


def norm_back(grad, x, gain):
    xh, rstd = norm_parts(x)
    dxh = grad * gain
    inner = dxh - jnp.mean(dxh, axis=-1, keepdims=True)
    return rstd * (inner - xh * jnp.mean(dxh * xh, axis=-1, keepdims=True)), grad * xh


def gelu_parts(h):
    t = 1.0 / (1.0 + (0.3275911 * 0.7071067811865476) * jnp.abs(h))
    e = jnp.exp(-0.5 * h * h)
    poly = t * (
        0.254829592
        + t * (-0.284496736 + t * (1.421413741 + t * (-1.453152027 + t * 1.061405429)))
    )
    tail = 0.5 * poly * e
    phi = jnp.where(h >= 0, 1.0 - tail, tail)
    return h * phi, phi + h * (0.3989422804014327 * e)


def lane_low(rows):
    return lax.broadcasted_iota(jnp.int32, (rows, 128), 1) < 64


def fwd_kernel(
    x_ref, gains, wqkv, wo, win, wout,
    x1_ref, x2_ref, x3_ref, qkv1_ref, qkv2_ref, o1_ref, o2_ref, p1_ref, p2_ref, u_ref, gp_ref, c_ref,
):
    ib = x_ref.shape[0]
    m = ib * ROWS
    lo = lane_low(ROWS)
    valid = lax.broadcasted_iota(jnp.int32, (ROWS, ROWS), 1) < PATCHES

    def attend(x, layer, gain, qkv_ref, o_ref, p_ref):
        a = (norm_parts(x)[0] * gain).astype(BF)
        qkv_ref[...] = dot(a, wqkv[layer]).astype(BF).reshape(ib, ROWS, 3 * D)
        for i in range(ib):
            for pair in range(HEADS // 2):
                at = 128 * pair
                q = qkv_ref[i, :, at : at + 128] * BF(0.125)
                k = qkv_ref[i, :, D + at : D + at + 128]
                w = qkv_ref[i, :, 2 * D + at : 2 * D + at + 128]
                mixed = []
                for h in range(2):
                    qm = jnp.where(lo if h == 0 else ~lo, q, BF(0))
                    s = jnp.where(valid, dot_t(qm, k), -1e30)
                    s = jnp.exp(s - jnp.max(s, axis=-1, keepdims=True))
                    p = (s * (1.0 / jnp.sum(s, axis=-1, keepdims=True))).astype(BF)
                    p_ref[i, 2 * pair + h] = p
                    mixed.append(dot(p, w))
                o_ref[i, :, at : at + 128] = jnp.where(lo, mixed[0], mixed[1]).astype(BF)
        return x + dot(o_ref[...].reshape(m, D), wo[layer])

    x0 = x_ref[...].astype(F32).reshape(m, D)
    x1 = attend(x0, 0, gains[0:1], qkv1_ref, o1_ref, p1_ref)
    x1_ref[...] = x1.reshape(ib, ROWS, D)
    b = (norm_parts(x1)[0] * gains[1:2]).astype(BF)
    x2 = x1
    for f in range(0, FF, 512):
        u, gp = gelu_parts(dot(b, win[:, f : f + 512]))
        u = u.astype(BF)
        u_ref[:, :, f : f + 512] = u.reshape(ib, ROWS, 512)
        gp_ref[:, :, f : f + 512] = gp.astype(BF).reshape(ib, ROWS, 512)
        x2 = x2 + dot(u, wout[f : f + 512])
    x2_ref[...] = x2.reshape(ib, ROWS, D)
    x3 = attend(x2, 1, gains[2:3], qkv2_ref, o2_ref, p2_ref)
    x3_ref[...] = x3.reshape(ib, ROWS, D)
    c_ref[...] = (norm_parts(x3)[0] * gains[3:4]).astype(BF).reshape(ib, ROWS, D)


def dense_forward(x, gains, wqkv, wo, win, wout):
    n = x.shape[0]
    ib = 2 if n % 2 == 0 else 1

    def out(*shape, dtype=BF):
        return jax.ShapeDtypeStruct((n,) + shape, dtype)

    def block(shape):
        return pl.BlockSpec((ib,) + tuple(shape[1:]), lambda i: (i,) + (0,) * (len(shape) - 1))

    outs = [out(ROWS, D, dtype=F32)] * 3 + [out(ROWS, 3 * D)] * 2 + [out(ROWS, D)] * 2
    outs += [out(HEADS, ROWS, ROWS)] * 2 + [out(ROWS, FF)] * 2 + [out(ROWS, D)]
    return pl.pallas_call(
        fwd_kernel,
        grid=(n // ib,),
        out_shape=outs,
        in_specs=[block(x.shape)] + [VMEM] * 5,
        out_specs=[block(o.shape) for o in outs],
        compiler_params=pltpu.CompilerParams(vmem_limit_bytes=60 << 20),
        name="dense_forward",
    )(x, gains, wqkv, wo, win, wout)


def gate_rows(router_t, c, routes):
    logits = dot_t(router_t, c)
    expert = lax.broadcasted_iota(jnp.int32, logits.shape, 0)
    first, second = expert == routes[0:1], expert == routes[1:2]
    diff = jnp.sum(jnp.where(first, logits, 0.0) - jnp.where(second, logits, 0.0), axis=0, keepdims=True)
    return 1.0 / (1.0 + jnp.exp(-diff)), 1.0 / (1.0 + jnp.exp(diff)), first, second


def experts_kernel(groups, local, exp_axis, *refs):
    c_refs, g_refs, r_refs = refs[:groups], refs[groups : 2 * groups], refs[2 * groups : 3 * groups]
    router_t, win, wout = refs[3 * groups : 3 * groups + 3]
    outs = refs[3 * groups + 3 :]
    eg_ref, y_refs, d_refs, delta_refs = outs[0], outs[1 : groups + 1], outs[groups + 1 : 2 * groups + 1], outs[2 * groups + 1 : 3 * groups + 1]
    ci, g4, rows, cols, slots, acc_out, acc_in, u_scr, gp_scr, back, counts = outs[3 * groups + 1 :]
    n_tok = c_refs[0].shape[0]
    total = groups * n_tok
    step = pl.program_id(0)
    first_expert = lax.axis_index(exp_axis) * local

    @pl.when(step == 0)
    def _():
        for s in range(groups):
            at = s * n_tok
            ci[at : at + n_tok, 0:D] = c_refs[s][...]
            g4[at : at + n_tok] = g_refs[s][...]
        routes = jnp.concatenate([r[0:2] for r in r_refs], axis=1)
        g0, g1, _, _ = gate_rows(router_t[...], ci[:, 0:D], routes)
        mine = first_expert + lax.broadcasted_iota(jnp.int32, (8, total), 0)
        inside = lax.broadcasted_iota(jnp.int32, (8, total), 0) < local
        is0, is1 = (mine == routes[0:1]) & inside, (mine == routes[1:2]) & inside
        member = jnp.where(is0 | is1, 1.0, 0.0)
        lane = lax.broadcasted_iota(jnp.int32, (8, total), 1)
        upto = member
        shift = 1
        while shift < total:
            upto = upto + jnp.where(lane >= shift, pltpu.roll(upto, shift, 1), 0.0)
            shift *= 2
        position = jnp.where(member > 0, upto - 1.0, -1.0)
        rows[0:8] = position
        base = jnp.int32(0)
        starts = []
        for e in range(local):
            n = jnp.sum(member[e : e + 1]).astype(jnp.int32)
            tiles = (n + TILE - 1) // TILE
            counts[e] = tiles
            counts[8 + e] = base
            starts.append((base * TILE).astype(F32))
            base = base + tiles
        counts[16] = base
        start = jnp.zeros((8, total), F32)
        expert_row = lax.broadcasted_iota(jnp.int32, (8, total), 0)
        for e in range(local):
            start = jnp.where(expert_row == e, starts[e], start)
        slot = start + position
        slot0 = jnp.sum(jnp.where(is0, slot + 1.0, 0.0), axis=0, keepdims=True) - 1.0
        slot1 = jnp.sum(jnp.where(is1, slot + 1.0, 0.0), axis=0, keepdims=True) - 1.0
        gates = jnp.where(is0, g0, jnp.where(is1, g1, 0.0))
        sign = jnp.where(is0, 1.0, jnp.where(is1, -1.0, 0.0))
        slot_rows = jnp.where(expert_row == 0, slot0, jnp.where(expert_row == 1, slot1, 0.0))
        stacked = jnp.concatenate([gates, sign, slot_rows, jnp.zeros((104, total), F32)], axis=0)
        lane128 = lax.broadcasted_iota(jnp.int32, (128, 128), 1)
        for at in range(0, total, 128):
            col = stacked[:, at : at + 128].T
            cols[at : at + 128] = col
            low = col - col.astype(BF).astype(F32)
            info = jnp.where(lane128 < 16, col, jnp.where(lane128 < 24, pltpu.roll(low, 16, 1), 0.0))
            ci[at : at + 128, D : D + 128] = info.astype(BF)

    acc_out[...] = jnp.zeros_like(acc_out)
    acc_in[...] = jnp.zeros_like(acc_in)
    position = rows[pl.ds(step, 1)]
    lane = lax.broadcasted_iota(jnp.int32, (TILE, 128), 1)

    def tile(j, _):
        slot = (j * TILE + lax.broadcasted_iota(jnp.int32, (TILE, total), 0)).astype(F32)
        pick = jnp.where(position == slot, 1.0, 0.0).astype(BF)
        xi = dot(pick, ci[...])
        g4r = dot(pick, g4[...])
        x = xi[:, 0:D].astype(BF)
        info = xi[:, D : D + 128]
        gate = jnp.sum(jnp.where((lane == step) | (lane == step + 16), info, 0.0), axis=-1, keepdims=True)
        sign = jnp.sum(jnp.where(lane == step + 8, info, 0.0), axis=-1, keepdims=True)
        dy = (gate * g4r).astype(BF)
        for f in range(0, FF, 512):
            u, gp = gelu_parts(dot(x, win[0, :, f : f + 512]))
            u_scr[:, f : f + 512] = u.astype(BF)
            gp_scr[:, f : f + 512] = gp.astype(BF)
        ey = dot(u_scr[...], wout[0]).astype(BF).astype(F32)
        dg = sign * jnp.sum(g4r * ey, axis=-1, keepdims=True)
        acc_out[...] += t_dot(u_scr[...], dy)
        for f in range(0, FF, 512):
            du = dot_t(dy, wout[0, f : f + 512])
            gp_scr[:, f : f + 512] = (du * gp_scr[:, f : f + 512].astype(F32)).astype(BF)
        dcp = dot_t(gp_scr[...], win[0])
        acc_in[...] += t_dot(gp_scr[...], x)
        at = pl.multiple_of((counts[8 + step] + j) * TILE, TILE)
        slots[pl.ds(at, TILE), 0:D] = (gate * ey).astype(BF)
        slots[pl.ds(at, TILE), D : 2 * D] = dcp.astype(BF)
        low = dg - dg.astype(BF).astype(F32)
        slots[pl.ds(at, TILE), 2 * D : 2 * D + 128] = jnp.where(lane == 0, dg, jnp.where(lane == 1, low, 0.0)).astype(BF)
        return 0

    lax.fori_loop(0, counts[step], tile, 0)
    eg_ref[0, 0] = acc_in[...].astype(BF).reshape(eg_ref.shape[2:])
    eg_ref[0, 1] = acc_out[...].astype(BF).reshape(eg_ref.shape[2:])

    @pl.when(step == local - 1)
    def _():
        used = counts[16]
        chunks = (used * TILE + CHUNK - 1) // CHUNK

        def clear(j, _):
            at = pl.multiple_of(j * TILE, TILE)
            slots[pl.ds(at, TILE)] = jnp.zeros((TILE, 2 * D + 128), BF)
            return 0

        lax.fori_loop(used, chunks * (CHUNK // TILE), clear, 0)
        lane_chunk = lax.broadcasted_iota(jnp.int32, (ROWS, CHUNK), 1)

        for s in range(groups):
            for b in range(n_tok // ROWS):
                at = s * n_tok + b * ROWS
                slot0, slot1 = cols[at : at + ROWS, 16:17], cols[at : at + ROWS, 17:18]
                back[...] = jnp.zeros_like(back)

                def gather(j, _):
                    slot = (j * CHUNK + lane_chunk).astype(F32)
                    pick = jnp.where((slot0 == slot) | (slot1 == slot), 1.0, 0.0).astype(BF)
                    back[...] += dot(pick, slots[pl.ds(pl.multiple_of(j * CHUNK, CHUNK), CHUNK)])
                    return 0

                lax.fori_loop(0, chunks, gather, 0)
                y_refs[s][b * ROWS : (b + 1) * ROWS] = back[:, 0:D].astype(BF)
                d_refs[s][b * ROWS : (b + 1) * ROWS] = back[:, D : 2 * D].astype(BF)
                cols[at : at + ROWS] = back[:, 2 * D : 2 * D + 128]
        for at in range(0, total, 128):
            rows[:, at : at + 128] = cols[at : at + 128].T[0:8]
        for s in range(groups):
            delta_refs[s][...] = rows[:, s * n_tok : (s + 1) * n_tok]


def experts_all(cs, gs, rs, router_t, win, wout, slots_most, owners):
    groups = len(cs)
    local = win.shape[0]
    n_tok = cs[0].shape[0]
    total = groups * n_tok
    room = -(-(slots_most + local * TILE) // CHUNK) * CHUNK

    def full(shape):
        return pl.BlockSpec(tuple(shape), lambda i: (0,) * len(shape))

    outs = [jax.ShapeDtypeStruct((local, 2) + owners + (FF // math.prod(owners), D), BF)]
    outs += [jax.ShapeDtypeStruct((n_tok, D), BF)] * (2 * groups)
    outs += [jax.ShapeDtypeStruct((8, n_tok), F32)] * groups
    result = pl.pallas_call(
        functools.partial(experts_kernel, groups, local, "exp"),
        grid=(local,),
        out_shape=outs,
        in_specs=[VMEM] * (3 * groups + 1)
        + [pl.BlockSpec((1, D, FF), lambda i: (i, 0, 0)), pl.BlockSpec((1, FF, D), lambda i: (i, 0, 0))],
        out_specs=[pl.BlockSpec((1,) + outs[0].shape[1:], lambda i: (i,) + (0,) * (len(outs[0].shape) - 1))] + [full(o.shape) for o in outs[1:]],
        scratch_shapes=[
            pltpu.VMEM((total, D + 128), BF),
            pltpu.VMEM((total, D), BF),
            pltpu.VMEM((8, total), F32),
            pltpu.VMEM((total, 128), F32),
            pltpu.VMEM((room, 2 * D + 128), BF),
            pltpu.VMEM((FF, D), F32),
            pltpu.VMEM((FF, D), F32),
            pltpu.VMEM((TILE, FF), BF),
            pltpu.VMEM((TILE, FF), BF),
            pltpu.VMEM((ROWS, 2 * D + 128), F32),
            pltpu.SMEM((24,), jnp.int32),
        ],
        compiler_params=pltpu.CompilerParams(vmem_limit_bytes=60 << 20),
        name="experts",
    )(*cs, *gs, *rs, router_t, win, wout)
    return result[0], result[1 : groups + 1], result[groups + 1 : 2 * groups + 1], result[2 * groups + 1 :]


def bwd_kernel(groups, n_in, *refs):
    ins, outs, scr = refs[:n_in], refs[n_in : n_in + 5], refs[n_in + 5 :]
    (gains, wqkv, wo, win, wout, router_t, x0, x1, x2, x3, qkv1, qkv2, o1, o2, p1, p2, u, gp, c, cot, routes) = ins[:21]
    y_refs, d_refs, delta_refs = ins[21 : 21 + groups], ins[21 + groups : 21 + 2 * groups], ins[21 + 2 * groups :]
    act, gin, shared, dgain, drouter = outs
    gv, a_scr, dbr_scr, big = scr
    images = x0.shape[0]
    m = images * ROWS
    lo = lane_low(ROWS)

    g0, g1, first, second = gate_rows(router_t[...], c[...].reshape(m, D), routes[...])
    delta = delta_refs[0][0:1] + delta_refs[0][1:2]
    for r in delta_refs[1:]:
        delta = delta + (r[0:1] + r[1:2])
    dl = g0 * g1 * delta
    dlog = jnp.where(first, dl, jnp.where(second, -dl, 0.0)).astype(BF)
    drouter[...] = dot(dlog, c[...].reshape(m, D))
    gv[...] = t_dot(dlog, router_t[...]).reshape(images, ROWS, D)

    def open_image(i, total):
        y = y_refs[0][i].astype(F32)
        dc = gv[i] + d_refs[0][i].astype(F32)
        for k in range(1, groups):
            y = y + y_refs[k][i].astype(F32)
            dc = dc + d_refs[k][i].astype(F32)
        act[i] = (x3[i] + y).astype(BF)
        dx, by_gain = norm_back(dc, x3[i], gains[3:4])
        gv[i] = cot[i].astype(F32) + dx
        return total + jnp.sum(by_gain, axis=0, keepdims=True)

    dgain[3:4] = lax.fori_loop(0, images, open_image, jnp.zeros((1, D), F32))

    def attend_back(layer, gain_row, x, qkv, o, p, at_block, last):
        gain = gains[gain_row : gain_row + 1]

        def image(i, _):
            a_scr[i] = (norm_parts(x[i].astype(F32))[0] * gain).astype(BF)
            dbr = gv[i].astype(BF)
            dbr_scr[i] = dbr
            do = dot_t(dbr, wo[layer])
            dod = do.astype(BF).astype(F32) * o[i].astype(F32)
            do = do.astype(BF)
            for pair in range(HEADS // 2):
                at = 128 * pair
                q = qkv[i, :, at : at + 128] * BF(0.125)
                k = qkv[i, :, D + at : D + at + 128]
                w = qkv[i, :, 2 * D + at : 2 * D + at + 128]
                dqs, dk, dw = [], 0.0, 0.0
                for h in range(2):
                    mask = lo if h == 0 else ~lo
                    dom = jnp.where(mask, do[:, at : at + 128], BF(0))
                    inner = jnp.sum(jnp.where(mask, dod[:, at : at + 128], 0.0), axis=-1, keepdims=True)
                    ph = p[i, 2 * pair + h]
                    ds = (ph.astype(F32) * (dot_t(dom, w) - inner)).astype(BF)
                    dw = dw + t_dot(ph, dom)
                    dqs.append(dot(ds, k))
                    dk = dk + t_dot(ds, jnp.where(mask, q, BF(0)))
                big[i, :, at : at + 128] = (jnp.where(lo, dqs[0], dqs[1]) * 0.125).astype(BF)
                big[i, :, D + at : D + at + 128] = dk.astype(BF)
                big[i, :, 2 * D + at : 2 * D + at + 128] = dw.astype(BF)
            return 0

        lax.fori_loop(0, images, image, 0)
        shared[at_block + 3] = t_dot(o[...].reshape(m, D), dbr_scr[...].reshape(m, D)).astype(BF)
        a_all = a_scr[...].reshape(m, D)
        for f in range(3):
            shared[at_block + f] = t_dot(a_all, big[:, :, f * D : f * D + D].reshape(m, D)).astype(BF)

        def close(i, total):
            da = dot_t(big[i, :, 0 : 3 * D], wqkv[layer])
            dx, by_gain = norm_back(da, x[i].astype(F32), gain)
            new = gv[i] + dx
            if last:
                gin[i] = new
            else:
                gv[i] = new
            return total + jnp.sum(by_gain, axis=0, keepdims=True)

        dgain[gain_row : gain_row + 1] = lax.fori_loop(0, images, close, jnp.zeros((1, D), F32))

    attend_back(1, 2, x2, qkv2, o2, p2, 0, False)

    def mlp_image(i, _):
        a_scr[i] = (norm_parts(x1[i])[0] * gains[1:2]).astype(BF)
        dm = gv[i].astype(BF)
        dbr_scr[i] = dm
        for f in range(0, FF, 512):
            big[i, :, f : f + 512] = (dot_t(dm, wout[f : f + 512]) * gp[i, :, f : f + 512].astype(F32)).astype(BF)
        return 0

    lax.fori_loop(0, images, mlp_image, 0)
    dm_all = dbr_scr[...].reshape(m, D)
    b_all = a_scr[...].reshape(m, D)
    for f in range(4):
        shared[4 + f] = t_dot(u[:, :, f * D : f * D + D].reshape(m, D), dm_all).astype(BF)
        shared[8 + f] = t_dot(b_all, big[:, :, f * D : f * D + D].reshape(m, D)).astype(BF)

    def mlp_close(i, total):
        db = dot_t(big[i], win[...])
        dx, by_gain = norm_back(db, x1[i], gains[1:2])
        gv[i] = gv[i] + dx
        return total + jnp.sum(by_gain, axis=0, keepdims=True)

    dgain[1:2] = lax.fori_loop(0, images, mlp_close, jnp.zeros((1, D), F32))

    attend_back(0, 0, x0, qkv1, o1, p1, 12, True)


def dense_backward(weights, saved, cot, routes, ys, ds, deltas):
    groups = len(ys)
    images = saved[0].shape[0]
    experts = weights[-1].shape[0]
    ins = list(weights) + list(saved) + [cot, routes] + list(ys) + list(ds) + list(deltas)
    outs = [
        jax.ShapeDtypeStruct((images, ROWS, D), BF),
        jax.ShapeDtypeStruct((images, ROWS, D), F32),
        jax.ShapeDtypeStruct((16, D, D), BF),
        jax.ShapeDtypeStruct((4, D), F32),
        jax.ShapeDtypeStruct((experts, D), F32),
    ]
    return pl.pallas_call(
        functools.partial(bwd_kernel, groups, len(ins)),
        out_shape=outs,
        in_specs=[VMEM] * len(ins),
        out_specs=[VMEM] * len(outs),
        scratch_shapes=[
            pltpu.VMEM((images, ROWS, D), F32),
            pltpu.VMEM((images, ROWS, D), BF),
            pltpu.VMEM((images, ROWS, D), BF),
            pltpu.VMEM((images, ROWS, FF), BF),
        ],
        compiler_params=pltpu.CompilerParams(vmem_limit_bytes=60 << 20),
        name="dense_backward",
    )(*ins)


OUTER, SHARE = 4, 48
MESH = pl.DeviceIdType.MESH


class Place:
    def __init__(self):
        r = lax.axis_index("rep")
        self.y = lax.axis_index("exp")
        self.z, self.x, self.c = r // 4, (r // 2) % 2, r % 2
        self.core = (r + 1 - 2 * self.c, self.y)
        self.across = (r + 2 - 4 * self.x, self.y)
        self.beside = (r, 1 - self.y)
        self.along = [((self.z + k) % OUTER) for k in range(1, OUTER)]

    def at_z(self, z):
        return (z * 4 + self.x * 2 + self.c, self.y)

    def meet(self):
        barrier = pltpu.get_barrier_semaphore()
        partners = [self.core, self.across, self.beside] + [self.at_z(z) for z in self.along]
        for partner in partners:
            pl.semaphore_signal(barrier, inc=1, device_id=partner, device_id_type=MESH)
        pl.semaphore_wait(barrier, len(partners))


class Links:
    def __init__(self, send, recv):
        self.send, self.recv, self.used = send, recv, 0

    def start(self, src, dst, device):
        copy = pltpu.make_async_remote_copy(
            src_ref=src, dst_ref=dst, send_sem=self.send.at[self.used], recv_sem=self.recv.at[self.used],
            device_id=device, device_id_type=MESH,
        )
        self.used += 1
        copy.start()
        return copy


def add_into(count, target, *others):
    def block(i, _):
        total = target(i)[...].astype(F32)
        for other in others:
            total = total + other(i)[...].astype(F32)
        target(i)[...] = total.astype(target(i).dtype)
        return 0

    lax.fori_loop(0, count, block, 0)


class ExpertSum:
    COPIES = 2 + OUTER - 1

    def __init__(self, place, links, j, eg, own, core_rx, x_rx, z_rx, out, local_sem):
        self.p, self.links, self.j, self.out = place, links, j, out
        self.eg, self.own, self.core_rx, self.x_rx, self.z_rx = eg, own, core_rx, x_rx, z_rx
        self.sem = local_sem.at[j]

    def core(self):
        p, j = self.p, self.j
        self.load = pltpu.make_async_copy(self.eg.at[j, :, :, :, p.c], self.own.at[j], self.sem)
        self.load.start()
        self.c1 = self.links.start(self.eg.at[j, :, :, :, 1 - p.c], self.core_rx.at[j], p.core)

    def across(self):
        p, j = self.p, self.j
        self.load.wait()
        self.c1.wait()
        for x in (1 - p.x, p.x):
            add_into(
                2 * OUTER,
                lambda i: self.own.at[j, i // OUTER, i % OUTER, x],
                lambda i: self.core_rx.at[j, i // OUTER, i % OUTER, x],
            )
            if x is not p.x:
                self.c2 = self.links.start(self.own.at[j, :, :, 1 - p.x], self.x_rx.at[j], p.across)

    def along(self):
        p, j = self.p, self.j
        self.c2.wait()
        add_into(
            2 * OUTER,
            lambda i: self.own.at[j, i // OUTER, i % OUTER, p.x],
            lambda i: self.x_rx.at[j, i // OUTER, i % OUTER],
        )
        self.c3 = [
            self.links.start(self.own.at[j, :, z, p.x], self.z_rx.at[j, k], p.at_z(z)) for k, z in enumerate(p.along)
        ]

    def finish(self):
        p, j = self.p, self.j
        for c in self.c3:
            c.wait()
        for part in range(2):
            total = self.own[j, part, p.z, p.x].astype(F32)
            for k in range(OUTER - 1):
                total = total + self.z_rx[j, k, part].astype(F32)
            self.out[j, part] = total


class SharedSum:
    COPIES = 2 * (3 + OUTER - 1)

    def __init__(self, place, links, g, src, rx1, rx2, rx3, rx4, out):
        self.p, self.links, self.out = place, links, out.at[g]
        self.src, self.rx1, self.rx2, self.rx3, self.rx4 = src.at[g], rx1.at[g], rx2.at[g], rx3.at[g], rx4.at[g]

    def core(self):
        p = self.p
        self.c = self.links.start(self.src.at[1 - p.c], self.rx1, p.core)

    def beside(self):
        p = self.p
        self.c.wait()
        add_into(
            4 * OUTER,
            lambda i: self.src.at[p.c, i // (2 * OUTER), (i // OUTER) % 2, i % OUTER],
            lambda i: self.rx1.at[i // (2 * OUTER), (i // OUTER) % 2, i % OUTER],
        )
        self.c = self.links.start(self.src.at[p.c, 1 - p.y], self.rx2, p.beside)

    def across(self):
        p = self.p
        self.c.wait()
        add_into(
            2 * OUTER,
            lambda i: self.src.at[p.c, p.y, i // OUTER, i % OUTER],
            lambda i: self.rx2.at[i // OUTER, i % OUTER],
        )
        self.c = self.links.start(self.src.at[p.c, p.y, 1 - p.x], self.rx3, p.across)

    def along(self):
        p = self.p
        self.c.wait()
        add_into(OUTER, lambda i: self.src.at[p.c, p.y, p.x, i], lambda i: self.rx3.at[i])
        self.cs = [
            self.links.start(self.src.at[p.c, p.y, p.x, z], self.rx4.at[k], p.at_z(z)) for k, z in enumerate(p.along)
        ]

    def out_along(self):
        p = self.p
        for c in self.cs:
            c.wait()
        total = self.src[p.c, p.y, p.x, p.z].astype(F32)
        for k in range(OUTER - 1):
            total = total + self.rx4[k].astype(F32)
        mine = self.out.at[p.c, p.y, p.x, p.z]
        mine[...] = total.astype(BF)
        self.cs = [self.links.start(mine, mine, p.at_z(z)) for z in p.along]

    def out_across(self):
        p = self.p
        for c in self.cs:
            c.wait()
        mine = self.out.at[p.c, p.y, p.x]
        self.c = self.links.start(mine, mine, p.across)

    def out_beside(self):
        p = self.p
        self.c.wait()
        mine = self.out.at[p.c, p.y]
        self.c = self.links.start(mine, mine, p.beside)

    def out_core(self):
        p = self.p
        self.c.wait()
        mine = self.out.at[p.c]
        self.c = self.links.start(mine, mine, p.core)

    def finish(self):
        self.c.wait()


class SmallSum:
    COPIES = 3 + OUTER - 1

    def __init__(self, place, links, src, rx):
        self.p, self.links, self.src, self.rx = place, links, src, rx

    def step(self, k):
        device = (self.p.core, self.p.beside, self.p.across)[k]
        if k:
            self.c.wait()
            self.src[k] = self.src[k - 1] + self.rx[k - 1]
        self.c = self.links.start(self.src.at[k], self.rx.at[k], device)

    def along(self):
        self.c.wait()
        self.src[3] = self.src[2] + self.rx[2]
        self.cs = [
            self.links.start(self.src.at[3], self.rx.at[3 + k], self.p.at_z(z)) for k, z in enumerate(self.p.along)
        ]

    def finish(self, out):
        for c in self.cs:
            c.wait()
        total = self.src[3]
        for k in range(OUTER - 1):
            total = total + self.rx[3 + k]
        out[...] = total


def sums_kernel(
    eg, sh, small, eg_out, sh_out, small_out,
    own, core_rx, x_rx, z_rx, rx1, rx2, rx3, rx4, small_src, small_rx, local_sem, send, recv,
):
    place = Place()
    links = Links(send, recv)
    place.meet()
    experts = [ExpertSum(place, links, j, eg, own, core_rx, x_rx, z_rx, eg_out, local_sem) for j in range(eg.shape[0])]
    groups = [SharedSum(place, links, g, sh, rx1, rx2, rx3, rx4, sh_out) for g in range(sh.shape[0])]
    few = SmallSum(place, links, small_src, small_rx)
    small_src[0] = small[...]
    few.step(0)
    for e in experts:
        e.core()
    for g in groups:
        g.core()
    for e in experts:
        e.across()
    few.step(1)
    for g in groups:
        g.beside()
    few.step(2)
    for g in groups:
        g.across()
    few.along()
    for e in experts:
        e.along()
    for g in groups:
        g.along()
    few.finish(small_out)
    for g in groups:
        g.out_along()
    for e in experts:
        e.finish()
    for g in groups:
        g.out_across()
    for g in groups:
        g.out_beside()
    for g in groups:
        g.out_core()
    for g in groups:
        g.finish()


def device_sums(eg, sh, small):
    local, groups = eg.shape[0], sh.shape[0]
    copies = local * ExpertSum.COPIES + groups * SharedSum.COPIES + SmallSum.COPIES
    share = eg.shape[-2]
    vm = pltpu.VMEM
    return pl.pallas_call(
        sums_kernel,
        out_shape=[
            jax.ShapeDtypeStruct((local, 2, share, D), F32),
            jax.ShapeDtypeStruct(sh.shape, BF),
            jax.ShapeDtypeStruct(small.shape, F32),
        ],
        in_specs=[pl.BlockSpec(memory_space=pl.ANY), VMEM, VMEM],
        out_specs=[VMEM] * 3,
        scratch_shapes=[
            vm((local, 2, OUTER, 2, share, D), BF),
            vm((local, 2, OUTER, 2, share, D), BF),
            vm((local, 2, OUTER, share, D), BF),
            vm((local, OUTER - 1, 2, share, D), BF),
            vm((groups, 2, 2, OUTER, SHARE, D), BF),
            vm((groups, 2, OUTER, SHARE, D), BF),
            vm((groups, OUTER, SHARE, D), BF),
            vm((groups, OUTER - 1, SHARE, D), BF),
            vm((4,) + small.shape, F32),
            vm((OUTER + 2,) + small.shape, F32),
            pltpu.SemaphoreType.DMA((local,)),
            pltpu.SemaphoreType.DMA((copies,)),
            pltpu.SemaphoreType.DMA((copies,)),
        ],
        compiler_params=pltpu.CompilerParams(collective_id=1, has_side_effects=True, vmem_limit_bytes=60 << 20),
        name="sums",
    )(eg, sh, small)


def from_peer(array, groups, shift):
    return lax.ppermute(array, "exp", [(i, (i + shift) % groups) for i in range(groups)])


def pad_images(rows, value=0):
    rows = rows.reshape(-1, PATCHES, rows.shape[-1])
    return jnp.pad(rows, ((0, 0), (0, ROWS - PATCHES), (0, 0)), constant_values=value)


def side_by_side(blocks):
    return jnp.swapaxes(blocks, 0, 1).reshape(D, -1)


def shards(
    tokens, routes, norm_gains, attn_qkv, attn_out, mlp_in, mlp_out, router, experts_in, experts_out, cotangent
):
    row_count = tokens.shape[0]
    groups = lax.axis_size("exp")
    local = experts_in.shape[0]
    choices = routes.shape[1]
    capacity = 2 * choices * row_count // (local * groups)
    images = row_count // PATCHES
    n_tok = images * ROWS
    x0, cot = pad_images(tokens), pad_images(cotangent)
    routes_t = pad_images(routes, -1).reshape(n_tok, choices).T
    routes_t = jnp.pad(routes_t, ((0, 8 - choices), (0, 0)), constant_values=-1)
    router_t = router.T
    flat = cot.reshape(n_tok, D)
    gs = [flat] + [from_peer(flat, groups, k) for k in range(1, groups)]
    rs = [routes_t] + [from_peer(routes_t, groups, k) for k in range(1, groups)]
    x1, x2, x3, qkv1, qkv2, o1, o2, p1, p2, u, gp, c = dense_forward(
        x0, norm_gains, attn_qkv, attn_out, mlp_in, mlp_out
    )
    c_flat = c.reshape(n_tok, D)
    cs = [c_flat] + [from_peer(c_flat, groups, k) for k in range(1, groups)]
    rep = lax.axis_size("rep")
    known = (rep, groups, local) == (16, 2, 4)
    owners = (OUTER, 2, 2) if known else (rep,)
    eg, ys, ds, deltas = experts_all(
        cs, gs, rs, router_t, experts_in, experts_out, local * capacity * groups, owners
    )

    def back(parts):
        return [parts[0]] + [from_peer(parts[k], groups, groups - k) for k in range(1, groups)]

    ds, deltas, ys = back(ds), back(deltas), back(ys)
    ys = [y.reshape(images, ROWS, D) for y in ys]
    ds = [d.reshape(images, ROWS, D) for d in ds]
    act, gin, shared, dgain, drouter = dense_backward(
        (norm_gains, attn_qkv, attn_out, mlp_in, mlp_out, router_t),
        (x0, x1, x2, x3, qkv1, qkv2, o1, o2, p1, p2, u, gp, c),
        cot, routes_t, ys, ds, deltas,
    )
    experts = drouter.shape[0]
    small = jnp.concatenate([dgain, drouter], axis=0)
    if known:
        small = jnp.pad(small, ((0, 16 - small.shape[0]), (0, 0)))
        eg, shared, small = device_sums(eg, shared.reshape(4, 2, 2, 2, OUTER, SHARE, D), small)
        shared = shared.reshape(16, D, D)
    else:
        eg = lax.psum_scatter(eg, "rep", scatter_dimension=2, tiled=True).reshape(local, 2, FF // rep, D).astype(F32)
        shared, small = lax.psum((shared, small), ("rep", "exp"))
    shared = shared.astype(F32)
    return (
        act[:, :PATCHES].reshape(row_count, D),
        gin[:, :PATCHES].reshape(row_count, D),
        jnp.stack([side_by_side(shared[12:15]), side_by_side(shared[0:3])]),
        jnp.stack([shared[15], shared[3]]),
        small[0:4],
        side_by_side(shared[8:12]),
        shared[4:8].reshape(FF, D),
        small[4 : 4 + experts].T,
        jnp.swapaxes(eg[:, 0], 1, 2),
        eg[:, 1],
    )


def solution(mesh):
    rows = P(("rep", "exp"), None)
    return jax.shard_map(
        shards,
        mesh=mesh,
        in_specs=(rows, rows, P(), P(), P(), P(), P(), P(), P("exp", None, None), P("exp", None, None), rows),
        out_specs=(rows, rows, P(), P(), P(), P(), P(), P(), P("exp", None, "rep"), P("exp", "rep", None)),
        check_vma=False,
    )
```

```python
import functools
import math

import jax
import jax.numpy as jnp
from jax import lax
from jax.experimental import pallas as pl
from jax.experimental.pallas import tpu as pltpu
from jax.sharding import PartitionSpec as P

F32 = jnp.float32
BF = jnp.bfloat16
HEADS = 6
PATCHES = 197
ROWS = 208
EPS = 1e-6
TILE = 128
CHUNK = 1024
D = 384
FF = 1536
VMEM = pl.BlockSpec(memory_space=pltpu.VMEM)


def dot(a, b):
    return lax.dot_general(a, b, (((1,), (0,)), ((), ())), preferred_element_type=F32)


def dot_t(a, b):
    return lax.dot_general(a, b, (((1,), (1,)), ((), ())), preferred_element_type=F32)


def t_dot(a, b):
    return lax.dot_general(a, b, (((0,), (0,)), ((), ())), preferred_element_type=F32)


def norm_parts(x):
    centred = x - jnp.mean(x, axis=-1, keepdims=True)
    rstd = lax.rsqrt(jnp.mean(centred * centred, axis=-1, keepdims=True) + EPS)
    return centred * rstd, rstd


def norm_back(grad, x, gain):
    xh, rstd = norm_parts(x)
    dxh = grad * gain
    inner = dxh - jnp.mean(dxh, axis=-1, keepdims=True)
    return rstd * (inner - xh * jnp.mean(dxh * xh, axis=-1, keepdims=True)), grad * xh


def gelu_parts(h):
    t = 1.0 / (1.0 + (0.3275911 * 0.7071067811865476) * jnp.abs(h))
    e = jnp.exp(-0.5 * h * h)
    poly = t * (
        0.254829592
        + t * (-0.284496736 + t * (1.421413741 + t * (-1.453152027 + t * 1.061405429)))
    )
    tail = 0.5 * poly * e
    phi = jnp.where(h >= 0, 1.0 - tail, tail)
    return h * phi, phi + h * (0.3989422804014327 * e)


def lane_low(rows):
    return lax.broadcasted_iota(jnp.int32, (rows, 128), 1) < 64


def fwd_kernel(
    x_ref, gains, wqkv, wo, win, wout,
    x1_ref, x2_ref, x3_ref, qkv1_ref, qkv2_ref, o1_ref, o2_ref, p1_ref, p2_ref, u_ref, gp_ref, c_ref,
):
    ib = x_ref.shape[0]
    m = ib * ROWS
    lo = lane_low(ROWS)
    valid = lax.broadcasted_iota(jnp.int32, (ROWS, ROWS), 1) < PATCHES

    def attend(x, layer, gain, qkv_ref, o_ref, p_ref):
        a = (norm_parts(x)[0] * gain).astype(BF)
        qkv_ref[...] = dot(a, wqkv[layer]).astype(BF).reshape(ib, ROWS, 3 * D)
        for i in range(ib):
            for pair in range(HEADS // 2):
                at = 128 * pair
                q = qkv_ref[i, :, at : at + 128] * BF(0.125)
                k = qkv_ref[i, :, D + at : D + at + 128]
                w = qkv_ref[i, :, 2 * D + at : 2 * D + at + 128]
                mixed = []
                for h in range(2):
                    qm = jnp.where(lo if h == 0 else ~lo, q, BF(0))
                    s = jnp.where(valid, dot_t(qm, k), -1e30)
                    s = jnp.exp(s - jnp.max(s, axis=-1, keepdims=True))
                    p = (s * (1.0 / jnp.sum(s, axis=-1, keepdims=True))).astype(BF)
                    p_ref[i, 2 * pair + h] = p
                    mixed.append(dot(p, w))
                o_ref[i, :, at : at + 128] = jnp.where(lo, mixed[0], mixed[1]).astype(BF)
        return x + dot(o_ref[...].reshape(m, D), wo[layer])

    x0 = x_ref[...].astype(F32).reshape(m, D)
    x1 = attend(x0, 0, gains[0:1], qkv1_ref, o1_ref, p1_ref)
    x1_ref[...] = x1.reshape(ib, ROWS, D)
    b = (norm_parts(x1)[0] * gains[1:2]).astype(BF)
    x2 = x1
    for f in range(0, FF, 512):
        u, gp = gelu_parts(dot(b, win[:, f : f + 512]))
        u = u.astype(BF)
        u_ref[:, :, f : f + 512] = u.reshape(ib, ROWS, 512)
        gp_ref[:, :, f : f + 512] = gp.astype(BF).reshape(ib, ROWS, 512)
        x2 = x2 + dot(u, wout[f : f + 512])
    x2_ref[...] = x2.reshape(ib, ROWS, D)
    x3 = attend(x2, 1, gains[2:3], qkv2_ref, o2_ref, p2_ref)
    x3_ref[...] = x3.reshape(ib, ROWS, D)
    c_ref[...] = (norm_parts(x3)[0] * gains[3:4]).astype(BF).reshape(ib, ROWS, D)


def dense_forward(x, gains, wqkv, wo, win, wout):
    n = x.shape[0]
    ib = 2 if n % 2 == 0 else 1

    def out(*shape, dtype=BF):
        return jax.ShapeDtypeStruct((n,) + shape, dtype)

    def block(shape):
        return pl.BlockSpec((ib,) + tuple(shape[1:]), lambda i: (i,) + (0,) * (len(shape) - 1))

    outs = [out(ROWS, D, dtype=F32)] * 3 + [out(ROWS, 3 * D)] * 2 + [out(ROWS, D)] * 2
    outs += [out(HEADS, ROWS, ROWS)] * 2 + [out(ROWS, FF)] * 2 + [out(ROWS, D)]
    return pl.pallas_call(
        fwd_kernel,
        grid=(n // ib,),
        out_shape=outs,
        in_specs=[block(x.shape)] + [VMEM] * 5,
        out_specs=[block(o.shape) for o in outs],
        compiler_params=pltpu.CompilerParams(vmem_limit_bytes=60 << 20),
        name="dense_forward",
    )(x, gains, wqkv, wo, win, wout)


def gate_rows(router_t, c, routes):
    logits = dot_t(router_t, c)
    expert = lax.broadcasted_iota(jnp.int32, logits.shape, 0)
    first, second = expert == routes[0:1], expert == routes[1:2]
    diff = jnp.sum(jnp.where(first, logits, 0.0) - jnp.where(second, logits, 0.0), axis=0, keepdims=True)
    return 1.0 / (1.0 + jnp.exp(-diff)), 1.0 / (1.0 + jnp.exp(diff)), first, second


def experts_kernel(groups, local, exp_axis, *refs):
    c_refs, g_refs, r_refs = refs[:groups], refs[groups : 2 * groups], refs[2 * groups : 3 * groups]
    router_t, win, wout = refs[3 * groups : 3 * groups + 3]
    outs = refs[3 * groups + 3 :]
    eg_ref, y_refs, d_refs, delta_refs = outs[0], outs[1 : groups + 1], outs[groups + 1 : 2 * groups + 1], outs[2 * groups + 1 : 3 * groups + 1]
    ci, g4, rows, cols, slots, acc_out, acc_in, u_scr, gp_scr, back, counts = outs[3 * groups + 1 :]
    n_tok = c_refs[0].shape[0]
    total = groups * n_tok
    step = pl.program_id(0)
    first_expert = lax.axis_index(exp_axis) * local

    @pl.when(step == 0)
    def _():
        for s in range(groups):
            at = s * n_tok
            ci[at : at + n_tok, 0:D] = c_refs[s][...]
            g4[at : at + n_tok] = g_refs[s][...]
        routes = jnp.concatenate([r[0:2] for r in r_refs], axis=1)
        g0, g1, _, _ = gate_rows(router_t[...], ci[:, 0:D], routes)
        mine = first_expert + lax.broadcasted_iota(jnp.int32, (8, total), 0)
        inside = lax.broadcasted_iota(jnp.int32, (8, total), 0) < local
        is0, is1 = (mine == routes[0:1]) & inside, (mine == routes[1:2]) & inside
        member = jnp.where(is0 | is1, 1.0, 0.0)
        lane = lax.broadcasted_iota(jnp.int32, (8, total), 1)
        upto = member
        shift = 1
        while shift < total:
            upto = upto + jnp.where(lane >= shift, pltpu.roll(upto, shift, 1), 0.0)
            shift *= 2
        position = jnp.where(member > 0, upto - 1.0, -1.0)
        rows[0:8] = position
        base = jnp.int32(0)
        starts = []
        for e in range(local):
            n = jnp.sum(member[e : e + 1]).astype(jnp.int32)
            tiles = (n + TILE - 1) // TILE
            counts[e] = tiles
            counts[8 + e] = base
            starts.append((base * TILE).astype(F32))
            base = base + tiles
        counts[16] = base
        start = jnp.zeros((8, total), F32)
        expert_row = lax.broadcasted_iota(jnp.int32, (8, total), 0)
        for e in range(local):
            start = jnp.where(expert_row == e, starts[e], start)
        slot = start + position
        slot0 = jnp.sum(jnp.where(is0, slot + 1.0, 0.0), axis=0, keepdims=True) - 1.0
        slot1 = jnp.sum(jnp.where(is1, slot + 1.0, 0.0), axis=0, keepdims=True) - 1.0
        gates = jnp.where(is0, g0, jnp.where(is1, g1, 0.0))
        sign = jnp.where(is0, 1.0, jnp.where(is1, -1.0, 0.0))
        slot_rows = jnp.where(expert_row == 0, slot0, jnp.where(expert_row == 1, slot1, 0.0))
        stacked = jnp.concatenate([gates, sign, slot_rows, jnp.zeros((104, total), F32)], axis=0)
        lane128 = lax.broadcasted_iota(jnp.int32, (128, 128), 1)
        for at in range(0, total, 128):
            col = stacked[:, at : at + 128].T
            cols[at : at + 128] = col
            low = col - col.astype(BF).astype(F32)
            info = jnp.where(lane128 < 16, col, jnp.where(lane128 < 24, pltpu.roll(low, 16, 1), 0.0))
            ci[at : at + 128, D : D + 128] = info.astype(BF)

    acc_out[...] = jnp.zeros_like(acc_out)
    acc_in[...] = jnp.zeros_like(acc_in)
    position = rows[pl.ds(step, 1)]
    lane = lax.broadcasted_iota(jnp.int32, (TILE, 128), 1)

    def tile(j, _):
        slot = (j * TILE + lax.broadcasted_iota(jnp.int32, (TILE, total), 0)).astype(F32)
        pick = jnp.where(position == slot, 1.0, 0.0).astype(BF)
        xi = dot(pick, ci[...])
        g4r = dot(pick, g4[...])
        x = xi[:, 0:D].astype(BF)
        info = xi[:, D : D + 128]
        gate = jnp.sum(jnp.where((lane == step) | (lane == step + 16), info, 0.0), axis=-1, keepdims=True)
        sign = jnp.sum(jnp.where(lane == step + 8, info, 0.0), axis=-1, keepdims=True)
        dy = (gate * g4r).astype(BF)
        for f in range(0, FF, 512):
            u, gp = gelu_parts(dot(x, win[0, :, f : f + 512]))
            u_scr[:, f : f + 512] = u.astype(BF)
            gp_scr[:, f : f + 512] = gp.astype(BF)
        ey = dot(u_scr[...], wout[0]).astype(BF).astype(F32)
        dg = sign * jnp.sum(g4r * ey, axis=-1, keepdims=True)
        acc_out[...] += t_dot(u_scr[...], dy)
        for f in range(0, FF, 512):
            du = dot_t(dy, wout[0, f : f + 512])
            gp_scr[:, f : f + 512] = (du * gp_scr[:, f : f + 512].astype(F32)).astype(BF)
        dcp = dot_t(gp_scr[...], win[0])
        acc_in[...] += t_dot(gp_scr[...], x)
        at = pl.multiple_of((counts[8 + step] + j) * TILE, TILE)
        slots[pl.ds(at, TILE), 0:D] = (gate * ey).astype(BF)
        slots[pl.ds(at, TILE), D : 2 * D] = dcp.astype(BF)
        low = dg - dg.astype(BF).astype(F32)
        slots[pl.ds(at, TILE), 2 * D : 2 * D + 128] = jnp.where(lane == 0, dg, jnp.where(lane == 1, low, 0.0)).astype(BF)
        return 0

    lax.fori_loop(0, counts[step], tile, 0)
    eg_ref[0, 0] = acc_in[...].astype(BF).reshape(eg_ref.shape[2:])
    eg_ref[0, 1] = acc_out[...].astype(BF).reshape(eg_ref.shape[2:])

    @pl.when(step == local - 1)
    def _():
        used = counts[16]
        chunks = (used * TILE + CHUNK - 1) // CHUNK

        def clear(j, _):
            at = pl.multiple_of(j * TILE, TILE)
            slots[pl.ds(at, TILE)] = jnp.zeros((TILE, 2 * D + 128), BF)
            return 0

        lax.fori_loop(used, chunks * (CHUNK // TILE), clear, 0)
        lane_chunk = lax.broadcasted_iota(jnp.int32, (ROWS, CHUNK), 1)

        for s in range(groups):
            for b in range(n_tok // ROWS):
                at = s * n_tok + b * ROWS
                slot0, slot1 = cols[at : at + ROWS, 16:17], cols[at : at + ROWS, 17:18]
                back[...] = jnp.zeros_like(back)

                def gather(j, _):
                    slot = (j * CHUNK + lane_chunk).astype(F32)
                    pick = jnp.where((slot0 == slot) | (slot1 == slot), 1.0, 0.0).astype(BF)
                    back[...] += dot(pick, slots[pl.ds(pl.multiple_of(j * CHUNK, CHUNK), CHUNK)])
                    return 0

                lax.fori_loop(0, chunks, gather, 0)
                y_refs[s][b * ROWS : (b + 1) * ROWS] = back[:, 0:D].astype(BF)
                d_refs[s][b * ROWS : (b + 1) * ROWS] = back[:, D : 2 * D].astype(BF)
                cols[at : at + ROWS] = back[:, 2 * D : 2 * D + 128]
        for at in range(0, total, 128):
            rows[:, at : at + 128] = cols[at : at + 128].T[0:8]
        for s in range(groups):
            delta_refs[s][...] = rows[:, s * n_tok : (s + 1) * n_tok]


def experts_all(cs, gs, rs, router_t, win, wout, slots_most, owners):
    groups = len(cs)
    local = win.shape[0]
    n_tok = cs[0].shape[0]
    total = groups * n_tok
    room = -(-(slots_most + local * TILE) // CHUNK) * CHUNK

    def full(shape):
        return pl.BlockSpec(tuple(shape), lambda i: (0,) * len(shape))

    outs = [jax.ShapeDtypeStruct((local, 2) + owners + (FF // math.prod(owners), D), BF)]
    outs += [jax.ShapeDtypeStruct((n_tok, D), BF)] * (2 * groups)
    outs += [jax.ShapeDtypeStruct((8, n_tok), F32)] * groups
    result = pl.pallas_call(
        functools.partial(experts_kernel, groups, local, "exp"),
        grid=(local,),
        out_shape=outs,
        in_specs=[VMEM] * (3 * groups + 1)
        + [pl.BlockSpec((1, D, FF), lambda i: (i, 0, 0)), pl.BlockSpec((1, FF, D), lambda i: (i, 0, 0))],
        out_specs=[pl.BlockSpec((1,) + outs[0].shape[1:], lambda i: (i,) + (0,) * (len(outs[0].shape) - 1))] + [full(o.shape) for o in outs[1:]],
        scratch_shapes=[
            pltpu.VMEM((total, D + 128), BF),
            pltpu.VMEM((total, D), BF),
            pltpu.VMEM((8, total), F32),
            pltpu.VMEM((total, 128), F32),
            pltpu.VMEM((room, 2 * D + 128), BF),
            pltpu.VMEM((FF, D), F32),
            pltpu.VMEM((FF, D), F32),
            pltpu.VMEM((TILE, FF), BF),
            pltpu.VMEM((TILE, FF), BF),
            pltpu.VMEM((ROWS, 2 * D + 128), F32),
            pltpu.SMEM((24,), jnp.int32),
        ],
        compiler_params=pltpu.CompilerParams(vmem_limit_bytes=60 << 20),
        name="experts",
    )(*cs, *gs, *rs, router_t, win, wout)
    return result[0], result[1 : groups + 1], result[groups + 1 : 2 * groups + 1], result[2 * groups + 1 :]


OUTER, SHARE = 4, 48
MESH = pl.DeviceIdType.MESH


class Place:
    def __init__(self):
        r = lax.axis_index("rep")
        self.y = lax.axis_index("exp")
        self.z, self.x, self.c = r // 4, (r // 2) % 2, r % 2
        self.core = (r + 1 - 2 * self.c, self.y)
        self.across = (r + 2 - 4 * self.x, self.y)
        self.beside = (r, 1 - self.y)
        self.along = [((self.z + k) % OUTER) for k in range(1, OUTER)]

    def at_z(self, z):
        return (z * 4 + self.x * 2 + self.c, self.y)

    def meet(self, partners):
        barrier = pltpu.get_barrier_semaphore()
        for partner in partners:
            pl.semaphore_signal(barrier, inc=1, device_id=partner, device_id_type=MESH)
        pl.semaphore_wait(barrier, len(partners))


class Links:
    def __init__(self, send, recv):
        self.send, self.recv, self.used = send, recv, 0

    def reserve(self, count):
        first = self.used
        self.used += count
        return first

    def copy(self, at, src, dst, device):
        return pltpu.make_async_remote_copy(
            src_ref=src, dst_ref=dst, send_sem=self.send.at[at], recv_sem=self.recv.at[at],
            device_id=device, device_id_type=MESH,
        )

    def start(self, at, src, dst, device):
        copy = self.copy(at, src, dst, device)
        copy.start()
        return copy


def add_into(count, target, *others):
    def block(i, _):
        total = target(i)[...].astype(F32)
        for other in others:
            total = total + other(i)[...].astype(F32)
        target(i)[...] = total.astype(target(i).dtype)
        return 0

    lax.fori_loop(0, count, block, 0)


class ExpertSums:
    COPIES = 2 + OUTER - 1

    def __init__(self, place, links, eg, own, part, x_rx, z_rx, out, local_sem):
        self.p, self.links, self.out, self.sem = place, links, out, local_sem
        self.eg, self.own, self.part, self.x_rx, self.z_rx = eg, own, part, x_rx, z_rx
        self.count = eg.shape[0]
        self.first = links.reserve(self.count * self.COPIES)

    def load(self, j):
        return pltpu.make_async_copy(self.eg.at[j, :, :, :, self.p.c], self.own.at[j % 2], self.sem.at[j % 2])

    def core_copy(self, j):
        return self.links.copy(
            self.first + j * self.COPIES, self.eg.at[j, :, :, :, 1 - self.p.c], self.part.at[j], self.p.core
        )

    def across_copy(self, j):
        return self.links.copy(
            self.first + j * self.COPIES + 1, self.part.at[j, :, :, 1 - self.p.x], self.x_rx.at[j], self.p.across
        )

    def along_copy(self, j, k):
        z = self.p.along[k]
        return self.links.copy(
            self.first + j * self.COPIES + 2 + k, self.part.at[j, :, z, self.p.x], self.z_rx.at[j, k], self.p.at_z(z)
        )

    def core(self, j):
        if j < 2:
            self.load(j).start()
        self.core_copy(j).start()

    def across(self, j):
        p = self.p

        def add(x):
            add_into(
                2 * OUTER,
                lambda i: self.part.at[j, i // OUTER, i % OUTER, x],
                lambda i: self.own.at[j % 2, i // OUTER, i % OUTER, x],
            )

        self.load(j).wait()
        self.core_copy(j).wait()
        add(1 - p.x)
        self.across_copy(j).start()
        add(p.x)
        if j + 2 < self.count:
            self.load(j + 2).start()

    def along(self, j):
        p = self.p
        self.across_copy(j).wait()
        add_into(
            2 * OUTER,
            lambda i: self.part.at[j, i // OUTER, i % OUTER, p.x],
            lambda i: self.x_rx.at[j, i // OUTER, i % OUTER],
        )
        for k in range(OUTER - 1):
            self.along_copy(j, k).start()

    def finish(self, j):
        p = self.p
        for k in range(OUTER - 1):
            self.along_copy(j, k).wait()
        for half in range(2):
            total = self.part[j, half, p.z, p.x].astype(F32)
            for k in range(OUTER - 1):
                total = total + self.z_rx[j, k, half].astype(F32)
            self.out[j, half] = total


class SharedSum:
    COPIES = 2 * (3 + OUTER - 1)

    def __init__(self, place, links, g, src, rx1, rx2, rx3, rx4, out):
        self.p, self.links, self.out = place, links, out.at[g]
        self.src, self.rx1, self.rx2, self.rx3, self.rx4 = src.at[g], rx1.at[g], rx2.at[g], rx3.at[g], rx4.at[g]
        self.at = links.reserve(self.COPIES)

    def start(self, *args):
        copy = self.links.start(self.at, *args)
        self.at += 1
        return copy

    def core(self):
        p = self.p
        self.c = self.start(self.src.at[1 - p.c], self.rx1, p.core)

    def beside(self):
        p = self.p
        self.c.wait()
        for y in (1 - p.y, p.y):
            add_into(
                2,
                lambda i: self.src.at[p.c, y, i],
                lambda i: self.rx1.at[y, i],
            )
            if y is not p.y:
                self.c = self.start(self.src.at[p.c, y], self.rx2, p.beside)

    def across(self):
        p = self.p
        self.c.wait()
        for x in (1 - p.x, p.x):
            add_into(1, lambda i: self.src.at[p.c, p.y, x], lambda i: self.rx2.at[x])
            if x is not p.x:
                self.c = self.start(self.src.at[p.c, p.y, x], self.rx3, p.across)

    def along(self):
        p = self.p
        self.c.wait()
        add_into(1, lambda i: self.src.at[p.c, p.y, p.x], lambda i: self.rx3)
        self.cs = [
            self.start(self.src.at[p.c, p.y, p.x, z], self.rx4.at[k], p.at_z(z)) for k, z in enumerate(p.along)
        ]

    def out_along(self):
        p = self.p
        for c in self.cs:
            c.wait()
        total = self.src[p.c, p.y, p.x, p.z].astype(F32)
        for k in range(OUTER - 1):
            total = total + self.rx4[k].astype(F32)
        mine = self.out.at[p.c, p.y, p.x, p.z]
        mine[...] = total.astype(BF)
        self.cs = [self.start(mine, mine, p.at_z(z)) for z in p.along]

    def out_across(self):
        p = self.p
        for c in self.cs:
            c.wait()
        mine = self.out.at[p.c, p.y, p.x]
        self.c = self.start(mine, mine, p.across)

    def out_beside(self):
        p = self.p
        self.c.wait()
        mine = self.out.at[p.c, p.y]
        self.c = self.start(mine, mine, p.beside)

    def out_core(self):
        p = self.p
        self.c.wait()
        mine = self.out.at[p.c]
        self.c = self.start(mine, mine, p.core)

    def finish(self):
        self.c.wait()


class SmallSum:
    COPIES = 3 + OUTER - 1

    def __init__(self, place, links, src, rx):
        self.p, self.links, self.src, self.rx = place, links, src, rx
        self.first = links.reserve(self.COPIES)

    def step(self, k):
        if k == 3:
            return self.along()
        device = (self.p.core, self.p.beside, self.p.across)[k]
        if k:
            self.c.wait()
            self.src[k] = self.src[k - 1] + self.rx[k - 1]
        self.c = self.links.start(self.first + k, self.src.at[k], self.rx.at[k], device)

    def along(self):
        self.c.wait()
        self.src[3] = self.src[2] + self.rx[2]
        self.cs = [
            self.links.start(self.first + 3 + k, self.src.at[3], self.rx.at[3 + k], self.p.at_z(z))
            for k, z in enumerate(self.p.along)
        ]

    def finish(self, out):
        for c in self.cs:
            c.wait()
        total = self.src[3]
        for k in range(OUTER - 1):
            total = total + self.rx[3 + k]
        out[...] = total


ORDER = (
    ("E", 1, "core"), ("d", 0, ""), ("run", 0, ""), ("d", 1, ""), ("E", 1, "across"), ("E", 0, "core"), ("d", 2, ""),
    ("E", 3, "core"), ("run", 1, ""), ("d", 3, ""), ("run", 2, ""), ("run", 3, ""), ("E", 0, "across"),
    ("run", 4, ""), ("E", 1, "along"), ("run", 5, ""), ("S", 0, "core"), ("run", 6, ""), ("run", 7, ""),
    ("run", 8, ""), ("run", 9, ""), ("S", 0, "beside"), ("run", 10, ""), ("E", 3, "across"), ("run", 11, ""),
    ("S", 1, "core"), ("E", 0, "along"), ("run", 12, ""), ("S", 1, "beside"), ("run", 13, ""), ("S", 2, "core"),
    ("S", 0, "across"), ("E", 2, "core"), ("run", 14, ""), ("run", 15, ""), ("S", 2, "beside"), ("run", 16, ""),
    ("S", 0, "along"), ("S", 1, "across"), ("run", 17, ""), ("run", 18, ""), ("S", 3, "core"), ("E", 0, "finish"),
    ("S", 0, "out_along"), ("S", 1, "along"), ("S", 3, "beside"), ("S", 2, "across"), ("E", 1, "finish"),
    ("run", 19, ""), ("few", 0, ""), ("S", 2, "along"), ("S", 0, "out_across"), ("E", 3, "along"), ("few", 1, ""),
    ("y", 0, ""), ("S", 1, "out_along"), ("S", 3, "across"), ("S", 0, "out_beside"), ("few", 2, ""),
    ("E", 2, "across"), ("S", 2, "out_along"), ("S", 3, "along"), ("few", 3, ""), ("S", 1, "out_across"),
    ("S", 2, "out_across"), ("S", 3, "out_along"), ("few", 4, ""), ("S", 1, "out_beside"), ("S", 2, "out_beside"),
    ("S", 3, "out_across"), ("E", 2, "along"), ("S", 1, "out_core"), ("S", 3, "out_beside"), ("S", 0, "out_core"),
    ("E", 3, "finish"), ("S", 2, "out_core"), ("S", 3, "out_core"), ("E", 2, "finish"), ("S", 0, "finish"),
    ("S", 2, "finish"), ("S", 1, "finish"), ("run", 20, ""), ("S", 3, "finish"),
)

LOADED = ("c", "x3", "cot", "d", "delta", "x2", "qkv", "o", "p", "wo", "wqkv", "x1", "wout", "gp", "u", "win", "y", "x0")


def bwd_kernel(linked, *refs):
    names = ["gains", "router_t", "routes", "wqkv", "wo", "win", "wout", "x0", "x1", "x2", "x3", "qkv1", "qkv2"]
    names += ["o1", "o2", "p1", "p2", "u", "gp", "c", "cot", "d", "delta", "y"]
    if linked:
        names += ["d_send", "delta_send", "y_send", "eg"]
    names += ["act_out", "gin_out", "shared_out", "small_out"]
    if linked:
        names += ["eg_out"]
    names += ["v_" + n for n in LOADED] + ["gv", "a_scr", "dbr_scr", "dqkv_scr", "sem"]
    if linked:
        names += ["d_rx", "delta_rx", "y_rx", "own", "part", "x_rx", "z_rx", "src", "rx1", "rx2", "rx3", "rx4"]
        names += ["small_src", "small_rx", "eg_sem", "send", "recv"]
    r = dict(zip(names, refs, strict=True))
    gains, gv, a_scr, dbr_scr, dqkv_scr = (r[n] for n in ("gains", "gv", "a_scr", "dbr_scr", "dqkv_scr"))
    images = gv.shape[0]
    m = images * ROWS
    lo = lane_low(ROWS)

    second = {"qkv": "qkv2", "o": "o2", "p": "p2"}
    copies = {}

    def fetch(name, source):
        copies[name] = pltpu.make_async_copy(r[source], r["v_" + name], r["sem"].at[LOADED.index(name)])
        copies[name].start()

    def need(*wanted):
        for name in wanted:
            copies[name].wait()

    if linked:
        place = Place()
        links = Links(r["send"], r["recv"])
        place.meet([place.core, place.across, place.beside] + [place.at_z(z) for z in place.along])
        delta_copy = links.start(links.reserve(1), r["delta_send"], r["delta_rx"], place.beside)
        d_first = links.reserve(images)

        def d_copy(i):
            return links.copy(d_first + i, r["d_send"].at[i], r["d_rx"].at[i], place.beside)

        experts = ExpertSums(
            place, links, r["eg"], r["own"], r["part"], r["x_rx"], r["z_rx"], r["eg_out"], r["eg_sem"]
        )
        y_copy = links.copy(links.reserve(1), r["y_send"], r["y_rx"], place.beside)
        sums = [
            SharedSum(place, links, g, r["src"], r["rx1"], r["rx2"], r["rx3"], r["rx4"], r["shared_out"])
            for g in range(4)
        ]
        few = SmallSum(place, links, r["small_src"], r["small_rx"])
        shared, small = r["src"], r["small_src"].at[0]
        small[...] = jnp.zeros(small.shape, F32)
    else:
        shared, small = r["shared_out"], r["small_out"]
    for name in LOADED:
        fetch(name, second.get(name, name))

    def keep(block, value):
        if linked:
            shared[block // 4, (block % 4) // 2, block % 2] = value.astype(BF).reshape(2, OUTER, SHARE, D)
        else:
            shared[block] = value.astype(BF)

    def router():
        need("c", "delta")
        c_all = r["v_c"][...].reshape(m, D)
        g0, g1, first, other = gate_rows(r["router_t"][...], c_all, r["routes"][...])
        delta = r["v_delta"][0:1] + r["v_delta"][1:2]
        if linked:
            delta_copy.wait()
            delta = delta + (r["delta_rx"][0:1] + r["delta_rx"][1:2])
        dl = g0 * g1 * delta
        dlog = jnp.where(first, dl, jnp.where(other, -dl, 0.0)).astype(BF)
        small[4 : 4 + dlog.shape[0]] = dot(dlog, c_all)
        small[0:4] = jnp.zeros((4, D), F32)
        gv[...] = t_dot(dlog, r["router_t"][...]).reshape(images, ROWS, D)
        need("x3", "cot", "d")

    def add_gain(row, by_gain):
        small[row : row + 1] += jnp.sum(by_gain, axis=0, keepdims=True)

    def first(i):
        dc = gv[i] + r["v_d"][i].astype(F32)
        if linked:
            d_copy(i).wait()
            dc = dc + r["d_rx"][i].astype(F32)
        dx, by_gain = norm_back(dc, r["v_x3"][i], gains[3:4])
        gv[i] = r["v_cot"][i].astype(F32) + dx
        add_gain(3, by_gain)
        if i == 0:
            need("x2", "qkv", "o", "p", "wo")
        attend_image(i, 1, gains[2:3], r["v_x2"])

    def attend_image(i, layer, gain, x):
        qkv, o, p = r["v_qkv"], r["v_o"], r["v_p"]
        a_scr[i] = (norm_parts(x[i].astype(F32))[0] * gain).astype(BF)
        dbr = gv[i].astype(BF)
        dbr_scr[i] = dbr
        do = dot_t(dbr, r["v_wo"][layer]).astype(BF)
        dod = do.astype(F32) * o[i].astype(F32)
        for pair in range(HEADS // 2):
            at = 128 * pair
            q = qkv[i, :, at : at + 128] * BF(0.125)
            k = qkv[i, :, D + at : D + at + 128]
            w = qkv[i, :, 2 * D + at : 2 * D + at + 128]
            dqs, dk, dw = [], 0.0, 0.0
            for h in range(2):
                mask = lo if h == 0 else ~lo
                dom = jnp.where(mask, do[:, at : at + 128], BF(0))
                inner = jnp.sum(jnp.where(mask, dod[:, at : at + 128], 0.0), axis=-1, keepdims=True)
                ph = p[i, 2 * pair + h]
                ds = (ph.astype(F32) * (dot_t(dom, w) - inner)).astype(BF)
                dw = dw + t_dot(ph, dom)
                dqs.append(dot(ds, k))
                dk = dk + t_dot(ds, jnp.where(mask, q, BF(0)))
            dqkv_scr[i, :, at : at + 128] = (jnp.where(lo, dqs[0], dqs[1]) * 0.125).astype(BF)
            dqkv_scr[i, :, D + at : D + at + 128] = dk.astype(BF)
            dqkv_scr[i, :, 2 * D + at : 2 * D + at + 128] = dw.astype(BF)

    def attend_weights(block):
        a_all = a_scr[...].reshape(m, D)
        for f in range(3):
            keep(block + f, t_dot(a_all, dqkv_scr[:, :, f * D : f * D + D].reshape(m, D)))
        keep(block + 3, t_dot(r["v_o"][...].reshape(m, D), dbr_scr[...].reshape(m, D)))

    def close(x, layer, row, out):
        def image(i, _):
            da = dot_t(dqkv_scr[i], r["v_wqkv"][layer])
            dx, by_gain = norm_back(da, x[i].astype(F32), gains[row : row + 1])
            out[i] = gv[i] + dx
            add_gain(row, by_gain)
            return 0

        lax.fori_loop(0, images, image, 0)

    def first_close():
        for name in ("qkv", "o", "p"):
            fetch(name, name + "1")
        need("wqkv")
        close(r["v_x2"], 1, 2, gv)
        need("x1", "wout", "gp", "u", "win")

    gp = r["v_gp"]

    def mlp(i):
        a_scr[i] = (norm_parts(r["v_x1"][i])[0] * gains[1:2]).astype(BF)
        dm = gv[i].astype(BF)
        dbr_scr[i] = dm
        for f in range(0, FF, 512):
            du = dot_t(dm, r["v_wout"][f : f + 512])
            gp[i, :, f : f + 512] = (du * gp[i, :, f : f + 512].astype(F32)).astype(BF)

    def mlp_out_weights():
        dm_all = dbr_scr[...].reshape(m, D)
        for f in range(4):
            keep(4 + f, t_dot(r["v_u"][:, :, f * D : f * D + D].reshape(m, D), dm_all))

    def mlp_in_weights():
        b_all = a_scr[...].reshape(m, D)
        for f in range(4):
            keep(8 + f, t_dot(b_all, gp[:, :, f * D : f * D + D].reshape(m, D)))

    def mlp_close():
        def image(i, _):
            db = dot_t(gp[i], r["v_win"][...])
            dx, by_gain = norm_back(db, r["v_x1"][i], gains[1:2])
            gv[i] = gv[i] + dx
            add_gain(1, by_gain)
            return 0

        lax.fori_loop(0, images, image, 0)
        need("x0", "qkv", "o", "p")

    def last(i):
        attend_image(i, 0, gains[0:1], r["v_x0"])

    def last_close():
        close(r["v_x0"], 0, 0, r["gin_out"])

    def act():
        need("y")
        if linked:
            y_copy.wait()
        for i in range(images):
            x4 = r["v_x3"][i] + r["v_y"][i].astype(F32)
            if linked:
                x4 = x4 + r["y_rx"][i].astype(F32)
            r["act_out"][i] = x4.astype(BF)

    compute = [router] + [functools.partial(first, i) for i in range(images)]
    compute += [lambda: attend_weights(0), first_close] + [functools.partial(mlp, i) for i in range(images)]
    compute += [mlp_out_weights, mlp_in_weights, mlp_close] + [functools.partial(last, i) for i in range(images)]
    compute += [lambda: attend_weights(12), last_close, act]
    if not linked:
        for step in compute:
            step()
        return
    done = 0
    for kind, at, what in ORDER:
        if kind == "run":
            compute[done]()
            done += 1
        elif kind == "d":
            d_copy(at).start()
        elif kind == "y":
            y_copy.start()
        elif kind == "few" and at < 4:
            few.step(at)
        elif kind == "few":
            few.finish(r["small_out"])
        elif kind == "E":
            getattr(experts, what)(at)
        else:
            getattr(sums[at], what)()


def dense_backward(weights, router_t, routes, saved, cot, d, delta, y, sent=None):
    gains, wqkv, wo, win, wout = weights
    x0, x1, x2, x3, qkv1, qkv2, o1, o2, p1, p2, u, gp, c = saved
    images = x0.shape[0]
    linked = sent is not None
    small_rows = 16 if linked else 4 + router_t.shape[0]
    ins = [gains, router_t, routes, wqkv, wo, win, wout, *saved, cot, d, delta, y] + (list(sent) if linked else [])
    outs = [
        jax.ShapeDtypeStruct((images, ROWS, D), BF),
        jax.ShapeDtypeStruct((images, ROWS, D), F32),
        jax.ShapeDtypeStruct((4, 2, 2, 2, OUTER, SHARE, D) if linked else (16, D, D), BF),
        jax.ShapeDtypeStruct((small_rows, D), F32),
    ]
    vm = pltpu.VMEM
    loaded = dict(
        c=c, x3=x3, cot=cot, d=d, delta=delta, x2=x2, qkv=qkv1, o=o1, p=p1, wo=wo, wqkv=wqkv, x1=x1, wout=wout,
        gp=gp, u=u, win=win, y=y, x0=x0,
    )
    scratch = [vm(loaded[name].shape, loaded[name].dtype) for name in LOADED]
    scratch += [vm((images, ROWS, D), F32), vm((images, ROWS, D), BF), vm((images, ROWS, D), BF)]
    scratch += [vm((images, ROWS, 3 * D), BF), pltpu.SemaphoreType.DMA((len(LOADED),))]
    params = dict(vmem_limit_bytes=62 << 20)
    if linked:
        eg = sent[-1]
        local, share = eg.shape[0], eg.shape[-2]
        outs.append(jax.ShapeDtypeStruct((local, 2, share, D), F32))
        copies = 2 + images + local * ExpertSums.COPIES + 4 * SharedSum.COPIES + SmallSum.COPIES
        scratch += [vm(d.shape, BF), vm(delta.shape, F32), vm(y.shape, BF)]
        scratch += [
            vm((2, 2, OUTER, 2, share, D), BF),
            vm((local, 2, OUTER, 2, share, D), BF),
            vm((local, 2, OUTER, share, D), BF),
            vm((local, OUTER - 1, 2, share, D), BF),
            vm((4, 2, 2, 2, OUTER, SHARE, D), BF),
            vm((4, 2, 2, OUTER, SHARE, D), BF),
            vm((4, 2, OUTER, SHARE, D), BF),
            vm((4, OUTER, SHARE, D), BF),
            vm((4, OUTER - 1, SHARE, D), BF),
            vm((4, small_rows, D), F32),
            vm((OUTER + 2, small_rows, D), F32),
            pltpu.SemaphoreType.DMA((2,)),
            pltpu.SemaphoreType.DMA((copies,)),
            pltpu.SemaphoreType.DMA((copies,)),
        ]
        params.update(collective_id=1, has_side_effects=True)
    return pl.pallas_call(
        functools.partial(bwd_kernel, linked),
        out_shape=outs,
        in_specs=[VMEM] * 3 + [pl.BlockSpec(memory_space=pl.ANY)] * (len(ins) - 3),
        out_specs=[VMEM] * len(outs),
        scratch_shapes=scratch,
        compiler_params=pltpu.CompilerParams(**params),
        name="dense_backward",
    )(*ins)


def finish_kernel(
    act, gin, shared, small, eg, act_out, gin_out, qkv_out, proj_out, gain_out, mlp_in_out, mlp_out_out, router_out,
    in_out, out_out, v_shared, v_wide, v_gin, v_act, in_sem, out_sem,
):
    images = act.shape[0]
    blocks = v_shared.shape[0]
    targets = {3: proj_out.at[1], 15: proj_out.at[0]}
    for f in range(3):
        targets[f] = qkv_out.at[1, :, pl.ds(f * D, D)]
        targets[12 + f] = qkv_out.at[0, :, pl.ds(f * D, D)]
    for f in range(4):
        targets[4 + f] = mlp_out_out.at[pl.ds(f * D, D)]
        targets[8 + f] = mlp_in_out.at[:, pl.ds(f * D, D)]

    def load(b):
        return pltpu.make_async_copy(shared.at[b], v_shared.at[b], in_sem.at[b])

    def store(b):
        return pltpu.make_async_copy(v_wide.at[b], targets[b], out_sem.at[b])

    load_gin = pltpu.make_async_copy(gin, v_gin, in_sem.at[blocks])
    load_act = pltpu.make_async_copy(act, v_act, in_sem.at[blocks + 1])
    for b in range(blocks):
        load(b).start()
    load_gin.start()
    load_act.start()
    gain_out[...] = small[0:4]
    router_out[...] = small[4 : 4 + router_out.shape[0]]
    for e in range(eg.shape[0]):
        in_out[e] = eg[e, 0]
        out_out[e] = eg[e, 1]
    for b in range(blocks):
        load(b).wait()
        v_wide[b] = v_shared[b].astype(F32)
        store(b).start()
    load_gin.wait()
    load_act.wait()
    for i in range(images):
        gin_out[i * PATCHES : (i + 1) * PATCHES] = v_act[i, 0:PATCHES].astype(F32)
    act_out[...] = gin_out[...].astype(BF)
    for i in range(images):
        gin_out[i * PATCHES : (i + 1) * PATCHES] = v_gin[i, 0:PATCHES]
    for b in range(blocks):
        store(b).wait()


def finish(act, gin, shared, small, eg, experts):
    images, local, share = act.shape[0], eg.shape[0], eg.shape[2]
    row_count = images * PATCHES
    outs = [
        jax.ShapeDtypeStruct((row_count, D), BF),
        jax.ShapeDtypeStruct((row_count, D), F32),
        jax.ShapeDtypeStruct((2, D, 3 * D), F32),
        jax.ShapeDtypeStruct((2, D, D), F32),
        jax.ShapeDtypeStruct((4, D), F32),
        jax.ShapeDtypeStruct((D, FF), F32),
        jax.ShapeDtypeStruct((FF, D), F32),
        jax.ShapeDtypeStruct((experts, D), F32),
        jax.ShapeDtypeStruct((local, share, D), F32),
        jax.ShapeDtypeStruct((local, share, D), F32),
    ]
    far = pl.BlockSpec(memory_space=pl.ANY)
    return pl.pallas_call(
        finish_kernel,
        out_shape=outs,
        in_specs=[far, far, far, VMEM, VMEM],
        out_specs=[VMEM, VMEM, far, far, VMEM, far, far, VMEM, VMEM, VMEM],
        scratch_shapes=[
            pltpu.VMEM(shared.shape, BF),
            pltpu.VMEM(shared.shape, F32),
            pltpu.VMEM(gin.shape, F32),
            pltpu.VMEM(act.shape, BF),
            pltpu.SemaphoreType.DMA((shared.shape[0] + 2,)),
            pltpu.SemaphoreType.DMA((shared.shape[0],)),
        ],
        compiler_params=pltpu.CompilerParams(vmem_limit_bytes=62 << 20),
        name="finish",
    )(act, gin, shared, small, eg)


def from_peer(array, groups, shift):
    return lax.ppermute(array, "exp", [(i, (i + shift) % groups) for i in range(groups)])


def pad_images(rows):
    rows = rows.reshape(-1, PATCHES, rows.shape[-1])
    return jnp.pad(rows, ((0, 0), (0, ROWS - PATCHES), (0, 0)))


def shards(
    tokens, routes, norm_gains, attn_qkv, attn_out, mlp_in, mlp_out, router, experts_in, experts_out, cotangent
):
    row_count = tokens.shape[0]
    groups = lax.axis_size("exp")
    local = experts_in.shape[0]
    choices = routes.shape[1]
    capacity = 2 * choices * row_count // (local * groups)
    images = row_count // PATCHES
    n_tok = images * ROWS
    x0, cot = pad_images(tokens), pad_images(cotangent)
    routes_t = routes.T.reshape(choices, images, PATCHES)
    routes_t = jnp.pad(routes_t, ((0, 8 - choices), (0, 0), (0, ROWS - PATCHES)), constant_values=-1)
    routes_t = routes_t.reshape(8, n_tok)
    router_t = router.T
    flat = cot.reshape(n_tok, D)
    gs = [flat] + [from_peer(flat, groups, k) for k in range(1, groups)]
    rs = [routes_t] + [from_peer(routes_t, groups, k) for k in range(1, groups)]
    x1, x2, x3, qkv1, qkv2, o1, o2, p1, p2, u, gp, c = dense_forward(
        x0, norm_gains, attn_qkv, attn_out, mlp_in, mlp_out
    )
    c_flat = c.reshape(n_tok, D)
    cs = [c_flat] + [from_peer(c_flat, groups, k) for k in range(1, groups)]
    rep = lax.axis_size("rep")
    known = (rep, groups, local) == (16, 2, 4)
    owners = (OUTER, 2, 2) if known else (rep,)
    eg, ys, ds, deltas = experts_all(
        cs, gs, rs, router_t, experts_in, experts_out, local * capacity * groups, owners
    )

    weights = (norm_gains, attn_qkv, attn_out, mlp_in, mlp_out)
    saved = (x0, x1, x2, x3, qkv1, qkv2, o1, o2, p1, p2, u, gp, c)
    by_image = (images, ROWS, D)
    experts = router_t.shape[0]
    if known:
        sent = (ds[1].reshape(by_image), deltas[1], ys[1].reshape(by_image), eg)
        act, gin, shared, small, eg = dense_backward(
            weights, router_t, routes_t, saved, cot, ds[0].reshape(by_image), deltas[0], ys[0].reshape(by_image), sent
        )
        shared = shared.reshape(16, D, D)
    else:

        def back(parts):
            total = parts[0].astype(F32)
            for k in range(1, groups):
                total = total + from_peer(parts[k], groups, groups - k).astype(F32)
            return total

        d, delta, y = back(ds).astype(BF), back(deltas), back(ys).astype(BF)
        act, gin, shared, small = dense_backward(
            weights, router_t, routes_t, saved, cot, d.reshape(by_image), delta, y.reshape(by_image)
        )
        eg = lax.psum_scatter(eg, "rep", scatter_dimension=2, tiled=True).reshape(local, 2, FF // rep, D).astype(F32)
        shared, small = lax.psum((shared, small), ("rep", "exp"))
    outs = list(finish(act, gin, shared, small, eg, experts))
    outs[7] = outs[7].T
    outs[8] = jnp.swapaxes(outs[8], 1, 2)
    return tuple(outs)


def solution(mesh):
    rows = P(("rep", "exp"), None)
    return jax.shard_map(
        shards,
        mesh=mesh,
        in_specs=(rows, rows, P(), P(), P(), P(), P(), P(), P("exp", None, None), P("exp", None, None), rows),
        out_specs=(rows, rows, P(), P(), P(), P(), P(), P(), P("exp", None, "rep"), P("exp", "rep", None)),
        check_vma=False,
    )
```

```python
import functools
import math

import jax
import jax.numpy as jnp
from jax import lax
from jax.experimental import pallas as pl
from jax.experimental.pallas import tpu as pltpu
from jax.sharding import PartitionSpec as P

F32 = jnp.float32
BF = jnp.bfloat16
HEADS = 6
PATCHES = 197
ROWS = 208
EPS = 1e-6
TILE = 256
D = 384
FF = 1536
VMEM = pl.BlockSpec(memory_space=pltpu.VMEM)


def dot(a, b):
    return lax.dot_general(a, b, (((1,), (0,)), ((), ())), preferred_element_type=F32)


def dot_t(a, b):
    return lax.dot_general(a, b, (((1,), (1,)), ((), ())), preferred_element_type=F32)


def t_dot(a, b):
    return lax.dot_general(a, b, (((0,), (0,)), ((), ())), preferred_element_type=F32)


def norm_parts(x):
    centred = x - jnp.mean(x, axis=-1, keepdims=True)
    rstd = lax.rsqrt(jnp.mean(centred * centred, axis=-1, keepdims=True) + EPS)
    return centred * rstd, rstd


def norm_back(grad, x, gain):
    xh, rstd = norm_parts(x)
    dxh = grad * gain
    inner = dxh - jnp.mean(dxh, axis=-1, keepdims=True)
    return rstd * (inner - xh * jnp.mean(dxh * xh, axis=-1, keepdims=True)), grad * xh


def gelu_parts(h):
    t = 1.0 / (1.0 + (0.3275911 * 0.7071067811865476) * jnp.abs(h))
    e = jnp.exp(-0.5 * h * h)
    poly = t * (
        0.254829592
        + t * (-0.284496736 + t * (1.421413741 + t * (-1.453152027 + t * 1.061405429)))
    )
    tail = 0.5 * poly * e
    phi = jnp.where(h >= 0, 1.0 - tail, tail)
    return h * phi, phi + h * (0.3989422804014327 * e)


def lane_low(rows):
    return lax.broadcasted_iota(jnp.int32, (rows, 128), 1) < 64


OUTER, SHARE = 4, 48
MESH = pl.DeviceIdType.MESH


class Place:
    def __init__(self):
        r = lax.axis_index("rep")
        self.y = lax.axis_index("exp")
        self.z, self.x, self.c = r // 4, (r // 2) % 2, r % 2
        self.core = (r + 1 - 2 * self.c, self.y)
        self.across = (r + 2 - 4 * self.x, self.y)
        self.beside = (r, 1 - self.y)
        self.along = [((self.z + k) % OUTER) for k in range(1, OUTER)]

    def at_z(self, z):
        return (z * 4 + self.x * 2 + self.c, self.y)

    def meet(self, partners):
        barrier = pltpu.get_barrier_semaphore()
        for partner in partners:
            pl.semaphore_signal(barrier, inc=1, device_id=partner, device_id_type=MESH)
        pl.semaphore_wait(barrier, len(partners))


class Links:
    def __init__(self, send, recv):
        self.send, self.recv, self.used = send, recv, 0

    def reserve(self, count):
        first = self.used
        self.used += count
        return first

    def copy(self, at, src, dst, device):
        return pltpu.make_async_remote_copy(
            src_ref=src, dst_ref=dst, send_sem=self.send.at[at], recv_sem=self.recv.at[at],
            device_id=device, device_id_type=MESH,
        )

    def start(self, at, src, dst, device):
        copy = self.copy(at, src, dst, device)
        copy.start()
        return copy


def fwd_kernel(linked, *refs):
    names = ["tokens", "cot", "routes", "gains", "wqkv", "wo", "win", "wout"]
    names += ["x0", "cot_out", "x1", "x2", "x3", "qkv1", "qkv2", "o1", "o2", "p1", "p2", "u", "gp", "c"]
    if linked:
        names += ["c_rx", "cot_rx", "routes_rx"]
    names += ["wide"]
    if linked:
        names += ["c_scr", "send", "recv"]
    r = dict(zip(names, refs, strict=True))
    gains = r["gains"]
    ib = r["x1"].shape[0]
    m = ib * ROWS
    images = r["x0"].shape[0]
    step = pl.program_id(0)
    lo = lane_low(ROWS)
    valid = lax.broadcasted_iota(jnp.int32, (ROWS, ROWS), 1) < PATCHES
    real = lax.broadcasted_iota(jnp.int32, (ROWS, D), 0) < PATCHES
    if linked:
        place = Place()
        links = Links(r["send"], r["recv"])

        def exchange(at, src, dst):
            return links.copy(at, src, dst, place.beside)

        early = [exchange(0, r["cot_out"], r["cot_rx"]), exchange(1, r["routes"], r["routes_rx"])]

        def c_copy(image):
            return exchange(2 + image, r["c_scr"].at[image], r["c_rx"].at[image])

    @pl.when(step == 0)
    def _():
        wide = r["wide"]
        for source, target in (("tokens", "x0"), ("cot", "cot_out")):
            wide[0 : images * PATCHES] = r[source][...].astype(F32)
            for i in range(images):
                rows = wide[i * PATCHES : i * PATCHES + ROWS]
                r[target][i] = jnp.where(real, rows, 0.0).astype(BF)
        if linked:
            place.meet([place.beside])
            for copy in early:
                copy.start()

    def attend_image(i, qkv_ref, o_ref, p_ref):
        for pair in range(HEADS // 2):
            at = 128 * pair
            q = qkv_ref[i, :, at : at + 128] * BF(0.125)
            k = qkv_ref[i, :, D + at : D + at + 128]
            w = qkv_ref[i, :, 2 * D + at : 2 * D + at + 128]
            mixed = []
            for h in range(2):
                qm = jnp.where(lo if h == 0 else ~lo, q, BF(0))
                s = jnp.where(valid, dot_t(qm, k), -1e30)
                s = jnp.exp(s - jnp.max(s, axis=-1, keepdims=True))
                p = (s * (1.0 / jnp.sum(s, axis=-1, keepdims=True))).astype(BF)
                p_ref[i, 2 * pair + h] = p
                mixed.append(dot(p, w))
            o_ref[i, :, at : at + 128] = jnp.where(lo, mixed[0], mixed[1]).astype(BF)

    def project(x, layer, gain, qkv_ref):
        a = (norm_parts(x)[0] * gain).astype(BF)
        qkv_ref[...] = dot(a, r["wqkv"][layer]).astype(BF).reshape(ib, ROWS, 3 * D)

    x0 = r["x0"][pl.ds(step * ib, ib)].astype(F32).reshape(m, D)
    project(x0, 0, gains[0:1], r["qkv1"])
    for i in range(ib):
        attend_image(i, r["qkv1"], r["o1"], r["p1"])
    x1 = x0 + dot(r["o1"][...].reshape(m, D), r["wo"][0])
    r["x1"][...] = x1.reshape(ib, ROWS, D)
    b = (norm_parts(x1)[0] * gains[1:2]).astype(BF)
    x2 = x1
    for f in range(0, FF, 512):
        u, gp = gelu_parts(dot(b, r["win"][:, f : f + 512]))
        u = u.astype(BF)
        r["u"][:, :, f : f + 512] = u.reshape(ib, ROWS, 512)
        r["gp"][:, :, f : f + 512] = gp.astype(BF).reshape(ib, ROWS, 512)
        x2 = x2 + dot(u, r["wout"][f : f + 512])
    r["x2"][...] = x2.reshape(ib, ROWS, D)
    project(x2, 1, gains[2:3], r["qkv2"])

    def last(i, _):
        attend_image(i, r["qkv2"], r["o2"], r["p2"])
        x3 = r["x2"][i] + dot(r["o2"][i], r["wo"][1])
        r["x3"][i] = x3
        c = (norm_parts(x3)[0] * gains[3:4]).astype(BF)
        r["c"][i] = c
        if linked:
            r["c_scr"][step * ib + i] = c
            c_copy(step * ib + i).start()
        return 0

    lax.fori_loop(0, ib, last, 0)

    if linked:

        @pl.when(step == pl.num_programs(0) - 1)
        def _():
            for copy in early + [c_copy(i) for i in range(images)]:
                copy.wait()


def dense_forward(tokens, cot, routes, gains, wqkv, wo, win, wout, linked):
    n = tokens.shape[0] // PATCHES
    ib = 2 if n % 2 == 0 else 1

    def out(*shape, dtype=BF):
        return jax.ShapeDtypeStruct((n,) + shape, dtype)

    def block(shape):
        return pl.BlockSpec((ib,) + tuple(shape[1:]), lambda i: (i,) + (0,) * (len(shape) - 1))

    whole = pl.BlockSpec((n, ROWS, D), lambda i: (0, 0, 0))
    outs = [out(ROWS, D)] * 2 + [out(ROWS, D, dtype=F32)] * 3 + [out(ROWS, 3 * D)] * 2 + [out(ROWS, D)] * 2
    outs += [out(HEADS, ROWS, ROWS)] * 2 + [out(ROWS, FF)] * 2 + [out(ROWS, D)]
    out_specs = [whole, whole] + [block(o.shape) for o in outs[2:]]
    scratch = [pltpu.VMEM(((n - 1) * PATCHES + ROWS, D), F32)]
    params = dict(vmem_limit_bytes=62 << 20)
    if linked:
        outs += [out(ROWS, D)] * 2 + [jax.ShapeDtypeStruct(routes.shape, jnp.int32)]
        out_specs += [pl.BlockSpec(memory_space=pl.ANY)] * 3
        copies = pltpu.SemaphoreType.DMA((2 + n,))
        scratch += [pltpu.VMEM((n, ROWS, D), BF), copies, copies]
        params.update(collective_id=2, has_side_effects=True)
    return pl.pallas_call(
        functools.partial(fwd_kernel, linked),
        grid=(n // ib,),
        out_shape=outs,
        in_specs=[VMEM] * 8,
        out_specs=out_specs,
        scratch_shapes=scratch,
        compiler_params=pltpu.CompilerParams(**params),
        name="dense_forward",
    )(tokens, cot, routes, gains, wqkv, wo, win, wout)


def gate_rows(router_t, c, routes):
    logits = dot_t(router_t, c)
    expert = lax.broadcasted_iota(jnp.int32, logits.shape, 0)
    first, second = expert == routes[0:1], expert == routes[1:2]
    diff = jnp.sum(jnp.where(first, logits, 0.0) - jnp.where(second, logits, 0.0), axis=0, keepdims=True)
    return 1.0 / (1.0 + jnp.exp(-diff)), 1.0 / (1.0 + jnp.exp(diff)), first, second


def experts_kernel(groups, local, exp_axis, *refs):
    c_refs, g_refs, r_refs = refs[:groups], refs[groups : 2 * groups], refs[2 * groups : 3 * groups]
    router_t, win, wout = refs[3 * groups : 3 * groups + 3]
    outs = refs[3 * groups + 3 :]
    eg_ref, y_refs, d_refs, delta_refs = outs[0], outs[1 : groups + 1], outs[groups + 1 : 2 * groups + 1], outs[2 * groups + 1 : 3 * groups + 1]
    ci, cols, place, xg, slots, acc_out, acc_in, u_scr, gp_scr, stack, back, count_v, count, plan, sem, load_sem = outs[3 * groups + 1 :]
    n_tok = c_refs[0].shape[0]
    total = groups * n_tok
    images = total // ROWS
    step = pl.program_id(0)
    first_expert = lax.axis_index(exp_axis) * local

    def window(e, i):
        begin = plan[e * (images + 1) + i]
        return begin, pl.multiple_of(begin // 16 * 16, 16)

    def windows(i):
        most = jnp.int32(1)
        for e in range(local):
            at = window(e, i)[1]
            most = jnp.maximum(most, (plan[e * (images + 1) + i + 1] - at + 127) // 128)
        return most

    @pl.when(step == 0)
    def _():
        loads = []
        for k, (sources, first) in enumerate(((c_refs, 0), (g_refs, D + 128))):
            for s in range(groups):
                target = ci.at[pl.ds(s * n_tok, n_tok), pl.ds(first, D)]
                loads.append(pltpu.make_async_copy(sources[s], target, load_sem.at[k * groups + s]))
                loads[-1].start()
        for load in loads:
            load.wait()
        routes = jnp.concatenate([r[0:2] for r in r_refs], axis=1)
        g0, g1, _, _ = gate_rows(router_t[...], ci[:, 0:D], routes)
        expert_row = lax.broadcasted_iota(jnp.int32, (8, total), 0)
        mine, inside = first_expert + expert_row, expert_row < local
        is0, is1 = (mine == routes[0:1]) & inside, (mine == routes[1:2]) & inside
        member = jnp.where(is0 | is1, 1.0, 0.0)
        lane = lax.broadcasted_iota(jnp.int32, (8, total), 1)
        of_image = lax.broadcasted_iota(jnp.int32, (total, 128), 0) // ROWS
        of_image = jnp.where(of_image == lax.broadcasted_iota(jnp.int32, (total, 128), 1), 1.0, 0.0)
        count_v[...] = dot(member.astype(BF), of_image.astype(BF)).astype(jnp.int32)
        to_scalars = pltpu.make_async_copy(count_v, count, sem)
        to_scalars.start()
        upto = member
        shift = 1
        while shift < total:
            upto = upto + jnp.where(lane >= shift, pltpu.roll(upto, shift, 1), 0.0)
            shift *= 2
        to_scalars.wait()
        begin = jnp.int32(0)
        starts = []
        for e in range(local):
            starts.append(begin.astype(F32))
            plan[local * (images + 1) + 2 * e] = begin
            first = begin
            for i in range(images):
                plan[e * (images + 1) + i] = begin
                begin = begin + count[e, i]
            plan[e * (images + 1) + images] = begin
            plan[local * (images + 1) + 2 * e + 1] = begin - first
            begin = first + (begin - first + 127) // 128 * 128 + 256
        start = jnp.zeros((8, total), F32)
        for e in range(local):
            start = jnp.where(expert_row == e, starts[e], start)
        slot = start + jnp.where(member > 0, upto, 0.0)
        slot0 = jnp.sum(jnp.where(is0, slot, 0.0), axis=0, keepdims=True) - 1.0
        slot1 = jnp.sum(jnp.where(is1, slot, 0.0), axis=0, keepdims=True) - 1.0
        slot = jnp.where(member > 0, slot - 1.0, -1.0)
        for i in range(images):
            place[i] = slot[:, i * ROWS : (i + 1) * ROWS]
        gates = jnp.where(is0, g0, jnp.where(is1, g1, 0.0))
        sign = jnp.where(is0, 1.0, jnp.where(is1, -1.0, 0.0))
        slot_rows = jnp.where(expert_row == 0, slot0, jnp.where(expert_row == 1, slot1, 0.0))
        stacked = jnp.concatenate([gates, sign, slot_rows, jnp.zeros((104, total), F32)], axis=0)
        lane128 = lax.broadcasted_iota(jnp.int32, (128, 128), 1)
        for at in range(0, total, 128):
            col = stacked[:, at : at + 128].T
            cols[at : at + 128] = col
            low = col - col.astype(BF).astype(F32)
            info = jnp.where(lane128 < 16, col, jnp.where(lane128 < 24, pltpu.roll(low, 16, 1), 0.0))
            ci[at : at + 128, D : D + 128] = info.astype(BF)

        row = lax.broadcasted_iota(jnp.int32, (128, ROWS), 0)
        head = lax.broadcasted_iota(jnp.int32, (16, 2 * D + 128), 0)

        def gather(i, _):
            rows = ci[pl.ds(pl.multiple_of(i * ROWS, 16), ROWS)]

            def part(w, _):
                picks = []
                for e in range(local):
                    at = window(e, i)[1] + 128 * w
                    picks.append(jnp.where(place[i, e : e + 1] == (at + row).astype(F32), 1.0, 0.0).astype(BF))
                found = dot(jnp.concatenate(picks, axis=0), rows).astype(BF)
                for e in range(local):
                    begin, at = window(e, i)
                    at = pl.multiple_of(at + 128 * w, 16)
                    old = xg[pl.ds(at, 16)]
                    new = found[e * 128 : e * 128 + 16]
                    xg[pl.ds(at, 16)] = jnp.where(at + head < begin, old, new)
                    xg[pl.ds(pl.multiple_of(at + 16, 16), 112)] = found[e * 128 + 16 : e * 128 + 128]
                return 0

            return lax.fori_loop(0, windows(i), part, 0)

        lax.fori_loop(0, images, gather, 0)
        for e in range(local):
            end, at = window(e, images)
            xg[pl.ds(at, 16)] = jnp.where(at + head < end, xg[pl.ds(at, 16)], jnp.zeros(head.shape, BF))
            xg[pl.ds(pl.multiple_of(at + 16, 16), 112)] = jnp.zeros((112, 2 * D + 128), BF)

    acc_out[...] = jnp.zeros_like(acc_out)
    acc_in[...] = jnp.zeros_like(acc_in)
    begin, n = plan[local * (images + 1) + 2 * step], plan[local * (images + 1) + 2 * step + 1]

    def tile(at, size):
        at = pl.multiple_of(at, 16)
        lane = lax.broadcasted_iota(jnp.int32, (size, 128), 1)
        x = xg[pl.ds(at, size), 0:D]
        info = xg[pl.ds(at, size), D : D + 128].astype(F32)
        g4r = xg[pl.ds(at, size), D + 128 :].astype(F32)
        gate = jnp.sum(jnp.where((lane == step) | (lane == step + 16), info, 0.0), axis=-1, keepdims=True)
        sign = jnp.sum(jnp.where(lane == step + 8, info, 0.0), axis=-1, keepdims=True)
        dy = (gate * g4r).astype(BF)
        for f in range(0, FF, 512):
            u, gp = gelu_parts(dot(x, win[0, :, f : f + 512]))
            u_scr[0:size, f : f + 512] = u.astype(BF)
            gp_scr[0:size, f : f + 512] = gp.astype(BF)
        u_all = u_scr[0:size]
        ey = dot(u_all, wout[0]).astype(BF).astype(F32)
        dg = sign * jnp.sum(g4r * ey, axis=-1, keepdims=True)
        acc_out[...] += t_dot(u_all, dy)
        for f in range(0, FF, 512):
            du = dot_t(dy, wout[0, f : f + 512])
            gp_scr[0:size, f : f + 512] = (du * gp_scr[0:size, f : f + 512].astype(F32)).astype(BF)
        deh = gp_scr[0:size]
        dcp = dot_t(deh, win[0])
        acc_in[...] += t_dot(deh, x)
        slots[pl.ds(at, size), 0:D] = (gate * ey).astype(BF)
        slots[pl.ds(at, size), D : 2 * D] = dcp.astype(BF)
        low = dg - dg.astype(BF).astype(F32)
        slots[pl.ds(at, size), 2 * D :] = jnp.where(lane == 0, dg, jnp.where(lane == 1, low, 0.0)).astype(BF)

    whole = (n + TILE // 2 - 1) // TILE

    def full_tile(j, _):
        tile(begin + j * TILE, TILE)
        return 0

    lax.fori_loop(0, whole, full_tile, 0)

    @pl.when(n > whole * TILE)
    def _():
        tile(begin + whole * TILE, TILE // 2)

    after = pl.multiple_of(begin + (n + 127) // 128 * 128, 16)
    slots[pl.ds(after, 256)] = jnp.zeros((256, 2 * D + 128), BF)
    eg_ref[0, 0] = acc_in[...].astype(BF).reshape(eg_ref.shape[2:])
    eg_ref[0, 1] = acc_out[...].astype(BF).reshape(eg_ref.shape[2:])

    @pl.when(step == local - 1)
    def _():
        lane = lax.broadcasted_iota(jnp.int32, (ROWS, 128), 1)

        def restore(s, i):
            image = s * (n_tok // ROWS) + i
            at_rows = pl.multiple_of(image * ROWS, 16)
            slot0, slot1 = cols[pl.ds(at_rows, ROWS), 16:17], cols[pl.ds(at_rows, ROWS), 17:18]
            back[...] = jnp.zeros_like(back)

            def part(w, _):
                picks = []
                for e in range(local):
                    at = pl.multiple_of(window(e, image)[1] + 128 * w, 16)
                    stack[e * 128 : (e + 1) * 128] = slots[pl.ds(at, 128)]
                    slot = (at + lane).astype(F32)
                    picks.append(jnp.where((slot0 == slot) | (slot1 == slot), 1.0, 0.0).astype(BF))
                back[...] += dot(jnp.concatenate(picks, axis=1), stack[...])
                return 0

            lax.fori_loop(0, windows(image), part, 0)
            at = pl.multiple_of(i * ROWS, 16)
            y_refs[s][pl.ds(at, ROWS)] = back[:, 0:D].astype(BF)
            d_refs[s][pl.ds(at, ROWS)] = back[:, D : 2 * D].astype(BF)
            cols[pl.ds(at_rows, ROWS)] = back[:, 2 * D :]

        for s in range(groups):

            def one(i, _, s=s):
                restore(s, i)
                return 0

            lax.fori_loop(0, n_tok // ROWS, one, 0)
        for at in range(0, total, 128):
            place_t = cols[at : at + 128].T[0:8]
            s, left = divmod(at, n_tok)
            here = min(128, n_tok - left)
            delta_refs[s][:, left : left + here] = place_t[:, 0:here]
            if here < 128:
                delta_refs[s + 1][:, 0 : 128 - here] = place_t[:, here:]


def experts_all(cs, gs, rs, router_t, win, wout, slots_most, owners):
    groups = len(cs)
    local = win.shape[0]
    n_tok = cs[0].shape[0]
    total = groups * n_tok
    images = total // ROWS
    room = -(-(slots_most + local * 384 + TILE) // 128) * 128
    width = 2 * D + 128

    def full(shape):
        return pl.BlockSpec(tuple(shape), lambda i: (0,) * len(shape))

    outs = [jax.ShapeDtypeStruct((local, 2) + owners + (FF // math.prod(owners), D), BF)]
    outs += [jax.ShapeDtypeStruct((n_tok, D), BF)] * (2 * groups)
    outs += [jax.ShapeDtypeStruct((8, n_tok), F32)] * groups
    vm = pltpu.VMEM
    result = pl.pallas_call(
        functools.partial(experts_kernel, groups, local, "exp"),
        grid=(local,),
        out_shape=outs,
        in_specs=[pl.BlockSpec(memory_space=pl.ANY)] * (2 * groups)
        + [VMEM] * (groups + 1)
        + [pl.BlockSpec((1, D, FF), lambda i: (i, 0, 0)), pl.BlockSpec((1, FF, D), lambda i: (i, 0, 0))],
        out_specs=[pl.BlockSpec((1,) + outs[0].shape[1:], lambda i: (i,) + (0,) * (len(outs[0].shape) - 1))]
        + [full(o.shape) for o in outs[1:]],
        scratch_shapes=[
            vm((total, width), BF),
            vm((total, 128), F32),
            vm((images, 8, ROWS), F32),
            vm((room, width), BF),
            vm((room, width), BF),
            vm((FF, D), F32),
            vm((FF, D), F32),
            vm((TILE, FF), BF),
            vm((TILE, FF), BF),
            vm((local * 128, width), BF),
            vm((ROWS, width), F32),
            vm((8, 128), jnp.int32),
            pltpu.SMEM((8, 128), jnp.int32),
            pltpu.SMEM((local * (images + 3),), jnp.int32),
            pltpu.SemaphoreType.DMA(()),
            pltpu.SemaphoreType.DMA((2 * groups,)),
        ],
        compiler_params=pltpu.CompilerParams(vmem_limit_bytes=62 << 20),
        name="experts",
    )(*cs, *gs, *rs, router_t, win, wout)
    return result[0], result[1 : groups + 1], result[groups + 1 : 2 * groups + 1], result[2 * groups + 1 :]


def add_into(count, target, *others):
    def block(i, _):
        total = target(i)[...].astype(F32)
        for other in others:
            total = total + other(i)[...].astype(F32)
        target(i)[...] = total.astype(target(i).dtype)
        return 0

    lax.fori_loop(0, count, block, 0)


class ExpertSums:
    COPIES = 2 + OUTER - 1

    def __init__(self, place, links, eg, own, part, x_rx, z_rx, out, local_sem):
        self.p, self.links, self.out, self.sem = place, links, out, local_sem
        self.eg, self.own, self.part, self.x_rx, self.z_rx = eg, own, part, x_rx, z_rx
        self.count = eg.shape[0]
        self.first = links.reserve(self.count * self.COPIES)

    def load(self, j):
        return pltpu.make_async_copy(self.eg.at[j, :, :, :, self.p.c], self.own.at[j % 2], self.sem.at[j % 2])

    def core_copy(self, j):
        return self.links.copy(
            self.first + j * self.COPIES, self.eg.at[j, :, :, :, 1 - self.p.c], self.part.at[j], self.p.core
        )

    def across_copy(self, j):
        return self.links.copy(
            self.first + j * self.COPIES + 1, self.part.at[j, :, :, 1 - self.p.x], self.x_rx.at[j], self.p.across
        )

    def along_copy(self, j, k):
        z = self.p.along[k]
        return self.links.copy(
            self.first + j * self.COPIES + 2 + k, self.part.at[j, :, z, self.p.x], self.z_rx.at[j, k], self.p.at_z(z)
        )

    def core(self, j):
        if j < 2:
            self.load(j).start()
        self.core_copy(j).start()

    def across(self, j):
        p = self.p

        def add(x):
            add_into(
                2 * OUTER,
                lambda i: self.part.at[j, i // OUTER, i % OUTER, x],
                lambda i: self.own.at[j % 2, i // OUTER, i % OUTER, x],
            )

        self.load(j).wait()
        self.core_copy(j).wait()
        add(1 - p.x)
        self.across_copy(j).start()
        add(p.x)
        if j + 2 < self.count:
            self.load(j + 2).start()

    def along(self, j):
        p = self.p
        self.across_copy(j).wait()
        add_into(
            2 * OUTER,
            lambda i: self.part.at[j, i // OUTER, i % OUTER, p.x],
            lambda i: self.x_rx.at[j, i // OUTER, i % OUTER],
        )
        for k in range(OUTER - 1):
            self.along_copy(j, k).start()

    def finish(self, j):
        p = self.p
        for k in range(OUTER - 1):
            self.along_copy(j, k).wait()
        for half in range(2):
            total = self.part[j, half, p.z, p.x].astype(F32)
            for k in range(OUTER - 1):
                total = total + self.z_rx[j, k, half].astype(F32)
            self.out[j, half] = total


class SharedSum:
    COPIES = 2 * (3 + OUTER - 1)

    def __init__(self, place, links, g, src, rx1, rx2, rx3, rx4, out):
        self.p, self.links, self.out = place, links, out.at[g]
        self.src, self.rx1, self.rx2, self.rx3, self.rx4 = src.at[g], rx1.at[g], rx2.at[g], rx3.at[g], rx4.at[g]
        self.at = links.reserve(self.COPIES)

    def start(self, *args):
        copy = self.links.start(self.at, *args)
        self.at += 1
        return copy

    def core(self):
        p = self.p
        self.c = self.start(self.src.at[1 - p.c], self.rx1, p.core)

    def beside(self):
        p = self.p
        self.c.wait()
        for y in (1 - p.y, p.y):
            add_into(
                2,
                lambda i: self.src.at[p.c, y, i],
                lambda i: self.rx1.at[y, i],
            )
            if y is not p.y:
                self.c = self.start(self.src.at[p.c, y], self.rx2, p.beside)

    def across(self):
        p = self.p
        self.c.wait()
        for x in (1 - p.x, p.x):
            add_into(1, lambda i: self.src.at[p.c, p.y, x], lambda i: self.rx2.at[x])
            if x is not p.x:
                self.c = self.start(self.src.at[p.c, p.y, x], self.rx3, p.across)

    def along(self):
        p = self.p
        self.c.wait()
        add_into(1, lambda i: self.src.at[p.c, p.y, p.x], lambda i: self.rx3)
        self.cs = [
            self.start(self.src.at[p.c, p.y, p.x, z], self.rx4.at[k], p.at_z(z)) for k, z in enumerate(p.along)
        ]

    def out_along(self):
        p = self.p
        for c in self.cs:
            c.wait()
        total = self.src[p.c, p.y, p.x, p.z].astype(F32)
        for k in range(OUTER - 1):
            total = total + self.rx4[k].astype(F32)
        mine = self.out.at[p.c, p.y, p.x, p.z]
        mine[...] = total.astype(BF)
        self.cs = [self.start(mine, mine, p.at_z(z)) for z in p.along]

    def out_across(self):
        p = self.p
        for c in self.cs:
            c.wait()
        mine = self.out.at[p.c, p.y, p.x]
        self.c = self.start(mine, mine, p.across)

    def out_beside(self):
        p = self.p
        self.c.wait()
        mine = self.out.at[p.c, p.y]
        self.c = self.start(mine, mine, p.beside)

    def out_core(self):
        p = self.p
        self.c.wait()
        mine = self.out.at[p.c]
        self.c = self.start(mine, mine, p.core)

    def finish(self):
        self.c.wait()


class SmallSum:
    COPIES = 3 + OUTER - 1

    def __init__(self, place, links, src, rx):
        self.p, self.links, self.src, self.rx = place, links, src, rx
        self.first = links.reserve(self.COPIES)

    def step(self, k):
        if k == 3:
            return self.along()
        device = (self.p.core, self.p.beside, self.p.across)[k]
        if k:
            self.c.wait()
            self.src[k] = self.src[k - 1] + self.rx[k - 1]
        self.c = self.links.start(self.first + k, self.src.at[k], self.rx.at[k], device)

    def along(self):
        self.c.wait()
        self.src[3] = self.src[2] + self.rx[2]
        self.cs = [
            self.links.start(self.first + 3 + k, self.src.at[3], self.rx.at[3 + k], self.p.at_z(z))
            for k, z in enumerate(self.p.along)
        ]

    def finish(self, out):
        for c in self.cs:
            c.wait()
        total = self.src[3]
        for k in range(OUTER - 1):
            total = total + self.rx[3 + k]
        out[...] = total


ORDER = (
    ("E", 1, "core"), ("d", 0, ""), ("run", 0, ""), ("d", 1, ""), ("E", 1, "across"), ("E", 0, "core"), ("d", 2, ""),
    ("E", 3, "core"), ("run", 1, ""), ("d", 3, ""), ("run", 2, ""), ("run", 3, ""), ("E", 0, "across"),
    ("run", 4, ""), ("E", 1, "along"), ("run", 5, ""), ("S", 0, "core"), ("run", 6, ""), ("run", 7, ""),
    ("run", 8, ""), ("run", 9, ""), ("S", 0, "beside"), ("run", 10, ""), ("E", 3, "across"), ("run", 11, ""),
    ("S", 1, "core"), ("E", 0, "along"), ("run", 12, ""), ("S", 1, "beside"), ("run", 13, ""), ("S", 2, "core"),
    ("S", 0, "across"), ("E", 2, "core"), ("run", 14, ""), ("run", 15, ""), ("S", 2, "beside"), ("run", 16, ""),
    ("S", 0, "along"), ("S", 1, "across"), ("run", 17, ""), ("run", 18, ""), ("S", 3, "core"), ("E", 0, "finish"),
    ("S", 0, "out_along"), ("S", 1, "along"), ("S", 3, "beside"), ("S", 2, "across"), ("E", 1, "finish"),
    ("run", 19, ""), ("few", 0, ""), ("S", 2, "along"), ("S", 0, "out_across"), ("E", 3, "along"), ("few", 1, ""),
    ("y", 0, ""), ("S", 1, "out_along"), ("S", 3, "across"), ("S", 0, "out_beside"), ("few", 2, ""),
    ("E", 2, "across"), ("S", 2, "out_along"), ("S", 3, "along"), ("few", 3, ""), ("S", 1, "out_across"),
    ("S", 2, "out_across"), ("S", 3, "out_along"), ("few", 4, ""), ("S", 1, "out_beside"), ("S", 2, "out_beside"),
    ("S", 3, "out_across"), ("E", 2, "along"), ("S", 1, "out_core"), ("S", 3, "out_beside"), ("S", 0, "out_core"),
    ("E", 3, "finish"), ("S", 2, "out_core"), ("S", 3, "out_core"), ("E", 2, "finish"), ("S", 0, "finish"),
    ("S", 2, "finish"), ("S", 1, "finish"), ("run", 20, ""), ("S", 3, "finish"),
)

LOADED = ("c", "x3", "cot", "d", "delta", "x2", "qkv", "o", "p", "wo", "wqkv", "x1", "wout", "gp", "u", "win", "y", "x0")


def bwd_kernel(linked, *refs):
    names = ["gains", "router_t", "routes", "wqkv", "wo", "win", "wout", "x0", "x1", "x2", "x3", "qkv1", "qkv2"]
    names += ["o1", "o2", "p1", "p2", "u", "gp", "c", "cot", "d", "delta", "y"]
    if linked:
        names += ["d_send", "delta_send", "y_send", "eg"]
    names += ["act_out", "gin_out", "shared_out", "small_out"]
    if linked:
        names += ["eg_out"]
    names += ["v_" + n for n in LOADED] + ["gv", "a_scr", "dbr_scr", "dqkv_scr", "sem"]
    if linked:
        names += ["d_rx", "delta_rx", "y_rx", "own", "part", "x_rx", "z_rx", "src", "rx1", "rx2", "rx3", "rx4"]
        names += ["small_src", "small_rx", "eg_sem", "send", "recv"]
    r = dict(zip(names, refs, strict=True))
    gains, gv, a_scr, dbr_scr, dqkv_scr = (r[n] for n in ("gains", "gv", "a_scr", "dbr_scr", "dqkv_scr"))
    images = gv.shape[0]
    m = images * ROWS
    lo = lane_low(ROWS)

    second = {"qkv": "qkv2", "o": "o2", "p": "p2"}
    copies = {}

    def fetch(name, source):
        copies[name] = pltpu.make_async_copy(r[source], r["v_" + name], r["sem"].at[LOADED.index(name)])
        copies[name].start()

    def need(*wanted):
        for name in wanted:
            copies[name].wait()

    if linked:
        place = Place()
        links = Links(r["send"], r["recv"])
        place.meet([place.core, place.across, place.beside] + [place.at_z(z) for z in place.along])
        delta_copy = links.start(links.reserve(1), r["delta_send"], r["delta_rx"], place.beside)
        d_first = links.reserve(images)

        def d_copy(i):
            return links.copy(d_first + i, r["d_send"].at[i], r["d_rx"].at[i], place.beside)

        experts = ExpertSums(
            place, links, r["eg"], r["own"], r["part"], r["x_rx"], r["z_rx"], r["eg_out"], r["eg_sem"]
        )
        y_copy = links.copy(links.reserve(1), r["y_send"], r["y_rx"], place.beside)
        sums = [
            SharedSum(place, links, g, r["src"], r["rx1"], r["rx2"], r["rx3"], r["rx4"], r["shared_out"])
            for g in range(4)
        ]
        few = SmallSum(place, links, r["small_src"], r["small_rx"])
        shared, small = r["src"], r["small_src"].at[0]
        small[...] = jnp.zeros(small.shape, F32)
    else:
        shared, small = r["shared_out"], r["small_out"]
    for name in LOADED:
        fetch(name, second.get(name, name))

    def keep(block, value):
        if linked:
            shared[block // 4, (block % 4) // 2, block % 2] = value.astype(BF).reshape(2, OUTER, SHARE, D)
        else:
            shared[block] = value.astype(BF)

    def router():
        need("c", "delta")
        c_all = r["v_c"][...].reshape(m, D)
        g0, g1, first, other = gate_rows(r["router_t"][...], c_all, r["routes"][...])
        delta = r["v_delta"][0:1] + r["v_delta"][1:2]
        if linked:
            delta_copy.wait()
            delta = delta + (r["delta_rx"][0:1] + r["delta_rx"][1:2])
        dl = g0 * g1 * delta
        dlog = jnp.where(first, dl, jnp.where(other, -dl, 0.0)).astype(BF)
        small[4 : 4 + dlog.shape[0]] = dot(dlog, c_all)
        small[0:4] = jnp.zeros((4, D), F32)
        gv[...] = t_dot(dlog, r["router_t"][...]).reshape(images, ROWS, D)
        need("x3", "cot", "d")

    def add_gain(row, by_gain):
        small[row : row + 1] += jnp.sum(by_gain, axis=0, keepdims=True)

    def first(i):
        dc = gv[i] + r["v_d"][i].astype(F32)
        if linked:
            d_copy(i).wait()
            dc = dc + r["d_rx"][i].astype(F32)
        dx, by_gain = norm_back(dc, r["v_x3"][i], gains[3:4])
        gv[i] = r["v_cot"][i].astype(F32) + dx
        add_gain(3, by_gain)
        if i == 0:
            need("x2", "qkv", "o", "p", "wo")
        attend_image(i, 1, gains[2:3], r["v_x2"])

    def attend_image(i, layer, gain, x):
        qkv, o, p = r["v_qkv"], r["v_o"], r["v_p"]
        a_scr[i] = (norm_parts(x[i].astype(F32))[0] * gain).astype(BF)
        dbr = gv[i].astype(BF)
        dbr_scr[i] = dbr
        do = dot_t(dbr, r["v_wo"][layer]).astype(BF)
        dod = do.astype(F32) * o[i].astype(F32)
        for pair in range(HEADS // 2):
            at = 128 * pair
            q = qkv[i, :, at : at + 128] * BF(0.125)
            k = qkv[i, :, D + at : D + at + 128]
            w = qkv[i, :, 2 * D + at : 2 * D + at + 128]
            dqs, dk, dw = [], 0.0, 0.0
            for h in range(2):
                mask = lo if h == 0 else ~lo
                dom = jnp.where(mask, do[:, at : at + 128], BF(0))
                inner = jnp.sum(jnp.where(mask, dod[:, at : at + 128], 0.0), axis=-1, keepdims=True)
                ph = p[i, 2 * pair + h]
                ds = (ph.astype(F32) * (dot_t(dom, w) - inner)).astype(BF)
                dw = dw + t_dot(ph, dom)
                dqs.append(dot(ds, k))
                dk = dk + t_dot(ds, jnp.where(mask, q, BF(0)))
            dqkv_scr[i, :, at : at + 128] = (jnp.where(lo, dqs[0], dqs[1]) * 0.125).astype(BF)
            dqkv_scr[i, :, D + at : D + at + 128] = dk.astype(BF)
            dqkv_scr[i, :, 2 * D + at : 2 * D + at + 128] = dw.astype(BF)

    def attend_weights(block):
        a_all = a_scr[...].reshape(m, D)
        for f in range(3):
            keep(block + f, t_dot(a_all, dqkv_scr[:, :, f * D : f * D + D].reshape(m, D)))
        keep(block + 3, t_dot(r["v_o"][...].reshape(m, D), dbr_scr[...].reshape(m, D)))

    def close(x, layer, row, out):
        def image(i, _):
            da = dot_t(dqkv_scr[i], r["v_wqkv"][layer])
            dx, by_gain = norm_back(da, x[i].astype(F32), gains[row : row + 1])
            out[i] = gv[i] + dx
            add_gain(row, by_gain)
            return 0

        lax.fori_loop(0, images, image, 0)

    def first_close():
        for name in ("qkv", "o", "p"):
            fetch(name, name + "1")
        need("wqkv")
        close(r["v_x2"], 1, 2, gv)
        need("x1", "wout", "gp", "u", "win")

    gp = r["v_gp"]

    def mlp(i):
        a_scr[i] = (norm_parts(r["v_x1"][i])[0] * gains[1:2]).astype(BF)
        dm = gv[i].astype(BF)
        dbr_scr[i] = dm
        for f in range(0, FF, 512):
            du = dot_t(dm, r["v_wout"][f : f + 512])
            gp[i, :, f : f + 512] = (du * gp[i, :, f : f + 512].astype(F32)).astype(BF)

    def mlp_out_weights():
        dm_all = dbr_scr[...].reshape(m, D)
        for f in range(4):
            keep(4 + f, t_dot(r["v_u"][:, :, f * D : f * D + D].reshape(m, D), dm_all))

    def mlp_in_weights():
        b_all = a_scr[...].reshape(m, D)
        for f in range(4):
            keep(8 + f, t_dot(b_all, gp[:, :, f * D : f * D + D].reshape(m, D)))

    def mlp_close():
        def image(i, _):
            db = dot_t(gp[i], r["v_win"][...])
            dx, by_gain = norm_back(db, r["v_x1"][i], gains[1:2])
            gv[i] = gv[i] + dx
            add_gain(1, by_gain)
            return 0

        lax.fori_loop(0, images, image, 0)
        need("x0", "qkv", "o", "p")

    def last(i):
        attend_image(i, 0, gains[0:1], r["v_x0"])

    def last_close():
        close(r["v_x0"], 0, 0, r["gin_out"])

    def act():
        need("y")
        if linked:
            y_copy.wait()
        for i in range(images):
            x4 = r["v_x3"][i] + r["v_y"][i].astype(F32)
            if linked:
                x4 = x4 + r["y_rx"][i].astype(F32)
            r["act_out"][i] = x4.astype(BF)

    compute = [router] + [functools.partial(first, i) for i in range(images)]
    compute += [lambda: attend_weights(0), first_close] + [functools.partial(mlp, i) for i in range(images)]
    compute += [mlp_out_weights, mlp_in_weights, mlp_close] + [functools.partial(last, i) for i in range(images)]
    compute += [lambda: attend_weights(12), last_close, act]
    if not linked:
        for step in compute:
            step()
        return
    done = 0
    for kind, at, what in ORDER:
        if kind == "run":
            compute[done]()
            done += 1
        elif kind == "d":
            d_copy(at).start()
        elif kind == "y":
            y_copy.start()
        elif kind == "few" and at < 4:
            few.step(at)
        elif kind == "few":
            few.finish(r["small_out"])
        elif kind == "E":
            getattr(experts, what)(at)
        else:
            getattr(sums[at], what)()


def dense_backward(weights, router_t, routes, saved, cot, d, delta, y, sent=None):
    gains, wqkv, wo, win, wout = weights
    x0, x1, x2, x3, qkv1, qkv2, o1, o2, p1, p2, u, gp, c = saved
    images = x0.shape[0]
    linked = sent is not None
    small_rows = 16 if linked else 4 + router_t.shape[0]
    ins = [gains, router_t, routes, wqkv, wo, win, wout, *saved, cot, d, delta, y] + (list(sent) if linked else [])
    outs = [
        jax.ShapeDtypeStruct((images, ROWS, D), BF),
        jax.ShapeDtypeStruct((images, ROWS, D), F32),
        jax.ShapeDtypeStruct((4, 2, 2, 2, OUTER, SHARE, D) if linked else (16, D, D), BF),
        jax.ShapeDtypeStruct((small_rows, D), F32),
    ]
    vm = pltpu.VMEM
    loaded = dict(
        c=c, x3=x3, cot=cot, d=d, delta=delta, x2=x2, qkv=qkv1, o=o1, p=p1, wo=wo, wqkv=wqkv, x1=x1, wout=wout,
        gp=gp, u=u, win=win, y=y, x0=x0,
    )
    scratch = [vm(loaded[name].shape, loaded[name].dtype) for name in LOADED]
    scratch += [vm((images, ROWS, D), F32), vm((images, ROWS, D), BF), vm((images, ROWS, D), BF)]
    scratch += [vm((images, ROWS, 3 * D), BF), pltpu.SemaphoreType.DMA((len(LOADED),))]
    params = dict(vmem_limit_bytes=62 << 20)
    if linked:
        eg = sent[-1]
        local, share = eg.shape[0], eg.shape[-2]
        outs.append(jax.ShapeDtypeStruct((local, 2, share, D), F32))
        copies = 2 + images + local * ExpertSums.COPIES + 4 * SharedSum.COPIES + SmallSum.COPIES
        scratch += [vm(d.shape, BF), vm(delta.shape, F32), vm(y.shape, BF)]
        scratch += [
            vm((2, 2, OUTER, 2, share, D), BF),
            vm((local, 2, OUTER, 2, share, D), BF),
            vm((local, 2, OUTER, share, D), BF),
            vm((local, OUTER - 1, 2, share, D), BF),
            vm((4, 2, 2, 2, OUTER, SHARE, D), BF),
            vm((4, 2, 2, OUTER, SHARE, D), BF),
            vm((4, 2, OUTER, SHARE, D), BF),
            vm((4, OUTER, SHARE, D), BF),
            vm((4, OUTER - 1, SHARE, D), BF),
            vm((4, small_rows, D), F32),
            vm((OUTER + 2, small_rows, D), F32),
            pltpu.SemaphoreType.DMA((2,)),
            pltpu.SemaphoreType.DMA((copies,)),
            pltpu.SemaphoreType.DMA((copies,)),
        ]
        params.update(collective_id=1, has_side_effects=True)
    return pl.pallas_call(
        functools.partial(bwd_kernel, linked),
        out_shape=outs,
        in_specs=[VMEM] * 3 + [pl.BlockSpec(memory_space=pl.ANY)] * (len(ins) - 3),
        out_specs=[VMEM] * len(outs),
        scratch_shapes=scratch,
        compiler_params=pltpu.CompilerParams(**params),
        name="dense_backward",
    )(*ins)


def finish_kernel(
    act, gin, shared, small, eg, act_out, gin_out, qkv_out, proj_out, gain_out, mlp_in_out, mlp_out_out, router_out,
    in_out, out_out, v_shared, v_wide, v_gin, v_act, in_sem, out_sem,
):
    images = act.shape[0]
    blocks = v_shared.shape[0]
    targets = {3: proj_out.at[1], 15: proj_out.at[0]}
    for f in range(3):
        targets[f] = qkv_out.at[1, :, pl.ds(f * D, D)]
        targets[12 + f] = qkv_out.at[0, :, pl.ds(f * D, D)]
    for f in range(4):
        targets[4 + f] = mlp_out_out.at[pl.ds(f * D, D)]
        targets[8 + f] = mlp_in_out.at[:, pl.ds(f * D, D)]

    def load(b):
        return pltpu.make_async_copy(shared.at[b], v_shared.at[b], in_sem.at[b])

    def store(b):
        return pltpu.make_async_copy(v_wide.at[b], targets[b], out_sem.at[b])

    load_gin = pltpu.make_async_copy(gin, v_gin, in_sem.at[blocks])
    load_act = pltpu.make_async_copy(act, v_act, in_sem.at[blocks + 1])
    for b in range(blocks):
        load(b).start()
    load_gin.start()
    load_act.start()
    gain_out[...] = small[0:4]
    router_out[...] = small[4 : 4 + router_out.shape[0]]
    for e in range(eg.shape[0]):
        in_out[e] = eg[e, 0]
        out_out[e] = eg[e, 1]
    for b in range(blocks):
        load(b).wait()
        v_wide[b] = v_shared[b].astype(F32)
        store(b).start()
    load_gin.wait()
    load_act.wait()
    for i in range(images):
        gin_out[i * PATCHES : (i + 1) * PATCHES] = v_act[i, 0:PATCHES].astype(F32)
    act_out[...] = gin_out[...].astype(BF)
    for i in range(images):
        gin_out[i * PATCHES : (i + 1) * PATCHES] = v_gin[i, 0:PATCHES]
    for b in range(blocks):
        store(b).wait()


def finish(act, gin, shared, small, eg, experts):
    images, local, share = act.shape[0], eg.shape[0], eg.shape[2]
    row_count = images * PATCHES
    outs = [
        jax.ShapeDtypeStruct((row_count, D), BF),
        jax.ShapeDtypeStruct((row_count, D), F32),
        jax.ShapeDtypeStruct((2, D, 3 * D), F32),
        jax.ShapeDtypeStruct((2, D, D), F32),
        jax.ShapeDtypeStruct((4, D), F32),
        jax.ShapeDtypeStruct((D, FF), F32),
        jax.ShapeDtypeStruct((FF, D), F32),
        jax.ShapeDtypeStruct((experts, D), F32),
        jax.ShapeDtypeStruct((local, share, D), F32),
        jax.ShapeDtypeStruct((local, share, D), F32),
    ]
    far = pl.BlockSpec(memory_space=pl.ANY)
    return pl.pallas_call(
        finish_kernel,
        out_shape=outs,
        in_specs=[far, far, far, VMEM, VMEM],
        out_specs=[VMEM, VMEM, far, far, VMEM, far, far, VMEM, VMEM, VMEM],
        scratch_shapes=[
            pltpu.VMEM(shared.shape, BF),
            pltpu.VMEM(shared.shape, F32),
            pltpu.VMEM(gin.shape, F32),
            pltpu.VMEM(act.shape, BF),
            pltpu.SemaphoreType.DMA((shared.shape[0] + 2,)),
            pltpu.SemaphoreType.DMA((shared.shape[0],)),
        ],
        compiler_params=pltpu.CompilerParams(vmem_limit_bytes=62 << 20),
        name="finish",
    )(act, gin, shared, small, eg)


def from_peer(array, groups, shift):
    return lax.ppermute(array, "exp", [(i, (i + shift) % groups) for i in range(groups)])


def shards(
    tokens, routes, norm_gains, attn_qkv, attn_out, mlp_in, mlp_out, router, experts_in, experts_out, cotangent
):
    row_count = tokens.shape[0]
    groups = lax.axis_size("exp")
    local = experts_in.shape[0]
    choices = routes.shape[1]
    capacity = 2 * choices * row_count // (local * groups)
    images = row_count // PATCHES
    n_tok = images * ROWS
    routes_t = routes.T.reshape(choices, images, PATCHES)
    routes_t = jnp.pad(routes_t, ((0, 8 - choices), (0, 0), (0, ROWS - PATCHES)), constant_values=-1)
    routes_t = routes_t.reshape(8, n_tok)
    router_t = router.T
    rep = lax.axis_size("rep")
    known = (rep, groups, local) == (16, 2, 4)
    owners = (OUTER, 2, 2) if known else (rep,)
    x0, cot, x1, x2, x3, qkv1, qkv2, o1, o2, p1, p2, u, gp, c, *received = dense_forward(
        tokens, cotangent, routes_t, norm_gains, attn_qkv, attn_out, mlp_in, mlp_out, known
    )

    def of_all(mine, place):
        if known:
            others = [received[place]]
        else:
            others = [from_peer(mine, groups, k) for k in range(1, groups)]
        return [part.reshape(-1, part.shape[-1]) for part in [mine] + others]

    cs, gs, rs = of_all(c, 0), of_all(cot, 1), of_all(routes_t, 2)
    eg, ys, ds, deltas = experts_all(
        cs, gs, rs, router_t, experts_in, experts_out, local * capacity * groups, owners
    )

    weights = (norm_gains, attn_qkv, attn_out, mlp_in, mlp_out)
    saved = (x0, x1, x2, x3, qkv1, qkv2, o1, o2, p1, p2, u, gp, c)
    by_image = (images, ROWS, D)
    experts = router_t.shape[0]
    if known:
        sent = (ds[1].reshape(by_image), deltas[1], ys[1].reshape(by_image), eg)
        act, gin, shared, small, eg = dense_backward(
            weights, router_t, routes_t, saved, cot, ds[0].reshape(by_image), deltas[0], ys[0].reshape(by_image), sent
        )
        shared = shared.reshape(16, D, D)
    else:

        def back(parts):
            total = parts[0].astype(F32)
            for k in range(1, groups):
                total = total + from_peer(parts[k], groups, groups - k).astype(F32)
            return total

        d, delta, y = back(ds).astype(BF), back(deltas), back(ys).astype(BF)
        act, gin, shared, small = dense_backward(
            weights, router_t, routes_t, saved, cot, d.reshape(by_image), delta, y.reshape(by_image)
        )
        eg = lax.psum_scatter(eg, "rep", scatter_dimension=2, tiled=True).reshape(local, 2, FF // rep, D).astype(F32)
        shared, small = lax.psum((shared, small), ("rep", "exp"))
    outs = list(finish(act, gin, shared, small, eg, experts))
    outs[7] = outs[7].T
    outs[8] = jnp.swapaxes(outs[8], 1, 2)
    return tuple(outs)


def solution(mesh):
    rows = P(("rep", "exp"), None)
    return jax.shard_map(
        shards,
        mesh=mesh,
        in_specs=(rows, rows, P(), P(), P(), P(), P(), P(), P("exp", None, None), P("exp", None, None), rows),
        out_specs=(rows, rows, P(), P(), P(), P(), P(), P(), P("exp", None, "rep"), P("exp", "rep", None)),
        check_vma=False,
    )
```

```python
import functools
import math

import jax
import jax.numpy as jnp
from jax import lax
from jax.experimental import pallas as pl
from jax.experimental.pallas import tpu as pltpu
from jax.sharding import PartitionSpec as P

F32 = jnp.float32
BF = jnp.bfloat16
HEADS = 6
PATCHES = 197
ROWS = 208
EPS = 1e-6
TILE = 256
D = 384
FF = 1536
VMEM = pl.BlockSpec(memory_space=pltpu.VMEM)


def dot(a, b):
    return lax.dot_general(a, b, (((1,), (0,)), ((), ())), preferred_element_type=F32)


def dot_t(a, b):
    return lax.dot_general(a, b, (((1,), (1,)), ((), ())), preferred_element_type=F32)


def t_dot(a, b):
    return lax.dot_general(a, b, (((0,), (0,)), ((), ())), preferred_element_type=F32)


def norm_parts(x):
    centred = x - jnp.mean(x, axis=-1, keepdims=True)
    rstd = lax.rsqrt(jnp.mean(centred * centred, axis=-1, keepdims=True) + EPS)
    return centred * rstd, rstd


def norm_back(grad, x, gain):
    xh, rstd = norm_parts(x)
    dxh = grad * gain
    inner = dxh - jnp.mean(dxh, axis=-1, keepdims=True)
    return rstd * (inner - xh * jnp.mean(dxh * xh, axis=-1, keepdims=True)), grad * xh


def gelu_parts(h):
    phi = 0.5 + 0.5 * lax.erf(0.7071067811865476 * h)
    e = jnp.exp2(h * h * -0.7213475204444817)
    return h * phi, phi + h * (0.3989422804014327 * e)


def lane_low(rows):
    return lax.broadcasted_iota(jnp.int32, (rows, 128), 1) < 64


MESH = pl.DeviceIdType.MESH
BITS = "cyxhl"


class Place:
    def __init__(self):
        r = lax.axis_index("rep")
        y = lax.axis_index("exp")
        self.bit = {"c": r % 2, "y": y, "x": (r // 2) % 2, "h": r // 8, "l": (r // 4) % 2}
        stride = {"c": 1, "x": 2, "l": 4, "h": 8}
        self.partner = {b: (r + stride[b] * (1 - 2 * self.bit[b]), y) for b in stride}
        self.partner["y"] = (r, 1 - y)
        self.others = []
        for k in range(1, 4):
            z = (r // 4 + k) % 4
            self.others.append(({"h": z // 2, "l": z % 2}, (z * 4 + r % 4, y)))

    def meet(self, partners):
        barrier = pltpu.get_barrier_semaphore()
        for partner in partners:
            pl.semaphore_signal(barrier, inc=1, device_id=partner, device_id_type=MESH)
        pl.semaphore_wait(barrier, len(partners))


class Links:
    def __init__(self, send, recv):
        self.send, self.recv, self.used = send, recv, 0

    def reserve(self, count):
        first = self.used
        self.used += count
        return first

    def copy(self, at, src, dst, device):
        return pltpu.make_async_remote_copy(
            src_ref=src, dst_ref=dst, send_sem=self.send.at[at], recv_sem=self.recv.at[at],
            device_id=device, device_id_type=MESH,
        )

    def start(self, at, src, dst, device):
        copy = self.copy(at, src, dst, device)
        copy.start()
        return copy


def fwd_kernel(linked, *refs):
    names = ["tokens", "cot", "routes", "gains", "wqkv", "wo", "win", "wout"]
    names += ["x0", "cot_out", "x1", "x2", "x3", "qkv1", "qkv2", "o1", "o2", "p1", "p2", "u", "gp", "c"]
    if linked:
        names += ["c_rx", "cot_rx", "routes_rx"]
    names += ["wide"]
    if linked:
        names += ["c_scr", "send", "recv"]
    r = dict(zip(names, refs, strict=True))
    gains = r["gains"]
    ib = r["x1"].shape[0]
    m = ib * ROWS
    images = r["x0"].shape[0]
    step = pl.program_id(0)
    lo = lane_low(ROWS)
    valid = lax.broadcasted_iota(jnp.int32, (ROWS, ROWS), 1) < PATCHES
    real = lax.broadcasted_iota(jnp.int32, (ROWS, D), 0) < PATCHES
    if linked:
        place = Place()
        links = Links(r["send"], r["recv"])

        def exchange(at, src, dst):
            return links.copy(at, src, dst, place.partner["y"])

        early = [exchange(0, r["cot_out"], r["cot_rx"]), exchange(1, r["routes"], r["routes_rx"])]

        def c_copy(image):
            return exchange(2 + image, r["c_scr"].at[image], r["c_rx"].at[image])

    @pl.when(step == 0)
    def _():
        wide = r["wide"]
        for source, target in (("tokens", "x0"), ("cot", "cot_out")):
            wide[0 : images * PATCHES] = r[source][...].astype(F32)
            for i in range(images):
                rows = wide[i * PATCHES : i * PATCHES + ROWS]
                r[target][i] = jnp.where(real, rows, 0.0).astype(BF)
        if linked:
            place.meet([place.partner["y"]])
            for copy in early:
                copy.start()

    def attend_image(i, qkv_ref, o_ref, p_ref):
        for pair in range(HEADS // 2):
            at = 128 * pair
            q = qkv_ref[i, :, at : at + 128] * BF(0.125)
            k = qkv_ref[i, :, D + at : D + at + 128]
            w = qkv_ref[i, :, 2 * D + at : 2 * D + at + 128]
            mixed = []
            for h in range(2):
                qm = jnp.where(lo if h == 0 else ~lo, q, BF(0))
                s = jnp.where(valid, dot_t(qm, k), -1e30)
                s = jnp.exp(s - jnp.max(s, axis=-1, keepdims=True))
                p = (s * (1.0 / jnp.sum(s, axis=-1, keepdims=True))).astype(BF)
                p_ref[i, 2 * pair + h] = p
                mixed.append(dot(p, w))
            o_ref[i, :, at : at + 128] = jnp.where(lo, mixed[0], mixed[1]).astype(BF)

    def project(x, layer, gain, qkv_ref):
        a = (norm_parts(x)[0] * gain).astype(BF)
        qkv_ref[...] = dot(a, r["wqkv"][layer]).astype(BF).reshape(ib, ROWS, 3 * D)

    x0 = r["x0"][pl.ds(step * ib, ib)].astype(F32).reshape(m, D)
    project(x0, 0, gains[0:1], r["qkv1"])
    for i in range(ib):
        attend_image(i, r["qkv1"], r["o1"], r["p1"])
    x1 = x0 + dot(r["o1"][...].reshape(m, D), r["wo"][0])
    r["x1"][...] = x1.reshape(ib, ROWS, D)
    b = (norm_parts(x1)[0] * gains[1:2]).astype(BF)
    x2 = x1
    for f in range(0, FF, 512):
        u, gp = gelu_parts(dot(b, r["win"][:, f : f + 512]))
        u = u.astype(BF)
        r["u"][:, :, f : f + 512] = u.reshape(ib, ROWS, 512)
        r["gp"][:, :, f : f + 512] = gp.astype(BF).reshape(ib, ROWS, 512)
        x2 = x2 + dot(u, r["wout"][f : f + 512])
    r["x2"][...] = x2.reshape(ib, ROWS, D)
    project(x2, 1, gains[2:3], r["qkv2"])

    def last(i, _):
        attend_image(i, r["qkv2"], r["o2"], r["p2"])
        x3 = r["x2"][i] + dot(r["o2"][i], r["wo"][1])
        r["x3"][i] = x3
        c = (norm_parts(x3)[0] * gains[3:4]).astype(BF)
        r["c"][i] = c
        if linked:
            r["c_scr"][step * ib + i] = c
            c_copy(step * ib + i).start()
        return 0

    lax.fori_loop(0, ib, last, 0)

    if linked:

        @pl.when(step == pl.num_programs(0) - 1)
        def _():
            for copy in early + [c_copy(i) for i in range(images)]:
                copy.wait()


def dense_forward(tokens, cot, routes, gains, wqkv, wo, win, wout, linked):
    n = tokens.shape[0] // PATCHES
    ib = 2 if n % 2 == 0 else 1

    def out(*shape, dtype=BF):
        return jax.ShapeDtypeStruct((n,) + shape, dtype)

    def block(shape):
        return pl.BlockSpec((ib,) + tuple(shape[1:]), lambda i: (i,) + (0,) * (len(shape) - 1))

    whole = pl.BlockSpec((n, ROWS, D), lambda i: (0, 0, 0))
    outs = [out(ROWS, D)] * 2 + [out(ROWS, D, dtype=F32)] * 3 + [out(ROWS, 3 * D)] * 2 + [out(ROWS, D)] * 2
    outs += [out(HEADS, ROWS, ROWS)] * 2 + [out(ROWS, FF)] * 2 + [out(ROWS, D)]
    out_specs = [whole, whole] + [block(o.shape) for o in outs[2:]]
    scratch = [pltpu.VMEM(((n - 1) * PATCHES + ROWS, D), F32)]
    params = dict(vmem_limit_bytes=62 << 20)
    if linked:
        outs += [out(ROWS, D)] * 2 + [jax.ShapeDtypeStruct(routes.shape, jnp.int32)]
        out_specs += [pl.BlockSpec(memory_space=pl.ANY)] * 3
        copies = pltpu.SemaphoreType.DMA((2 + n,))
        scratch += [pltpu.VMEM((n, ROWS, D), BF), copies, copies]
        params.update(collective_id=2, has_side_effects=True)
    return pl.pallas_call(
        functools.partial(fwd_kernel, linked),
        grid=(n // ib,),
        out_shape=outs,
        in_specs=[VMEM] * 8,
        out_specs=out_specs,
        scratch_shapes=scratch,
        compiler_params=pltpu.CompilerParams(**params),
        name="dense_forward",
    )(tokens, cot, routes, gains, wqkv, wo, win, wout)


def gate_rows(router_t, c, routes):
    logits = dot_t(router_t, c)
    expert = lax.broadcasted_iota(jnp.int32, logits.shape, 0)
    first, second = expert == routes[0:1], expert == routes[1:2]
    diff = jnp.sum(jnp.where(first, logits, 0.0) - jnp.where(second, logits, 0.0), axis=0, keepdims=True)
    return 1.0 / (1.0 + jnp.exp(-diff)), 1.0 / (1.0 + jnp.exp(diff)), first, second


def experts_kernel(groups, local, exp_axis, *refs):
    c_refs, g_refs, r_refs = refs[:groups], refs[groups : 2 * groups], refs[2 * groups : 3 * groups]
    router_t, win, wout = refs[3 * groups : 3 * groups + 3]
    outs = refs[3 * groups + 3 :]
    eg_ref, y_refs, d_refs, delta_refs = outs[0], outs[1 : groups + 1], outs[groups + 1 : 2 * groups + 1], outs[2 * groups + 1 : 3 * groups + 1]
    ci, cols, place, xg, slots, dy_scr, u_scr, gp_scr, stack, back, staged, count_v, count, plan, sem, load_sem, out_sem = outs[3 * groups + 1 :]
    n_tok = c_refs[0].shape[0]
    total = groups * n_tok
    images = total // ROWS
    step = pl.program_id(0)
    first_expert = lax.axis_index(exp_axis) * local

    def window(e, i):
        begin = plan[e * (images + 1) + i]
        return begin, pl.multiple_of(begin // 16 * 16, 16)

    def windows(i):
        most = jnp.int32(1)
        for e in range(local):
            at = window(e, i)[1]
            most = jnp.maximum(most, (plan[e * (images + 1) + i + 1] - at + 127) // 128)
        return most

    @pl.when(step == 0)
    def _():
        loads = []
        for k, (sources, first) in enumerate(((c_refs, 0), (g_refs, D + 128))):
            for s in range(groups):
                target = ci.at[pl.ds(s * n_tok, n_tok), pl.ds(first, D)]
                loads.append(pltpu.make_async_copy(sources[s], target, load_sem.at[k * groups + s]))
                loads[-1].start()
        for load in loads:
            load.wait()
        routes = jnp.concatenate([r[0:2] for r in r_refs], axis=1)
        g0, g1, _, _ = gate_rows(router_t[...], ci[:, 0:D], routes)
        expert_row = lax.broadcasted_iota(jnp.int32, (8, total), 0)
        mine, inside = first_expert + expert_row, expert_row < local
        is0, is1 = (mine == routes[0:1]) & inside, (mine == routes[1:2]) & inside
        member = jnp.where(is0 | is1, 1.0, 0.0)
        lane = lax.broadcasted_iota(jnp.int32, (8, total), 1)
        of_image = lax.broadcasted_iota(jnp.int32, (total, 128), 0) // ROWS
        of_image = jnp.where(of_image == lax.broadcasted_iota(jnp.int32, (total, 128), 1), 1.0, 0.0)
        count_v[...] = dot(member.astype(BF), of_image.astype(BF)).astype(jnp.int32)
        to_scalars = pltpu.make_async_copy(count_v, count, sem)
        to_scalars.start()
        upto = member
        shift = 1
        while shift < total:
            upto = upto + jnp.where(lane >= shift, pltpu.roll(upto, shift, 1), 0.0)
            shift *= 2
        to_scalars.wait()
        begin = jnp.int32(0)
        starts = []
        for e in range(local):
            starts.append(begin.astype(F32))
            plan[local * (images + 1) + 2 * e] = begin
            first = begin
            for i in range(images):
                plan[e * (images + 1) + i] = begin
                begin = begin + count[e, i]
            plan[e * (images + 1) + images] = begin
            plan[local * (images + 1) + 2 * e + 1] = begin - first
            begin = first + (begin - first + 127) // 128 * 128 + 256
        start = jnp.zeros((8, total), F32)
        for e in range(local):
            start = jnp.where(expert_row == e, starts[e], start)
        slot = start + jnp.where(member > 0, upto, 0.0)
        slot0 = jnp.sum(jnp.where(is0, slot, 0.0), axis=0, keepdims=True) - 1.0
        slot1 = jnp.sum(jnp.where(is1, slot, 0.0), axis=0, keepdims=True) - 1.0
        slot = jnp.where(member > 0, slot - 1.0, -1.0)
        for i in range(images):
            place[i] = slot[:, i * ROWS : (i + 1) * ROWS]
        gates = jnp.where(is0, g0, jnp.where(is1, g1, 0.0))
        sign = jnp.where(is0, 1.0, jnp.where(is1, -1.0, 0.0))
        slot_rows = jnp.where(expert_row == 0, slot0, jnp.where(expert_row == 1, slot1, 0.0))
        stacked = jnp.concatenate([gates, sign, slot_rows, jnp.zeros((104, total), F32)], axis=0)
        lane128 = lax.broadcasted_iota(jnp.int32, (128, 128), 1)
        for at in range(0, total, 128):
            col = stacked[:, at : at + 128].T
            cols[at : at + 128] = col
            low = col - col.astype(BF).astype(F32)
            info = jnp.where(lane128 < 16, col, jnp.where(lane128 < 24, pltpu.roll(low, 16, 1), 0.0))
            ci[at : at + 128, D : D + 128] = info.astype(BF)

        row = lax.broadcasted_iota(jnp.int32, (128, ROWS), 0)
        head = lax.broadcasted_iota(jnp.int32, (16, 2 * D + 128), 0)

        def gather(i, _):
            rows = ci[pl.ds(pl.multiple_of(i * ROWS, 16), ROWS)]

            def part(w, _):
                picks = []
                for e in range(local):
                    at = window(e, i)[1] + 128 * w
                    picks.append(jnp.where(place[i, e : e + 1] == (at + row).astype(F32), 1.0, 0.0).astype(BF))
                found = dot(jnp.concatenate(picks, axis=0), rows).astype(BF)
                for e in range(local):
                    begin, at = window(e, i)
                    at = pl.multiple_of(at + 128 * w, 16)
                    old = xg[pl.ds(at, 16)]
                    new = found[e * 128 : e * 128 + 16]
                    xg[pl.ds(at, 16)] = jnp.where(at + head < begin, old, new)
                    xg[pl.ds(pl.multiple_of(at + 16, 16), 112)] = found[e * 128 + 16 : e * 128 + 128]
                return 0

            return lax.fori_loop(0, windows(i), part, 0)

        lax.fori_loop(0, images, gather, 0)
        for e in range(local):
            end, at = window(e, images)
            xg[pl.ds(at, 16)] = jnp.where(at + head < end, xg[pl.ds(at, 16)], jnp.zeros(head.shape, BF))
            xg[pl.ds(pl.multiple_of(at + 16, 16), 240)] = jnp.zeros((240, 2 * D + 128), BF)

    begin, n = plan[local * (images + 1) + 2 * step], plan[local * (images + 1) + 2 * step + 1]

    def tile(row, size):
        at = pl.multiple_of(begin + row, 16)
        here = pl.ds(pl.multiple_of(row, 128), size)
        lane = lax.broadcasted_iota(jnp.int32, (size, 128), 1)
        x = xg[pl.ds(at, size), 0:D]
        info = xg[pl.ds(at, size), D : D + 128].astype(F32)
        g4r = xg[pl.ds(at, size), D + 128 :].astype(F32)
        gate = jnp.sum(jnp.where((lane == step) | (lane == step + 16), info, 0.0), axis=-1, keepdims=True)
        sign = jnp.sum(jnp.where(lane == step + 8, info, 0.0), axis=-1, keepdims=True)
        dy = (gate * g4r).astype(BF)
        dy_scr[here] = dy
        for f in range(0, FF, 512):
            u, gp = gelu_parts(dot(x, win[0, :, f : f + 512]))
            u_scr[here, f : f + 512] = u.astype(BF)
            gp_scr[here, f : f + 512] = gp.astype(BF)
        ey = dot(u_scr[here], wout[0]).astype(BF).astype(F32)
        dg = sign * jnp.sum(g4r * ey, axis=-1, keepdims=True)
        for f in range(0, FF, 512):
            du = dot_t(dy, wout[0, f : f + 512])
            gp_scr[here, f : f + 512] = (du * gp_scr[here, f : f + 512].astype(F32)).astype(BF)
        dcp = dot_t(gp_scr[here], win[0])
        slots[pl.ds(at, size), 0:D] = (gate * ey).astype(BF)
        slots[pl.ds(at, size), D : 2 * D] = dcp.astype(BF)
        low = dg - dg.astype(BF).astype(F32)
        slots[pl.ds(at, size), 2 * D :] = jnp.where(lane == 0, dg, jnp.where(lane == 1, low, 0.0)).astype(BF)

    whole = (n + TILE // 2 - 1) // TILE

    def full_tile(j, _):
        tile(j * TILE, TILE)
        return 0

    lax.fori_loop(0, whole, full_tile, 0)

    @pl.when(n > whole * TILE)
    def _():
        tile(whole * TILE, TILE // 2)
        rest = pl.ds(pl.multiple_of(whole * TILE + TILE // 2, 128), TILE // 2)
        for scratch in (dy_scr, u_scr, gp_scr):
            scratch[rest] = jnp.zeros((TILE // 2,) + scratch.shape[1:], BF)

    after = pl.multiple_of(begin + (n + 127) // 128 * 128, 16)
    slots[pl.ds(after, 256)] = jnp.zeros((256, 2 * D + 128), BF)

    rounded = (n + TILE - 1) // TILE

    @pl.when(rounded == 0)
    def _():
        eg_ref[...] = jnp.zeros_like(eg_ref)

    for tiles in range(1, u_scr.shape[0] // TILE + 1):

        @pl.when(rounded == tiles)
        def _(depth=tiles * TILE):
            x = xg[pl.ds(pl.multiple_of(begin, 16), depth), 0:D]
            dy = dy_scr[0:depth]
            for f in range(0, FF, D):
                eg_ref[0, 0, f : f + D] = t_dot(gp_scr[0:depth, f : f + D], x).astype(BF)
                eg_ref[0, 1, f : f + D] = t_dot(u_scr[0:depth, f : f + D], dy).astype(BF)

    @pl.when(step == local - 1)
    def _():
        lane = lax.broadcasted_iota(jnp.int32, (ROWS, 128), 1)

        def out_copies(s, i, slot):
            rows = pl.ds(pl.multiple_of(i * ROWS, 16), ROWS)
            return [
                pltpu.make_async_copy(staged.at[slot, k], target.at[rows], out_sem.at[slot, k])
                for k, target in enumerate((y_refs[s], d_refs[s]))
            ]

        def restore(s, i):
            image = s * (n_tok // ROWS) + i
            at_rows = pl.multiple_of(image * ROWS, 16)
            slot0, slot1 = cols[pl.ds(at_rows, ROWS), 16:17], cols[pl.ds(at_rows, ROWS), 17:18]

            def part(w):
                picks = []
                for e in range(local):
                    at = pl.multiple_of(window(e, image)[1] + 128 * w, 16)
                    stack[e * 128 : (e + 1) * 128] = slots[pl.ds(at, 128)]
                    slot = (at + lane).astype(F32)
                    picks.append(jnp.where((slot0 == slot) | (slot1 == slot), 1.0, 0.0).astype(BF))
                return dot(jnp.concatenate(picks, axis=1), stack[...])

            back[...] = part(0)

            def more(w, _):
                back[...] += part(w)
                return 0

            lax.fori_loop(1, windows(image), more, 0)
            slot = lax.rem(image, 2)

            @pl.when(image >= 2)
            def _():
                for copy in out_copies(s, i, slot):
                    copy.wait()

            staged[slot, 0] = back[:, 0:D].astype(BF)
            staged[slot, 1] = back[:, D : 2 * D].astype(BF)
            for copy in out_copies(s, i, slot):
                copy.start()
            cols[pl.ds(at_rows, ROWS)] = back[:, 2 * D :]

        for s in range(groups):

            def one(i, _, s=s):
                restore(s, i)
                return 0

            lax.fori_loop(0, n_tok // ROWS, one, 0)
        for slot in range(2):
            for copy in out_copies(groups - 1, 0, slot):
                copy.wait()
        for at in range(0, total, 128):
            place_t = cols[at : at + 128].T[0:8]
            s, left = divmod(at, n_tok)
            here = min(128, n_tok - left)
            delta_refs[s][:, left : left + here] = place_t[:, 0:here]
            if here < 128:
                delta_refs[s + 1][:, 0 : 128 - here] = place_t[:, here:]


def experts_all(cs, gs, rs, router_t, win, wout, slots_most, owners):
    groups = len(cs)
    local = win.shape[0]
    n_tok = cs[0].shape[0]
    total = groups * n_tok
    images = total // ROWS
    room = -(-(slots_most + local * 384 + TILE) // 128) * 128
    width = 2 * D + 128
    deepest = -(-slots_most // local // TILE) * TILE

    def full(shape):
        return pl.BlockSpec(tuple(shape), lambda i: (0,) * len(shape))

    outs = [jax.ShapeDtypeStruct((local, 2, FF, D), BF)]
    outs += [jax.ShapeDtypeStruct((n_tok, D), BF)] * (2 * groups)
    outs += [jax.ShapeDtypeStruct((8, n_tok), F32)] * groups
    vm = pltpu.VMEM
    result = pl.pallas_call(
        functools.partial(experts_kernel, groups, local, "exp"),
        grid=(local,),
        out_shape=outs,
        in_specs=[pl.BlockSpec(memory_space=pl.ANY)] * (2 * groups)
        + [VMEM] * (groups + 1)
        + [pl.BlockSpec((1, D, FF), lambda i: (i, 0, 0)), pl.BlockSpec((1, FF, D), lambda i: (i, 0, 0))],
        out_specs=[pl.BlockSpec((1, 2, FF, D), lambda i: (i, 0, 0, 0))]
        + [pl.BlockSpec(memory_space=pl.ANY)] * (2 * groups)
        + [full(o.shape) for o in outs[2 * groups + 1 :]],
        scratch_shapes=[
            vm((total, width), BF),
            vm((total, 128), F32),
            vm((images, 8, ROWS), F32),
            vm((room, width), BF),
            vm((room, width), BF),
            vm((deepest, D), BF),
            vm((deepest, FF), BF),
            vm((deepest, FF), BF),
            vm((local * 128, width), BF),
            vm((ROWS, width), F32),
            vm((2, 2, ROWS, D), BF),
            vm((8, 128), jnp.int32),
            pltpu.SMEM((8, 128), jnp.int32),
            pltpu.SMEM((local * (images + 3),), jnp.int32),
            pltpu.SemaphoreType.DMA(()),
            pltpu.SemaphoreType.DMA((2 * groups,)),
            pltpu.SemaphoreType.DMA((2, 2)),
        ],
        compiler_params=pltpu.CompilerParams(vmem_limit_bytes=62 << 20),
        name="experts",
    )(*cs, *gs, *rs, router_t, win, wout)
    eg = result[0].reshape((local, 2) + owners + (FF // math.prod(owners), D))
    return eg, result[1 : groups + 1], result[groups + 1 : 2 * groups + 1], result[2 * groups + 1 :]


class Halving:
    def __init__(self, place, links, total, dims, order, received, lead=()):
        self.p, self.links, self.total, self.dims, self.order = place, links, total, dims, order
        self.received, self.lead = received, lead
        self.first = links.reserve(len(order) + 2 * order.count("z"))

    def where(self, fixed):
        return (slice(None),) * len(self.lead) + tuple(fixed.get(b, slice(None)) for b in self.dims)

    def copies(self, k):
        b = self.order[k]
        fixed = {q: self.p.bit[q] for q in self.order[:k]}
        if b == "z":
            return [
                self.links.copy(self.first + k + n, self.total.at[self.where({**fixed, **bits})], self.received[k].at[n], device)
                for n, (bits, device) in enumerate(self.p.others)
            ]
        fixed[b] = 1 - self.p.bit[b]
        return [self.links.copy(self.first + k, self.total.at[self.where(fixed)], self.received[k], self.p.partner[b])]

    def add(self, fixed, other, other_dims):
        free = [b for b in self.dims if b not in fixed]
        sizes = list(self.lead) + [2] * len(free)

        def block(i, _):
            at = []
            for size in reversed(sizes):
                at.insert(0, i % size)
                i = i // size
            full = dict(fixed, **dict(zip(free, at[len(self.lead) :])))
            mine = self.total.at[tuple(at[: len(self.lead)]) + tuple(full[b] for b in self.dims)]
            term = other.at[tuple(at[: len(self.lead)]) + tuple(full[b] for b in other_dims)]
            mine[...] = (mine[...].astype(F32) + term[...].astype(F32)).astype(BF)
            return 0

        lax.fori_loop(0, math.prod(sizes), block, 0)

    def step(self, k, other=None):
        fixed = {q: self.p.bit[q] for q in self.order[:k] if q != "z"}
        other_dims = [b for b in self.dims if b not in fixed]
        if k:
            for copy in self.copies(k - 1):
                copy.wait()
            other = self.received[k - 1]
        if k == len(self.order) and self.order[-1] == "z":
            mine = self.own()
            total = mine[...].astype(F32)
            for n in range(len(self.p.others)):
                total = total + other[n].astype(F32)
            mine[...] = total.astype(BF)
        elif k < len(self.order) and self.order[k] != "z":
            b = self.order[k]
            self.add(dict(fixed, **{b: 1 - self.p.bit[b]}), other, other_dims)
            self.copies(k)[0].start()
            self.add(dict(fixed, **{b: self.p.bit[b]}), other, other_dims)
        else:
            self.add(fixed, other, other_dims)
            if k < len(self.order):
                for copy in self.copies(k):
                    copy.start()

    def own(self):
        return self.total.at[self.where(self.p.bit)]


class ExpertSum:
    def __init__(self, place, links, j, slot, eg, own, part, received, order, out, local_sem):
        self.p, self.links, self.out = place, links, out.at[j]
        self.given = eg.at[j]
        self.mine = own.at[slot]
        self.load = pltpu.make_async_copy(self.given.at[:, :, :, :, place.bit["c"]], self.mine, local_sem.at[slot])
        self.core = links.copy(
            links.reserve(1), self.given.at[:, :, :, :, 1 - place.bit["c"]], part.at[j], place.partner["c"]
        )
        self.halving = Halving(place, links, part.at[j], "hlx", order, received, lead=(2,))

    def run(self, k):
        if k == 0:
            self.core.start()
            return
        if k == 1:
            self.load.wait()
            self.core.wait()
        self.halving.step(k - 1, self.mine)
        if k == 4:
            self.out[...] = self.halving.own()[...].astype(F32)


class SharedSum:
    def __init__(self, place, links, src, core_rx, received, order, out):
        self.p, self.links, self.order, self.out, self.core_rx = place, links, order, out, core_rx
        self.core = links.copy(links.reserve(1), src.at[1 - place.bit["c"]], core_rx, place.partner["c"])
        self.halving = Halving(place, links, src.at[place.bit["c"]], "yxhl", order, received)
        self.first = links.reserve(len(order) + 3)

    def back(self, k):
        known = "c" + self.order[: len(self.order) - k] if k <= len(self.order) else ""
        bits = known.replace("z", "hl")
        mine = self.out.at[tuple(self.p.bit[b] if b in bits else slice(None) for b in BITS)]
        if known[-1] == "z":
            return [self.links.copy(self.first + n, mine, mine, device) for n, (_, device) in enumerate(self.p.others)]
        return [self.links.copy(self.first + 2 + k, mine, mine, self.p.partner[known[-1]])]

    def run(self, k):
        n = len(self.order)
        if k == 0:
            self.core.start()
        elif k <= n:
            if k == 1:
                self.core.wait()
            self.halving.step(k - 1, self.core_rx)
        elif k == n + 1:
            self.halving.step(n)
            self.out[tuple(self.p.bit[b] for b in BITS)] = self.halving.own()[...]
            for copy in self.back(0):
                copy.start()
        else:
            for copy in self.back(k - n - 2):
                copy.wait()
            if k <= 2 * n + 1:
                for copy in self.back(k - n - 1):
                    copy.start()


class SmallSum:
    def __init__(self, place, links, src, rx):
        self.p, self.links, self.src, self.rx = place, links, src, rx
        self.first = links.reserve(len(BITS))

    def copy(self, k):
        return self.links.copy(self.first + k, self.src.at[k], self.rx.at[k], self.p.partner[BITS[k]])

    def run(self, k, out):
        if k:
            self.copy(k - 1).wait()
            total = self.src[k - 1] + self.rx[k - 1]
            if k == len(BITS):
                out[...] = total
                return
            self.src[k] = total
        self.copy(k).start()


GROUPS = ((48, "yxz"), (48, "xyz"), (48, "yxz"), (32, "yxz"), (16, "xyz"))
GROUP_ROWS = (0, 1536, 3072, 4608, 5632)
EXPERT_ORDERS = ("lhx", "xlh", "xlh", "xlh")

ORDER = (
    ("E", 0, 0), ("d", 0, 0), ("d", 1, 0), ("E", 1, 0), ("run", 0, 0), ("E", 1, 1), ("d", 2, 0), ("E", 2, 0),
    ("d", 3, 0), ("E", 0, 1), ("run", 1, 0), ("y", 0, 0), ("E", 3, 0), ("run", 2, 0), ("E", 2, 1), ("run", 3, 0),
    ("run", 4, 0), ("run", 5, 0), ("E", 1, 2), ("run", 6, 0), ("run", 7, 0), ("S", 0, 0), ("E", 0, 2), ("run", 8, 0),
    ("E", 3, 1), ("run", 9, 0), ("run", 10, 0), ("run", 11, 0), ("run", 12, 0), ("S", 0, 1), ("S", 2, 0), ("E", 2, 2),
    ("run", 13, 0), ("S", 1, 0), ("run", 14, 0), ("S", 1, 1), ("S", 2, 1), ("E", 1, 3), ("run", 15, 0), ("S", 0, 2),
    ("run", 16, 0), ("E", 3, 2), ("run", 17, 0), ("S", 2, 2), ("run", 18, 0), ("S", 3, 0), ("S", 0, 3), ("S", 1, 2),
    ("E", 1, 4), ("run", 19, 0), ("S", 2, 3), ("S", 4, 0), ("S", 3, 1), ("S", 0, 4), ("S", 4, 1), ("S", 1, 3),
    ("S", 2, 4), ("S", 3, 2), ("S", 4, 2), ("S", 0, 5), ("S", 4, 3), ("few", 0, 0), ("S", 3, 3), ("S", 1, 4),
    ("few", 1, 0), ("S", 0, 6), ("few", 2, 0), ("S", 2, 5), ("S", 4, 4), ("S", 3, 4), ("E", 0, 3), ("few", 3, 0),
    ("S", 1, 5), ("S", 4, 5), ("S", 3, 5), ("S", 2, 6), ("E", 3, 3), ("run", 20, 0), ("S", 0, 7), ("S", 1, 6),
    ("few", 4, 0), ("S", 3, 6), ("S", 4, 6), ("E", 2, 3), ("E", 3, 4), ("E", 0, 4), ("S", 1, 7), ("few", 5, 0),
    ("S", 2, 7), ("S", 4, 7), ("S", 3, 7), ("S", 0, 8), ("S", 2, 8), ("S", 1, 8), ("S", 4, 8), ("E", 2, 4),
    ("S", 3, 8),
)

LOADED = ("c", "x3", "cot", "d", "delta", "x2", "qkv", "o", "p", "wo", "wqkv", "x1", "wout", "gp", "u", "win", "y", "x0")


def bwd_kernel(linked, *refs):
    names = ["gains", "router_t", "routes", "wqkv", "wo", "win", "wout", "x0", "x1", "x2", "x3", "qkv1", "qkv2"]
    names += ["o1", "o2", "p1", "p2", "u", "gp", "c", "cot", "d", "delta", "y"]
    if linked:
        names += ["d_send", "delta_send", "y_send", "eg"]
    names += ["act_out", "gin_out", "small_out"]
    if linked:
        names += ["eg_out"] + ["out" + str(g) for g in range(len(GROUPS))]
    else:
        names += ["shared_out"]
    names += ["v_" + n for n in LOADED] + ["gv", "a_scr", "dbr_scr", "dqkv_scr", "sem"]
    if linked:
        names += ["d_rx", "delta_rx", "y_rx", "own", "part", "small_src", "small_rx", "eg_sem", "send", "recv"]
        names += ["src" + str(g) for g in range(len(GROUPS))]
        names += ["rx" + str(g) + str(k) for g, (_, order) in enumerate(GROUPS) for k in range(len(order) + 1)]
        names += ["erx" + str(j) + str(k) for j in range(len(EXPERT_ORDERS)) for k in range(3)]
    r = dict(zip(names, refs, strict=True))
    gains, gv, a_scr, dbr_scr, dqkv_scr = (r[n] for n in ("gains", "gv", "a_scr", "dbr_scr", "dqkv_scr"))
    images = gv.shape[0]
    m = images * ROWS
    lo = lane_low(ROWS)

    second = {"qkv": "qkv2", "o": "o2", "p": "p2"}
    copies = {}

    def fetch(name, source):
        copies[name] = pltpu.make_async_copy(r[source], r["v_" + name], r["sem"].at[LOADED.index(name)])
        copies[name].start()

    def need(*wanted):
        for name in wanted:
            copies[name].wait()

    if linked:
        place = Place()
        links = Links(r["send"], r["recv"])
        place.meet([place.partner[b] for b in "cyx"] + [device for _, device in place.others])
        beside = place.partner["y"]
        delta_copy = links.copy(links.reserve(1), r["delta_send"], r["delta_rx"], beside)
        delta_copy.start()
        d_first = links.reserve(images)

        def d_copy(i):
            return links.copy(d_first + i, r["d_send"].at[i], r["d_rx"].at[i], beside)

        turn = [at for kind, at, what in ORDER if (kind, what) == ("E", 1)]
        experts = [
            ExpertSum(
                place, links, j, turn.index(j) % 2, r["eg"], r["own"], r["part"], [r["erx" + str(j) + str(k)] for k in range(3)],
                order, r["eg_out"], r["eg_sem"],
            )
            for j, order in enumerate(EXPERT_ORDERS)
        ]
        experts[turn[0]].load.start()
        experts[turn[1]].load.start()
        y_copy = links.copy(links.reserve(1), r["y_send"], r["y_rx"], beside)
        sums = []
        for g, (_, order) in enumerate(GROUPS):
            rx = [r["rx" + str(g) + str(k)] for k in range(len(order) + 1)]
            sums.append(SharedSum(place, links, r["src" + str(g)], rx[0], rx[1:], order, r["out" + str(g)]))
        few = SmallSum(place, links, r["small_src"], r["small_rx"])
        small = r["small_src"].at[0]
        small[...] = jnp.zeros(small.shape, F32)
    else:
        small = r["small_out"]
    for name in LOADED:
        fetch(name, second.get(name, name))

    def keep(block, value):
        value = value.astype(BF)
        if not linked:
            r["shared_out"][block] = value
            return
        row, end = block * D, block * D + D
        for g, (share, _) in enumerate(GROUPS):
            base, cell = GROUP_ROWS[g], 4 * share
            for q in range(8):
                at = base + q * cell
                if row <= at and at + cell <= end:
                    part = value[at - row : at - row + cell]
                    r["src" + str(g)][q // 4, q // 2 % 2, q % 2] = part.reshape(2, 2, share, D)

    def router():
        need("c", "delta")
        c_all = r["v_c"][...].reshape(m, D)
        g0, g1, first, other = gate_rows(r["router_t"][...], c_all, r["routes"][...])
        delta = r["v_delta"][0:1] + r["v_delta"][1:2]
        if linked:
            delta_copy.wait()
            delta = delta + (r["delta_rx"][0:1] + r["delta_rx"][1:2])
        dl = g0 * g1 * delta
        dlog = jnp.where(first, dl, jnp.where(other, -dl, 0.0)).astype(BF)
        small[4 : 4 + dlog.shape[0]] = dot(dlog, c_all)
        small[0:4] = jnp.zeros((4, D), F32)
        gv[...] = t_dot(dlog, r["router_t"][...]).reshape(images, ROWS, D)
        need("x3", "cot", "d")

    def add_gain(row, by_gain):
        small[row : row + 1] += jnp.sum(by_gain, axis=0, keepdims=True)

    def first(i):
        dc = gv[i] + r["v_d"][i].astype(F32)
        if linked:
            d_copy(i).wait()
            dc = dc + r["d_rx"][i].astype(F32)
        dx, by_gain = norm_back(dc, r["v_x3"][i], gains[3:4])
        gv[i] = r["v_cot"][i].astype(F32) + dx
        add_gain(3, by_gain)
        if i == 0:
            need("x2", "qkv", "o", "p", "wo")
        attend_image(i, 1, gains[2:3], r["v_x2"])

    def attend_image(i, layer, gain, x):
        qkv, o, p = r["v_qkv"], r["v_o"], r["v_p"]
        a_scr[i] = (norm_parts(x[i].astype(F32))[0] * gain).astype(BF)
        dbr = gv[i].astype(BF)
        dbr_scr[i] = dbr
        do = dot_t(dbr, r["v_wo"][layer]).astype(BF)
        dod = do.astype(F32) * o[i].astype(F32)
        for pair in range(HEADS // 2):
            at = 128 * pair
            q = qkv[i, :, at : at + 128] * BF(0.125)
            k = qkv[i, :, D + at : D + at + 128]
            w = qkv[i, :, 2 * D + at : 2 * D + at + 128]
            dqs, dk, dw = [], 0.0, 0.0
            for h in range(2):
                mask = lo if h == 0 else ~lo
                dom = jnp.where(mask, do[:, at : at + 128], BF(0))
                inner = jnp.sum(jnp.where(mask, dod[:, at : at + 128], 0.0), axis=-1, keepdims=True)
                ph = p[i, 2 * pair + h]
                ds = (ph.astype(F32) * (dot_t(dom, w) - inner)).astype(BF)
                dw = dw + t_dot(ph, dom)
                dqs.append(dot(ds, k))
                dk = dk + t_dot(ds, jnp.where(mask, q, BF(0)))
            dqkv_scr[i, :, at : at + 128] = (jnp.where(lo, dqs[0], dqs[1]) * 0.125).astype(BF)
            dqkv_scr[i, :, D + at : D + at + 128] = dk.astype(BF)
            dqkv_scr[i, :, 2 * D + at : 2 * D + at + 128] = dw.astype(BF)

    def attend_weights(block):
        a_all = a_scr[...].reshape(m, D)
        for f in range(3):
            keep(block + f, t_dot(a_all, dqkv_scr[:, :, f * D : f * D + D].reshape(m, D)))
        keep(block + 3, t_dot(r["v_o"][...].reshape(m, D), dbr_scr[...].reshape(m, D)))

    def close(x, layer, row, out):
        def image(i, _):
            da = dot_t(dqkv_scr[i], r["v_wqkv"][layer])
            dx, by_gain = norm_back(da, x[i].astype(F32), gains[row : row + 1])
            out[i] = gv[i] + dx
            add_gain(row, by_gain)
            return 0

        lax.fori_loop(0, images, image, 0)

    def first_close():
        for name in ("qkv", "o", "p"):
            fetch(name, name + "1")
        need("wqkv")
        close(r["v_x2"], 1, 2, gv)
        need("x1", "wout", "gp", "u", "win")

    gp = r["v_gp"]

    def mlp(i):
        a_scr[i] = (norm_parts(r["v_x1"][i])[0] * gains[1:2]).astype(BF)
        dm = gv[i].astype(BF)
        dbr_scr[i] = dm
        for f in range(0, FF, 512):
            du = dot_t(dm, r["v_wout"][f : f + 512])
            gp[i, :, f : f + 512] = (du * gp[i, :, f : f + 512].astype(F32)).astype(BF)

    def mlp_out_weights():
        dm_all = dbr_scr[...].reshape(m, D)
        for f in range(4):
            keep(4 + f, t_dot(r["v_u"][:, :, f * D : f * D + D].reshape(m, D), dm_all))

    def mlp_in_weights():
        b_all = a_scr[...].reshape(m, D)
        for f in range(4):
            keep(8 + f, t_dot(b_all, gp[:, :, f * D : f * D + D].reshape(m, D)))

    def mlp_close():
        def image(i, _):
            db = dot_t(gp[i], r["v_win"][...])
            dx, by_gain = norm_back(db, r["v_x1"][i], gains[1:2])
            gv[i] = gv[i] + dx
            add_gain(1, by_gain)
            return 0

        lax.fori_loop(0, images, image, 0)
        need("x0", "qkv", "o", "p")

    def last(i):
        attend_image(i, 0, gains[0:1], r["v_x0"])

    def last_close():
        close(r["v_x0"], 0, 0, r["gin_out"])

    def act():
        need("y")
        if linked:
            y_copy.wait()
        for i in range(images):
            x4 = r["v_x3"][i] + r["v_y"][i].astype(F32)
            if linked:
                x4 = x4 + r["y_rx"][i].astype(F32)
            r["act_out"][i] = x4.astype(BF)

    compute = [router] + [functools.partial(first, i) for i in range(images)]
    compute += [lambda: attend_weights(0), first_close] + [functools.partial(mlp, i) for i in range(images)]
    compute += [mlp_out_weights, mlp_in_weights, mlp_close] + [functools.partial(last, i) for i in range(images)]
    compute += [lambda: attend_weights(12), last_close, act]
    if not linked:
        for step in compute:
            step()
        return
    done = 0
    for kind, at, what in ORDER:
        if kind == "run":
            compute[done]()
            done += 1
        elif kind == "d":
            d_copy(at).start()
        elif kind == "y":
            y_copy.start()
        elif kind == "few":
            few.run(at, r["small_out"])
        elif kind == "E":
            experts[at].run(what)
            if what == 1 and turn.index(at) + 2 < len(turn):
                experts[turn[turn.index(at) + 2]].load.start()
        else:
            sums[at].run(what)


def dense_backward(weights, router_t, routes, saved, cot, d, delta, y, sent=None):
    gains, wqkv, wo, win, wout = weights
    x0, x1, x2, x3, qkv1, qkv2, o1, o2, p1, p2, u, gp, c = saved
    images = x0.shape[0]
    linked = sent is not None
    small_rows = 16 if linked else 4 + router_t.shape[0]
    ins = [gains, router_t, routes, wqkv, wo, win, wout, *saved, cot, d, delta, y] + (list(sent) if linked else [])
    outs = [
        jax.ShapeDtypeStruct((images, ROWS, D), BF),
        jax.ShapeDtypeStruct((images, ROWS, D), F32),
        jax.ShapeDtypeStruct((small_rows, D), F32),
    ]
    if not linked:
        outs.append(jax.ShapeDtypeStruct((16, D, D), BF))
    vm = pltpu.VMEM
    loaded = dict(
        c=c, x3=x3, cot=cot, d=d, delta=delta, x2=x2, qkv=qkv1, o=o1, p=p1, wo=wo, wqkv=wqkv, x1=x1, wout=wout,
        gp=gp, u=u, win=win, y=y, x0=x0,
    )
    scratch = [vm(loaded[name].shape, loaded[name].dtype) for name in LOADED]
    scratch += [vm((images, ROWS, D), F32), vm((images, ROWS, D), BF), vm((images, ROWS, D), BF)]
    scratch += [vm((images, ROWS, 3 * D), BF), pltpu.SemaphoreType.DMA((len(LOADED),))]
    params = dict(vmem_limit_bytes=62 << 20)
    if linked:
        eg = sent[-1]
        local, share = eg.shape[0], eg.shape[-2]
        outs.append(jax.ShapeDtypeStruct((local, 2, share, D), F32))
        outs += [jax.ShapeDtypeStruct((2,) * 5 + (rows, D), BF) for rows, _ in GROUPS]
        copies = 2 + images + 4 * local + 15 * len(GROUPS) + len(BITS)
        scratch += [vm(d.shape, BF), vm(delta.shape, F32), vm(y.shape, BF)]
        scratch += [
            vm((2, 2, 2, 2, 2, share, D), BF),
            vm((local, 2, 2, 2, 2, share, D), BF),
            vm((len(BITS), small_rows, D), F32),
            vm((len(BITS), small_rows, D), F32),
            pltpu.SemaphoreType.DMA((2,)),
            pltpu.SemaphoreType.DMA((copies,)),
            pltpu.SemaphoreType.DMA((copies,)),
        ]
        scratch += [vm((2,) * 5 + (rows, D), BF) for rows, _ in GROUPS]
        for rows, order in GROUPS:
            scratch += [vm((2,) * (4 - k) + (rows, D), BF) for k in range(len(order.strip("z")) + 1)]
            if "z" in order:
                scratch.append(vm((3, rows, D), BF))
        scratch += [vm((2,) * (3 - k) + (share, D), BF) for _ in EXPERT_ORDERS for k in range(3)]
        params.update(collective_id=1, has_side_effects=True)
    return pl.pallas_call(
        functools.partial(bwd_kernel, linked),
        out_shape=outs,
        in_specs=[VMEM] * 3 + [pl.BlockSpec(memory_space=pl.ANY)] * (len(ins) - 3),
        out_specs=[VMEM] * len(outs),
        scratch_shapes=scratch,
        compiler_params=pltpu.CompilerParams(**params),
        name="dense_backward",
    )(*ins)


def finish_kernel(n_shared, act, gin, small, eg, *refs):
    shared, refs = refs[:n_shared], refs[n_shared:]
    act_out, gin_out, qkv_out, proj_out, gain_out, mlp_in_out, mlp_out_out, router_out, in_out, out_out = refs[:10]
    v_shared, v_wide, v_gin, v_act, in_sem, out_sem = refs[10:]
    images = act.shape[0]
    blocks = v_wide.shape[0]
    targets = {3: proj_out.at[1], 15: proj_out.at[0]}
    for f in range(3):
        targets[f] = qkv_out.at[1, :, pl.ds(f * D, D)]
        targets[12 + f] = qkv_out.at[0, :, pl.ds(f * D, D)]
    for f in range(4):
        targets[4 + f] = mlp_out_out.at[pl.ds(f * D, D)]
        targets[8 + f] = mlp_in_out.at[:, pl.ds(f * D, D)]
    loads, at = [], 0
    for k, part in enumerate(shared):
        rows = part.shape[0]
        loads.append((at, pltpu.make_async_copy(part, v_shared.at[pl.ds(at, rows)], in_sem.at[k])))
        at += rows
    load_gin = pltpu.make_async_copy(gin, v_gin, in_sem.at[n_shared])
    load_act = pltpu.make_async_copy(act, v_act, in_sem.at[n_shared + 1])
    for _, load in loads:
        load.start()
    load_gin.start()
    load_act.start()

    def store(b):
        return pltpu.make_async_copy(v_wide.at[b], targets[b], out_sem.at[b])

    waited = 0
    for b in range(blocks):
        while waited < n_shared and loads[waited][0] < (b + 1) * D:
            loads[waited][1].wait()
            waited += 1
        v_wide[b] = v_shared[b * D : (b + 1) * D].astype(F32)
        store(b).start()
    gain_out[...] = small[0:4]
    router_out[...] = small[4 : 4 + router_out.shape[0]]
    for e in range(eg.shape[0]):
        in_out[e] = eg[e, 0]
        out_out[e] = eg[e, 1]
    load_gin.wait()
    load_act.wait()
    for i in range(images):
        gin_out[i * PATCHES : (i + 1) * PATCHES] = v_act[i, 0:PATCHES].astype(F32)
    act_out[...] = gin_out[...].astype(BF)
    for i in range(images):
        gin_out[i * PATCHES : (i + 1) * PATCHES] = v_gin[i, 0:PATCHES]
    for b in range(blocks):
        store(b).wait()


def finish(act, gin, shared, small, eg, experts):
    images, local, share = act.shape[0], eg.shape[0], eg.shape[2]
    row_count = images * PATCHES
    blocks = 16
    outs = [
        jax.ShapeDtypeStruct((row_count, D), BF),
        jax.ShapeDtypeStruct((row_count, D), F32),
        jax.ShapeDtypeStruct((2, D, 3 * D), F32),
        jax.ShapeDtypeStruct((2, D, D), F32),
        jax.ShapeDtypeStruct((4, D), F32),
        jax.ShapeDtypeStruct((D, FF), F32),
        jax.ShapeDtypeStruct((FF, D), F32),
        jax.ShapeDtypeStruct((experts, D), F32),
        jax.ShapeDtypeStruct((local, share, D), F32),
        jax.ShapeDtypeStruct((local, share, D), F32),
    ]
    far = pl.BlockSpec(memory_space=pl.ANY)
    return pl.pallas_call(
        functools.partial(finish_kernel, len(shared)),
        out_shape=outs,
        in_specs=[far, far, VMEM, VMEM] + [far] * len(shared),
        out_specs=[VMEM, VMEM, far, far, VMEM, far, far, VMEM, VMEM, VMEM],
        scratch_shapes=[
            pltpu.VMEM((blocks * D, D), BF),
            pltpu.VMEM((blocks, D, D), F32),
            pltpu.VMEM(gin.shape, F32),
            pltpu.VMEM(act.shape, BF),
            pltpu.SemaphoreType.DMA((len(shared) + 2,)),
            pltpu.SemaphoreType.DMA((blocks,)),
        ],
        compiler_params=pltpu.CompilerParams(vmem_limit_bytes=62 << 20),
        name="finish",
    )(act, gin, small, eg, *shared)


def from_peer(array, groups, shift):
    return lax.ppermute(array, "exp", [(i, (i + shift) % groups) for i in range(groups)])


def shards(
    tokens, routes, norm_gains, attn_qkv, attn_out, mlp_in, mlp_out, router, experts_in, experts_out, cotangent
):
    row_count = tokens.shape[0]
    groups = lax.axis_size("exp")
    local = experts_in.shape[0]
    choices = routes.shape[1]
    capacity = 2 * choices * row_count // (local * groups)
    images = row_count // PATCHES
    n_tok = images * ROWS
    routes_t = routes.T.reshape(choices, images, PATCHES)
    routes_t = jnp.pad(routes_t, ((0, 8 - choices), (0, 0), (0, ROWS - PATCHES)), constant_values=-1)
    routes_t = routes_t.reshape(8, n_tok)
    router_t = router.T
    rep = lax.axis_size("rep")
    known = (rep, groups, local) == (16, 2, 4)
    owners = (2, 2, 2, 2) if known else (rep,)
    x0, cot, x1, x2, x3, qkv1, qkv2, o1, o2, p1, p2, u, gp, c, *received = dense_forward(
        tokens, cotangent, routes_t, norm_gains, attn_qkv, attn_out, mlp_in, mlp_out, known
    )

    def of_all(mine, place):
        if known:
            others = [received[place]]
        else:
            others = [from_peer(mine, groups, k) for k in range(1, groups)]
        return [part.reshape(-1, part.shape[-1]) for part in [mine] + others]

    cs, gs, rs = of_all(c, 0), of_all(cot, 1), of_all(routes_t, 2)
    eg, ys, ds, deltas = experts_all(
        cs, gs, rs, router_t, experts_in, experts_out, local * capacity * groups, owners
    )

    weights = (norm_gains, attn_qkv, attn_out, mlp_in, mlp_out)
    saved = (x0, x1, x2, x3, qkv1, qkv2, o1, o2, p1, p2, u, gp, c)
    by_image = (images, ROWS, D)
    experts = router_t.shape[0]
    if known:
        sent = (ds[1].reshape(by_image), deltas[1], ys[1].reshape(by_image), eg)
        act, gin, small, eg, *shared = dense_backward(
            weights, router_t, routes_t, saved, cot, ds[0].reshape(by_image), deltas[0], ys[0].reshape(by_image), sent
        )
        shared = [part.reshape(-1, D) for part in shared]
    else:

        def back(parts):
            total = parts[0].astype(F32)
            for k in range(1, groups):
                total = total + from_peer(parts[k], groups, groups - k).astype(F32)
            return total

        d, delta, y = back(ds).astype(BF), back(deltas), back(ys).astype(BF)
        act, gin, small, shared = dense_backward(
            weights, router_t, routes_t, saved, cot, d.reshape(by_image), delta, y.reshape(by_image)
        )
        eg = lax.psum_scatter(eg, "rep", scatter_dimension=2, tiled=True).reshape(local, 2, FF // rep, D).astype(F32)
        shared, small = lax.psum((shared, small), ("rep", "exp"))
        shared = [shared.reshape(-1, D)]
    outs = list(finish(act, gin, shared, small, eg, experts))
    outs[7] = outs[7].T
    outs[8] = jnp.swapaxes(outs[8], 1, 2)
    return tuple(outs)


def solution(mesh):
    rows = P(("rep", "exp"), None)
    return jax.shard_map(
        shards,
        mesh=mesh,
        in_specs=(rows, rows, P(), P(), P(), P(), P(), P(), P("exp", None, None), P("exp", None, None), rows),
        out_specs=(rows, rows, P(), P(), P(), P(), P(), P(), P("exp", None, "rep"), P("exp", "rep", None)),
        check_vma=False,
    )
```

```python
import functools
import math

import jax
import jax.numpy as jnp
from jax import lax
from jax.experimental import pallas as pl
from jax.experimental.pallas import tpu as pltpu
from jax.sharding import PartitionSpec as P

F32 = jnp.float32
BF = jnp.bfloat16
HEADS = 6
PATCHES = 197
ROWS = 208
EPS = 1e-6
TILE = 256
D = 384
FF = 1536
IMAGES_AT_ONCE = 1
VMEM = pl.BlockSpec(memory_space=pltpu.VMEM)


def dot(a, b):
    return lax.dot_general(a, b, (((1,), (0,)), ((), ())), preferred_element_type=F32)


def dot_t(a, b):
    return lax.dot_general(a, b, (((1,), (1,)), ((), ())), preferred_element_type=F32)


def t_dot(a, b):
    return lax.dot_general(a, b, (((0,), (0,)), ((), ())), preferred_element_type=F32)


def norm_parts(x):
    centred = x - jnp.mean(x, axis=-1, keepdims=True)
    rstd = lax.rsqrt(jnp.mean(centred * centred, axis=-1, keepdims=True) + EPS)
    return centred * rstd, rstd


def norm_back(grad, x, gain):
    xh, rstd = norm_parts(x)
    dxh = grad * gain
    inner = dxh - jnp.mean(dxh, axis=-1, keepdims=True)
    return rstd * (inner - xh * jnp.mean(dxh * xh, axis=-1, keepdims=True)), grad * xh


def gelu_parts(h):
    phi = 0.5 + 0.5 * lax.erf(0.7071067811865476 * h)
    e = jnp.exp2(h * h * -0.7213475204444817)
    return h * phi, phi + h * (0.3989422804014327 * e)


def lane_low(rows):
    return lax.broadcasted_iota(jnp.int32, (rows, 128), 1) < 64


MESH = pl.DeviceIdType.MESH
BITS = "cyxhl"


class Place:
    def __init__(self):
        r = lax.axis_index("rep")
        y = lax.axis_index("exp")
        self.bit = {"c": r % 2, "y": y, "x": (r // 2) % 2, "h": r // 8, "l": (r // 4) % 2}
        stride = {"c": 1, "x": 2, "l": 4, "h": 8}
        self.partner = {b: (r + stride[b] * (1 - 2 * self.bit[b]), y) for b in stride}
        self.partner["y"] = (r, 1 - y)
        self.others = []
        for k in range(1, 4):
            z = (r // 4 + k) % 4
            self.others.append(({"h": z // 2, "l": z % 2}, (z * 4 + r % 4, y)))

    def greet(self, partners):
        for partner in partners:
            pl.semaphore_signal(pltpu.get_barrier_semaphore(), inc=1, device_id=partner, device_id_type=MESH)

    def meet(self, partners):
        pl.semaphore_wait(pltpu.get_barrier_semaphore(), len(partners))


class Links:
    def __init__(self, send, recv):
        self.send, self.recv, self.used = send, recv, 0

    def reserve(self, count):
        first = self.used
        self.used += count
        return first

    def copy(self, at, src, dst, device):
        return pltpu.make_async_remote_copy(
            src_ref=src, dst_ref=dst, send_sem=self.send.at[at], recv_sem=self.recv.at[at],
            device_id=device, device_id_type=MESH,
        )

    def start(self, at, src, dst, device):
        copy = self.copy(at, src, dst, device)
        copy.start()
        return copy


def fwd_kernel(linked, *refs):
    names = ["tokens", "cot", "routes", "gains", "wqkv", "wo", "win", "wout"]
    names += ["routes_out", "x0", "cot_out", "x1", "x2", "x3", "qkv1", "qkv2", "o1", "o2", "p1", "p2", "u", "gp", "c"]
    if linked:
        names += ["c_rx", "cot_rx", "routes_rx"]
    names += ["wide"]
    if linked:
        names += ["c_scr", "send", "recv"]
    r = dict(zip(names, refs, strict=True))
    gains = r["gains"]
    ib = r["x1"].shape[0]
    m = ib * ROWS
    images = r["x0"].shape[0]
    step = pl.program_id(0)
    lo = lane_low(ROWS)
    valid = lax.broadcasted_iota(jnp.int32, (ROWS, ROWS), 1) < PATCHES
    real = lax.broadcasted_iota(jnp.int32, (ROWS, D), 0) < PATCHES
    if linked:
        place = Place()
        links = Links(r["send"], r["recv"])

        def exchange(at, src, dst):
            return links.copy(at, src, dst, place.partner["y"])

        early = [exchange(0, r["cot_out"], r["cot_rx"]), exchange(1, r["routes_out"], r["routes_rx"])]

        def c_copy(image):
            return exchange(2 + image, r["c_scr"].at[image], r["c_rx"].at[image])

    @pl.when(step == 0)
    def _():
        if linked:
            place.greet([place.partner["y"]])
        wide = r["wide"]
        slots = r["routes_out"]
        slots[...] = jnp.full(slots.shape, -1, jnp.int32)
        for i in range(images):
            slots[0:2, i * ROWS : i * ROWS + PATCHES] = r["routes"][:, i * PATCHES : (i + 1) * PATCHES]
        for source, target in (("cot", "cot_out"), ("tokens", "x0")):
            wide[0 : images * PATCHES] = r[source][...].astype(F32)
            for i in range(images):
                rows = wide[i * PATCHES : i * PATCHES + ROWS]
                r[target][i] = jnp.where(real, rows, 0.0).astype(BF)
            if linked and source == "cot":
                place.meet([place.partner["y"]])
                for copy in early:
                    copy.start()

    def attend_image(i, qkv_ref, o_ref, p_ref):
        for pair in range(HEADS // 2):
            at = 128 * pair
            q = qkv_ref[i, :, at : at + 128] * BF(0.125)
            k = qkv_ref[i, :, D + at : D + at + 128]
            w = qkv_ref[i, :, 2 * D + at : 2 * D + at + 128]
            mixed = []
            for h in range(2):
                qm = jnp.where(lo if h == 0 else ~lo, q, BF(0))
                s = jnp.where(valid, dot_t(qm, k), -1e30)
                s = jnp.exp(s - jnp.max(s, axis=-1, keepdims=True))
                p = (s * (1.0 / jnp.sum(s, axis=-1, keepdims=True))).astype(BF)
                p_ref[i, 2 * pair + h] = p
                mixed.append(dot(p, w))
            o_ref[i, :, at : at + 128] = jnp.where(lo, mixed[0], mixed[1]).astype(BF)

    def project(x, layer, gain, qkv_ref):
        a = (norm_parts(x)[0] * gain).astype(BF)
        qkv_ref[...] = dot(a, r["wqkv"][layer]).astype(BF).reshape(ib, ROWS, 3 * D)

    x0 = r["x0"][pl.ds(step * ib, ib)].astype(F32).reshape(m, D)
    project(x0, 0, gains[0:1], r["qkv1"])
    for i in range(ib):
        attend_image(i, r["qkv1"], r["o1"], r["p1"])
    x1 = x0 + dot(r["o1"][...].reshape(m, D), r["wo"][0])
    r["x1"][...] = x1.reshape(ib, ROWS, D)
    b = (norm_parts(x1)[0] * gains[1:2]).astype(BF)
    x2 = x1
    for f in range(0, FF, 512):
        u, gp = gelu_parts(dot(b, r["win"][:, f : f + 512]))
        u = u.astype(BF)
        r["u"][:, :, f : f + 512] = u.reshape(ib, ROWS, 512)
        r["gp"][:, :, f : f + 512] = gp.astype(BF).reshape(ib, ROWS, 512)
        x2 = x2 + dot(u, r["wout"][f : f + 512])
    r["x2"][...] = x2.reshape(ib, ROWS, D)
    project(x2, 1, gains[2:3], r["qkv2"])

    def last(i, _):
        attend_image(i, r["qkv2"], r["o2"], r["p2"])
        x3 = r["x2"][i] + dot(r["o2"][i], r["wo"][1])
        r["x3"][i] = x3
        c = (norm_parts(x3)[0] * gains[3:4]).astype(BF)
        r["c"][i] = c
        if linked:
            r["c_scr"][step * ib + i] = c
            c_copy(step * ib + i).start()
        return 0

    lax.fori_loop(0, ib, last, 0)

    if linked:

        @pl.when(step == pl.num_programs(0) - 1)
        def _():
            for copy in early + [c_copy(i) for i in range(images)]:
                copy.wait()


def dense_forward(tokens, cot, routes, gains, wqkv, wo, win, wout, linked):
    n = tokens.shape[0] // PATCHES
    ib = IMAGES_AT_ONCE if n % IMAGES_AT_ONCE == 0 else 1

    def out(*shape, dtype=BF):
        return jax.ShapeDtypeStruct((n,) + shape, dtype)

    def block(shape):
        return pl.BlockSpec((ib,) + tuple(shape[1:]), lambda i: (i,) + (0,) * (len(shape) - 1))

    whole = pl.BlockSpec((n, ROWS, D), lambda i: (0, 0, 0))
    routes_shape = jax.ShapeDtypeStruct((8, n * ROWS), jnp.int32)
    outs = [routes_shape] + [out(ROWS, D)] * 2 + [out(ROWS, D, dtype=F32)] * 3 + [out(ROWS, 3 * D)] * 2 + [out(ROWS, D)] * 2
    outs += [out(HEADS, ROWS, ROWS)] * 2 + [out(ROWS, FF)] * 2 + [out(ROWS, D)]
    out_specs = [pl.BlockSpec(routes_shape.shape, lambda i: (0, 0)), whole, whole] + [block(o.shape) for o in outs[3:]]
    scratch = [pltpu.VMEM(((n - 1) * PATCHES + ROWS, D), F32)]
    params = dict(vmem_limit_bytes=62 << 20)
    if linked:
        outs += [out(ROWS, D)] * 2 + [routes_shape]
        out_specs += [pl.BlockSpec(memory_space=pl.ANY)] * 3
        copies = pltpu.SemaphoreType.DMA((2 + n,))
        scratch += [pltpu.VMEM((n, ROWS, D), BF), copies, copies]
        params.update(collective_id=2, has_side_effects=True)
    return pl.pallas_call(
        functools.partial(fwd_kernel, linked),
        grid=(n // ib,),
        out_shape=outs,
        in_specs=[VMEM] * 8,
        out_specs=out_specs,
        scratch_shapes=scratch,
        compiler_params=pltpu.CompilerParams(**params),
        name="dense_forward",
    )(tokens, cot, routes, gains, wqkv, wo, win, wout)


def gate_rows(router_t, c, routes):
    logits = dot_t(router_t, c)
    expert = lax.broadcasted_iota(jnp.int32, logits.shape, 0)
    first, second = expert == routes[0:1], expert == routes[1:2]
    diff = jnp.sum(jnp.where(first, logits, 0.0) - jnp.where(second, logits, 0.0), axis=0, keepdims=True)
    return 1.0 / (1.0 + jnp.exp(-diff)), 1.0 / (1.0 + jnp.exp(diff)), first, second


def experts_kernel(groups, local, exp_axis, *refs):
    c_refs, g_refs, r_refs = refs[:groups], refs[groups : 2 * groups], refs[2 * groups : 3 * groups]
    router_t, win, wout = refs[3 * groups : 3 * groups + 3]
    outs = refs[3 * groups + 3 :]
    eg_ref, y_refs, d_refs, delta_refs = outs[0], outs[1 : groups + 1], outs[groups + 1 : 2 * groups + 1], outs[2 * groups + 1 : 3 * groups + 1]
    ci, cols, place, xg, slots, dy_scr, u_scr, gp_scr, stack, back, staged, count_v, count, plan, sem, load_sem, out_sem = outs[3 * groups + 1 :]
    n_tok = c_refs[0].shape[0]
    total = groups * n_tok
    images = total // ROWS
    step = pl.program_id(0)
    first_expert = lax.axis_index(exp_axis) * local

    def window(e, i):
        begin = plan[e * (images + 1) + i]
        return begin, pl.multiple_of(begin // 16 * 16, 16)

    def windows(i):
        most = jnp.int32(1)
        for e in range(local):
            at = window(e, i)[1]
            most = jnp.maximum(most, (plan[e * (images + 1) + i + 1] - at + 127) // 128)
        return most

    @pl.when(step == 0)
    def _():
        loads = []
        for k, (sources, first) in enumerate(((c_refs, 0), (g_refs, D + 128))):
            for s in range(groups):
                target = ci.at[pl.ds(s * n_tok, n_tok), pl.ds(first, D)]
                loads.append(pltpu.make_async_copy(sources[s], target, load_sem.at[k * groups + s]))
                loads[-1].start()
        for load in loads:
            load.wait()
        routes = jnp.concatenate([r[0:2] for r in r_refs], axis=1)
        g0, g1, _, _ = gate_rows(router_t[...], ci[:, 0:D], routes)
        expert_row = lax.broadcasted_iota(jnp.int32, (8, total), 0)
        mine, inside = first_expert + expert_row, expert_row < local
        is0, is1 = (mine == routes[0:1]) & inside, (mine == routes[1:2]) & inside
        member = jnp.where(is0 | is1, 1.0, 0.0)
        lane = lax.broadcasted_iota(jnp.int32, (8, total), 1)
        of_image = lax.broadcasted_iota(jnp.int32, (total, 128), 0) // ROWS
        of_image = jnp.where(of_image == lax.broadcasted_iota(jnp.int32, (total, 128), 1), 1.0, 0.0)
        count_v[...] = dot(member.astype(BF), of_image.astype(BF)).astype(jnp.int32)
        to_scalars = pltpu.make_async_copy(count_v, count, sem)
        to_scalars.start()
        upto = member
        shift = 1
        while shift < total:
            upto = upto + jnp.where(lane >= shift, pltpu.roll(upto, shift, 1), 0.0)
            shift *= 2
        to_scalars.wait()
        begin = jnp.int32(0)
        starts = []
        for e in range(local):
            starts.append(begin.astype(F32))
            plan[local * (images + 1) + 2 * e] = begin
            first = begin
            for i in range(images):
                plan[e * (images + 1) + i] = begin
                begin = begin + count[e, i]
            plan[e * (images + 1) + images] = begin
            plan[local * (images + 1) + 2 * e + 1] = begin - first
            begin = first + (begin - first + 127) // 128 * 128 + 256
        start = jnp.zeros((8, total), F32)
        for e in range(local):
            start = jnp.where(expert_row == e, starts[e], start)
        slot = start + jnp.where(member > 0, upto, 0.0)
        slot0 = jnp.sum(jnp.where(is0, slot, 0.0), axis=0, keepdims=True) - 1.0
        slot1 = jnp.sum(jnp.where(is1, slot, 0.0), axis=0, keepdims=True) - 1.0
        slot = jnp.where(member > 0, slot - 1.0, -1.0)
        for i in range(images):
            place[i] = slot[:, i * ROWS : (i + 1) * ROWS]
        gates = jnp.where(is0, g0, jnp.where(is1, g1, 0.0))
        sign = jnp.where(is0, 1.0, jnp.where(is1, -1.0, 0.0))
        slot_rows = jnp.where(expert_row == 0, slot0, jnp.where(expert_row == 1, slot1, 0.0))
        stacked = jnp.concatenate([gates, sign, slot_rows, jnp.zeros((104, total), F32)], axis=0)
        lane128 = lax.broadcasted_iota(jnp.int32, (128, 128), 1)
        for at in range(0, total, 128):
            col = stacked[:, at : at + 128].T
            cols[at : at + 128] = col
            low = col - col.astype(BF).astype(F32)
            info = jnp.where(lane128 < 16, col, jnp.where(lane128 < 24, pltpu.roll(low, 16, 1), 0.0))
            ci[at : at + 128, D : D + 128] = info.astype(BF)

        row = lax.broadcasted_iota(jnp.int32, (128, ROWS), 0)
        head = lax.broadcasted_iota(jnp.int32, (16, 2 * D + 128), 0)

        def gather(i, _):
            rows = ci[pl.ds(pl.multiple_of(i * ROWS, 16), ROWS)]

            def part(w, _):
                picks = []
                for e in range(local):
                    at = window(e, i)[1] + 128 * w
                    picks.append(jnp.where(place[i, e : e + 1] == (at + row).astype(F32), 1.0, 0.0).astype(BF))
                found = dot(jnp.concatenate(picks, axis=0), rows).astype(BF)
                for e in range(local):
                    begin, at = window(e, i)
                    at = pl.multiple_of(at + 128 * w, 16)
                    old = xg[pl.ds(at, 16)]
                    new = found[e * 128 : e * 128 + 16]
                    xg[pl.ds(at, 16)] = jnp.where(at + head < begin, old, new)
                    xg[pl.ds(pl.multiple_of(at + 16, 16), 112)] = found[e * 128 + 16 : e * 128 + 128]
                return 0

            return lax.fori_loop(0, windows(i), part, 0)

        lax.fori_loop(0, images, gather, 0)
        for e in range(local):
            end, at = window(e, images)
            xg[pl.ds(at, 16)] = jnp.where(at + head < end, xg[pl.ds(at, 16)], jnp.zeros(head.shape, BF))
            xg[pl.ds(pl.multiple_of(at + 16, 16), 240)] = jnp.zeros((240, 2 * D + 128), BF)

    begin, n = plan[local * (images + 1) + 2 * step], plan[local * (images + 1) + 2 * step + 1]

    def tile(row, size):
        at = pl.multiple_of(begin + row, 16)
        here = pl.ds(pl.multiple_of(row, TILE // 4), size)
        lane = lax.broadcasted_iota(jnp.int32, (size, 128), 1)
        x = xg[pl.ds(at, size), 0:D]
        info = xg[pl.ds(at, size), D : D + 128].astype(F32)
        g4r = xg[pl.ds(at, size), D + 128 :].astype(F32)
        gate = jnp.sum(jnp.where((lane == step) | (lane == step + 16), info, 0.0), axis=-1, keepdims=True)
        sign = jnp.sum(jnp.where(lane == step + 8, info, 0.0), axis=-1, keepdims=True)
        dy = (gate * g4r).astype(BF)
        dy_scr[here] = dy
        for f in range(0, FF, 512):
            u, gp = gelu_parts(dot(x, win[0, :, f : f + 512]))
            u_scr[here, f : f + 512] = u.astype(BF)
            gp_scr[here, f : f + 512] = gp.astype(BF)
        ey = dot(u_scr[here], wout[0]).astype(BF).astype(F32)
        dg = sign * jnp.sum(g4r * ey, axis=-1, keepdims=True)
        for f in range(0, FF, 512):
            du = dot_t(dy, wout[0, f : f + 512])
            gp_scr[here, f : f + 512] = (du * gp_scr[here, f : f + 512].astype(F32)).astype(BF)
        dcp = dot_t(gp_scr[here], win[0])
        slots[pl.ds(at, size), 0:D] = (gate * ey).astype(BF)
        slots[pl.ds(at, size), D : 2 * D] = dcp.astype(BF)
        low = dg - dg.astype(BF).astype(F32)
        slots[pl.ds(at, size), 2 * D :] = jnp.where(lane == 0, dg, jnp.where(lane == 1, low, 0.0)).astype(BF)

    whole = (n + TILE // 4 - 1) // TILE

    def full_tile(j, _):
        tile(j * TILE, TILE)
        return 0

    lax.fori_loop(0, whole, full_tile, 0)

    for size in range(TILE // 4, TILE, TILE // 4):

        @pl.when((n > whole * TILE + size - TILE // 4) & (n <= whole * TILE + size))
        def _(size=size):
            tile(whole * TILE, size)
            rest = pl.ds(pl.multiple_of(whole * TILE + size, TILE // 4), TILE - size)
            for scratch in (dy_scr, u_scr, gp_scr):
                scratch[rest] = jnp.zeros((TILE - size,) + scratch.shape[1:], BF)

    after = pl.multiple_of(begin + (n + TILE // 4 - 1) // (TILE // 4) * (TILE // 4), 16)
    slots[pl.ds(after, 256)] = jnp.zeros((256, 2 * D + 128), BF)

    rounded = (n + TILE - 1) // TILE

    @pl.when(rounded == 0)
    def _():
        eg_ref[...] = jnp.zeros_like(eg_ref)

    for tiles in range(1, u_scr.shape[0] // TILE + 1):

        @pl.when(rounded == tiles)
        def _(depth=tiles * TILE):
            x = xg[pl.ds(pl.multiple_of(begin, 16), depth), 0:D]
            dy = dy_scr[0:depth]
            for f in range(0, FF, D):
                eg_ref[0, 0, f : f + D] = t_dot(gp_scr[0:depth, f : f + D], x).astype(BF)
                eg_ref[0, 1, f : f + D] = t_dot(u_scr[0:depth, f : f + D], dy).astype(BF)

    @pl.when(step == local - 1)
    def _():
        lane = lax.broadcasted_iota(jnp.int32, (ROWS, 128), 1)

        def out_copies(s, i, slot):
            rows = pl.ds(pl.multiple_of(i * ROWS, 16), ROWS)
            return [
                pltpu.make_async_copy(staged.at[slot, k], target.at[rows], out_sem.at[slot, k])
                for k, target in enumerate((y_refs[s], d_refs[s]))
            ]

        def restore(s, i):
            image = s * (n_tok // ROWS) + i
            at_rows = pl.multiple_of(image * ROWS, 16)
            slot0, slot1 = cols[pl.ds(at_rows, ROWS), 16:17], cols[pl.ds(at_rows, ROWS), 17:18]

            def part(w):
                picks = []
                for e in range(local):
                    at = pl.multiple_of(window(e, image)[1] + 128 * w, 16)
                    stack[e * 128 : (e + 1) * 128] = slots[pl.ds(at, 128)]
                    slot = (at + lane).astype(F32)
                    picks.append(jnp.where((slot0 == slot) | (slot1 == slot), 1.0, 0.0).astype(BF))
                return dot(jnp.concatenate(picks, axis=1), stack[...])

            back[...] = part(0)

            def more(w, _):
                back[...] += part(w)
                return 0

            lax.fori_loop(1, windows(image), more, 0)
            slot = lax.rem(image, 2)

            @pl.when(image >= 2)
            def _():
                for copy in out_copies(s, i, slot):
                    copy.wait()

            staged[slot, 0] = back[:, 0:D].astype(BF)
            staged[slot, 1] = back[:, D : 2 * D].astype(BF)
            for copy in out_copies(s, i, slot):
                copy.start()
            cols[pl.ds(at_rows, ROWS)] = back[:, 2 * D :]

        for s in range(groups):

            def one(i, _, s=s):
                restore(s, i)
                return 0

            lax.fori_loop(0, n_tok // ROWS, one, 0)
        for slot in range(2):
            for copy in out_copies(groups - 1, 0, slot):
                copy.wait()
        for at in range(0, total, 128):
            place_t = cols[at : at + 128].T[0:8]
            s, left = divmod(at, n_tok)
            here = min(128, n_tok - left)
            delta_refs[s][:, left : left + here] = place_t[:, 0:here]
            if here < 128:
                delta_refs[s + 1][:, 0 : 128 - here] = place_t[:, here:]


def experts_all(cs, gs, rs, router_t, win, wout, slots_most, owners):
    groups = len(cs)
    local = win.shape[0]
    n_tok = cs[0].shape[0]
    total = groups * n_tok
    images = total // ROWS
    room = -(-(slots_most + local * 384 + TILE) // 128) * 128
    width = 2 * D + 128
    deepest = -(-slots_most // local // TILE) * TILE

    def full(shape):
        return pl.BlockSpec(tuple(shape), lambda i: (0,) * len(shape))

    outs = [jax.ShapeDtypeStruct((local, 2, FF, D), BF)]
    outs += [jax.ShapeDtypeStruct((n_tok, D), BF)] * (2 * groups)
    outs += [jax.ShapeDtypeStruct((8, n_tok), F32)] * groups
    vm = pltpu.VMEM
    result = pl.pallas_call(
        functools.partial(experts_kernel, groups, local, "exp"),
        grid=(local,),
        out_shape=outs,
        in_specs=[pl.BlockSpec(memory_space=pl.ANY)] * (2 * groups)
        + [VMEM] * (groups + 1)
        + [pl.BlockSpec((1, D, FF), lambda i: (i, 0, 0)), pl.BlockSpec((1, FF, D), lambda i: (i, 0, 0))],
        out_specs=[pl.BlockSpec((1, 2, FF, D), lambda i: (i, 0, 0, 0))]
        + [pl.BlockSpec(memory_space=pl.ANY)] * (2 * groups)
        + [full(o.shape) for o in outs[2 * groups + 1 :]],
        scratch_shapes=[
            vm((total, width), BF),
            vm((total, 128), F32),
            vm((images, 8, ROWS), F32),
            vm((room, width), BF),
            vm((room, width), BF),
            vm((deepest, D), BF),
            vm((deepest, FF), BF),
            vm((deepest, FF), BF),
            vm((local * 128, width), BF),
            vm((ROWS, width), F32),
            vm((2, 2, ROWS, D), BF),
            vm((8, 128), jnp.int32),
            pltpu.SMEM((8, 128), jnp.int32),
            pltpu.SMEM((local * (images + 3),), jnp.int32),
            pltpu.SemaphoreType.DMA(()),
            pltpu.SemaphoreType.DMA((2 * groups,)),
            pltpu.SemaphoreType.DMA((2, 2)),
        ],
        compiler_params=pltpu.CompilerParams(vmem_limit_bytes=62 << 20),
        name="experts",
    )(*cs, *gs, *rs, router_t, win, wout)
    eg = result[0].reshape((local, 2) + owners + (FF // math.prod(owners), D))
    return eg, result[1 : groups + 1], result[groups + 1 : 2 * groups + 1], result[2 * groups + 1 :]


class Halving:
    def __init__(self, place, links, total, dims, order, received, lead=()):
        self.p, self.links, self.total, self.dims, self.order = place, links, total, dims, order
        self.received, self.lead = received, lead
        self.first = links.reserve(len(order) + 2 * order.count("z"))

    def where(self, fixed):
        return (slice(None),) * len(self.lead) + tuple(fixed.get(b, slice(None)) for b in self.dims)

    def copies(self, k):
        b = self.order[k]
        fixed = {q: self.p.bit[q] for q in self.order[:k]}
        if b == "z":
            return [
                self.links.copy(self.first + k + n, self.total.at[self.where({**fixed, **bits})], self.received[k].at[n], device)
                for n, (bits, device) in enumerate(self.p.others)
            ]
        fixed[b] = 1 - self.p.bit[b]
        return [self.links.copy(self.first + k, self.total.at[self.where(fixed)], self.received[k], self.p.partner[b])]

    def add(self, fixed, other, other_dims):
        free = [b for b in self.dims if b not in fixed]
        sizes = list(self.lead) + [2] * len(free)

        def block(i, _):
            at = []
            for size in reversed(sizes):
                at.insert(0, i % size)
                i = i // size
            full = dict(fixed, **dict(zip(free, at[len(self.lead) :])))
            mine = self.total.at[tuple(at[: len(self.lead)]) + tuple(full[b] for b in self.dims)]
            term = other.at[tuple(at[: len(self.lead)]) + tuple(full[b] for b in other_dims)]
            mine[...] = (mine[...].astype(F32) + term[...].astype(F32)).astype(BF)
            return 0

        lax.fori_loop(0, math.prod(sizes), block, 0)

    def step(self, k, other=None):
        fixed = {q: self.p.bit[q] for q in self.order[:k] if q != "z"}
        other_dims = [b for b in self.dims if b not in fixed]
        if k:
            for copy in self.copies(k - 1):
                copy.wait()
            other = self.received[k - 1]
        if k == len(self.order) and self.order[-1] == "z":
            mine = self.own()
            total = mine[...].astype(F32)
            for n in range(len(self.p.others)):
                total = total + other[n].astype(F32)
            mine[...] = total.astype(BF)
        elif k < len(self.order) and self.order[k] != "z":
            b = self.order[k]
            self.add(dict(fixed, **{b: 1 - self.p.bit[b]}), other, other_dims)
            self.copies(k)[0].start()
            self.add(dict(fixed, **{b: self.p.bit[b]}), other, other_dims)
        else:
            self.add(fixed, other, other_dims)
            if k < len(self.order):
                for copy in self.copies(k):
                    copy.start()

    def own(self):
        return self.total.at[self.where(self.p.bit)]


class ExpertSum:
    def __init__(self, place, links, j, slot, eg, own, part, received, order, out, local_sem):
        self.p, self.links, self.out = place, links, out.at[j]
        self.given = eg.at[j]
        self.mine = own.at[slot]
        self.load = pltpu.make_async_copy(self.given.at[:, :, :, :, place.bit["c"]], self.mine, local_sem.at[slot])
        self.core = links.copy(
            links.reserve(1), self.given.at[:, :, :, :, 1 - place.bit["c"]], part.at[j], place.partner["c"]
        )
        self.halving = Halving(place, links, part.at[j], "hlx", order, received, lead=(2,))

    def run(self, k):
        if k == 0:
            self.core.start()
            return
        if k == 1:
            self.load.wait()
            self.core.wait()
        self.halving.step(k - 1, self.mine)
        if k == 4:
            self.out[...] = self.halving.own()[...].astype(F32)


class SharedSum:
    def __init__(self, place, links, src, core_rx, received, order, out):
        self.p, self.links, self.order, self.out, self.core_rx = place, links, order, out, core_rx
        self.core = links.copy(links.reserve(1), src.at[1 - place.bit["c"]], core_rx, place.partner["c"])
        self.halving = Halving(place, links, src.at[place.bit["c"]], "yxhl", order, received)
        self.first = links.reserve(len(order) + 3)

    def back(self, k):
        known = "c" + self.order[: len(self.order) - k] if k <= len(self.order) else ""
        bits = known.replace("z", "hl")
        mine = self.out.at[tuple(self.p.bit[b] if b in bits else slice(None) for b in BITS)]
        if known[-1] == "z":
            return [self.links.copy(self.first + n, mine, mine, device) for n, (_, device) in enumerate(self.p.others)]
        return [self.links.copy(self.first + 2 + k, mine, mine, self.p.partner[known[-1]])]

    def run(self, k):
        n = len(self.order)
        if k == 0:
            self.core.start()
        elif k <= n:
            if k == 1:
                self.core.wait()
            self.halving.step(k - 1, self.core_rx)
        elif k == n + 1:
            self.halving.step(n)
            self.out[tuple(self.p.bit[b] for b in BITS)] = self.halving.own()[...]
            for copy in self.back(0):
                copy.start()
        else:
            for copy in self.back(k - n - 2):
                copy.wait()
            if k <= 2 * n + 1:
                for copy in self.back(k - n - 1):
                    copy.start()


class SmallSum:
    def __init__(self, place, links, src, rx):
        self.p, self.links, self.src, self.rx = place, links, src, rx
        self.first = links.reserve(len(BITS))

    def copy(self, k):
        return self.links.copy(self.first + k, self.src.at[k], self.rx.at[k], self.p.partner[BITS[k]])

    def run(self, k, out):
        if k:
            self.copy(k - 1).wait()
            total = self.src[k - 1] + self.rx[k - 1]
            if k == len(BITS):
                out[...] = total
                return
            self.src[k] = total
        self.copy(k).start()


GROUPS = ((48, "yxz"), (48, "xyz"), (48, "yxz"), (32, "yxz"), (16, "yxz"))
GROUP_ROWS = (0, 1536, 3072, 4608, 5632)
EXPERT_ORDERS = ("lhx", "xlh", "xlh", "xlh")

ORDER = (
    ("E", 3, 0), ("E", 0, 0), ("d", 0, 0), ("E", 1, 0), ("E", 2, 0), ("E", 3, 1), ("d", 1, 0), ("run", 0, 0),
    ("d", 2, 0), ("E", 0, 1), ("run", 1, 0), ("d", 3, 0), ("E", 1, 1), ("E", 2, 1), ("y", 0, 0), ("run", 2, 0),
    ("run", 3, 0), ("E", 3, 2), ("run", 4, 0), ("run", 5, 0), ("run", 6, 0), ("S", 0, 0), ("run", 7, 0),
    ("run", 8, 0), ("run", 9, 0), ("E", 0, 2), ("S", 0, 1), ("run", 10, 0), ("E", 1, 2), ("run", 11, 0),
    ("run", 12, 0), ("run", 13, 0), ("S", 1, 0), ("S", 2, 0), ("run", 14, 0), ("S", 0, 2), ("run", 15, 0),
    ("S", 2, 1), ("E", 3, 3), ("run", 16, 0), ("S", 1, 1), ("S", 0, 3), ("run", 17, 0), ("run", 18, 0), ("S", 4, 0),
    ("S", 3, 0), ("S", 2, 2), ("run", 19, 0), ("S", 4, 1), ("S", 1, 2), ("few", 0, 0), ("S", 0, 4), ("S", 3, 1),
    ("S", 2, 3), ("S", 4, 2), ("S", 0, 5), ("S", 4, 3), ("S", 1, 3), ("S", 3, 2), ("S", 2, 4), ("S", 0, 6),
    ("S", 3, 3), ("S", 1, 4), ("E", 3, 4), ("few", 1, 0), ("E", 0, 3), ("S", 3, 4), ("S", 4, 4), ("S", 2, 5),
    ("E", 2, 2), ("few", 2, 0), ("E", 1, 3), ("S", 1, 5), ("S", 3, 5), ("S", 2, 6), ("S", 4, 5), ("E", 0, 4),
    ("few", 3, 0), ("S", 1, 6), ("run", 20, 0), ("S", 3, 6), ("S", 4, 6), ("E", 2, 3), ("S", 1, 7), ("few", 4, 0),
    ("S", 2, 7), ("E", 1, 4), ("S", 3, 7), ("S", 0, 7), ("S", 1, 8), ("S", 4, 7), ("S", 3, 8), ("S", 2, 8),
    ("S", 0, 8), ("E", 2, 4), ("S", 4, 8), ("few", 5, 0),
)

LOADED = ("c", "x3", "cot", "d", "delta", "x2", "qkv", "o", "p", "wo", "wqkv", "x1", "wout", "gp", "u", "win", "y", "x0")


def bwd_kernel(linked, *refs):
    names = ["gains", "router_t", "routes", "wqkv", "wo", "win", "wout", "x0", "x1", "x2", "x3", "qkv1", "qkv2"]
    names += ["o1", "o2", "p1", "p2", "u", "gp", "c", "cot", "d", "delta", "y"]
    if linked:
        names += ["d_send", "delta_send", "y_send", "eg"]
    names += ["act_out", "gin_out", "small_out"]
    if linked:
        names += ["eg_out"] + ["out" + str(g) for g in range(len(GROUPS))]
    else:
        names += ["shared_out"]
    names += ["v_" + n for n in LOADED] + ["gv", "a_scr", "dbr_scr", "dqkv_scr", "sem"]
    if linked:
        names += ["d_rx", "delta_rx", "y_rx", "own", "part", "small_src", "small_rx", "eg_sem", "send", "recv"]
        names += ["src" + str(g) for g in range(len(GROUPS))]
        names += ["rx" + str(g) + str(k) for g, (_, order) in enumerate(GROUPS) for k in range(len(order) + 1)]
        names += ["erx" + str(j) + str(k) for j in range(len(EXPERT_ORDERS)) for k in range(3)]
    r = dict(zip(names, refs, strict=True))
    gains, gv, a_scr, dbr_scr, dqkv_scr = (r[n] for n in ("gains", "gv", "a_scr", "dbr_scr", "dqkv_scr"))
    images = gv.shape[0]
    m = images * ROWS
    lo = lane_low(ROWS)

    second = {"qkv": "qkv2", "o": "o2", "p": "p2"}
    copies = {}

    def fetch(name, source):
        copies[name] = pltpu.make_async_copy(r[source], r["v_" + name], r["sem"].at[LOADED.index(name)])
        copies[name].start()

    def need(*wanted):
        for name in wanted:
            copies[name].wait()

    if linked:
        place = Place()
        links = Links(r["send"], r["recv"])
        partners = [place.partner[b] for b in "cyx"] + [device for _, device in place.others]
        place.greet(partners)
        place.meet(partners)
        beside = place.partner["y"]
        delta_copy = links.copy(links.reserve(1), r["delta_send"], r["delta_rx"], beside)
        delta_copy.start()
        d_first = links.reserve(images)

        def d_copy(i):
            return links.copy(d_first + i, r["d_send"].at[i], r["d_rx"].at[i], beside)

        turn = [at for kind, at, what in ORDER if (kind, what) == ("E", 1)]
        experts = [
            ExpertSum(
                place, links, j, turn.index(j) % 2, r["eg"], r["own"], r["part"], [r["erx" + str(j) + str(k)] for k in range(3)],
                order, r["eg_out"], r["eg_sem"],
            )
            for j, order in enumerate(EXPERT_ORDERS)
        ]
        experts[turn[0]].load.start()
        experts[turn[1]].load.start()
        y_copy = links.copy(links.reserve(1), r["y_send"], r["y_rx"], beside)
        sums = []
        for g, (_, order) in enumerate(GROUPS):
            rx = [r["rx" + str(g) + str(k)] for k in range(len(order) + 1)]
            sums.append(SharedSum(place, links, r["src" + str(g)], rx[0], rx[1:], order, r["out" + str(g)]))
        few = SmallSum(place, links, r["small_src"], r["small_rx"])
        small = r["small_src"].at[0]
        small[...] = jnp.zeros(small.shape, F32)
    else:
        small = r["small_out"]
    for name in LOADED:
        fetch(name, second.get(name, name))

    def keep(block, value):
        value = value.astype(BF)
        if not linked:
            r["shared_out"][block] = value
            return
        row, end = block * D, block * D + D
        for g, (share, _) in enumerate(GROUPS):
            base, cell = GROUP_ROWS[g], 4 * share
            for q in range(8):
                at = base + q * cell
                if row <= at and at + cell <= end:
                    part = value[at - row : at - row + cell]
                    r["src" + str(g)][q // 4, q // 2 % 2, q % 2] = part.reshape(2, 2, share, D)

    def router():
        need("c", "delta")
        c_all = r["v_c"][...].reshape(m, D)
        g0, g1, first, other = gate_rows(r["router_t"][...], c_all, r["routes"][...])
        delta = r["v_delta"][0:1] + r["v_delta"][1:2]
        if linked:
            delta_copy.wait()
            delta = delta + (r["delta_rx"][0:1] + r["delta_rx"][1:2])
        dl = g0 * g1 * delta
        dlog = jnp.where(first, dl, jnp.where(other, -dl, 0.0)).astype(BF)
        small[4 : 4 + dlog.shape[0]] = dot(dlog, c_all)
        small[0:4] = jnp.zeros((4, D), F32)
        gv[...] = t_dot(dlog, r["router_t"][...]).reshape(images, ROWS, D)
        need("x3", "cot", "d")

    def add_gain(row, by_gain):
        small[row : row + 1] += jnp.sum(by_gain, axis=0, keepdims=True)

    def first(i):
        dc = gv[i] + r["v_d"][i].astype(F32)
        if linked:
            d_copy(i).wait()
            dc = dc + r["d_rx"][i].astype(F32)
        dx, by_gain = norm_back(dc, r["v_x3"][i], gains[3:4])
        gv[i] = r["v_cot"][i].astype(F32) + dx
        add_gain(3, by_gain)
        if i == 0:
            need("x2", "qkv", "o", "p", "wo")
        attend_image(i, 1, gains[2:3], r["v_x2"])

    def attend_image(i, layer, gain, x):
        qkv, o, p = r["v_qkv"], r["v_o"], r["v_p"]
        a_scr[i] = (norm_parts(x[i].astype(F32))[0] * gain).astype(BF)
        dbr = gv[i].astype(BF)
        dbr_scr[i] = dbr
        do = dot_t(dbr, r["v_wo"][layer]).astype(BF)
        dod = do.astype(F32) * o[i].astype(F32)
        for pair in range(HEADS // 2):
            at = 128 * pair
            q = qkv[i, :, at : at + 128] * BF(0.125)
            k = qkv[i, :, D + at : D + at + 128]
            w = qkv[i, :, 2 * D + at : 2 * D + at + 128]
            dqs, dk, dw = [], 0.0, 0.0
            for h in range(2):
                mask = lo if h == 0 else ~lo
                dom = jnp.where(mask, do[:, at : at + 128], BF(0))
                inner = jnp.sum(jnp.where(mask, dod[:, at : at + 128], 0.0), axis=-1, keepdims=True)
                ph = p[i, 2 * pair + h]
                ds = (ph.astype(F32) * (dot_t(dom, w) - inner)).astype(BF)
                dw = dw + t_dot(ph, dom)
                dqs.append(dot(ds, k))
                dk = dk + t_dot(ds, jnp.where(mask, q, BF(0)))
            dqkv_scr[i, :, at : at + 128] = (jnp.where(lo, dqs[0], dqs[1]) * 0.125).astype(BF)
            dqkv_scr[i, :, D + at : D + at + 128] = dk.astype(BF)
            dqkv_scr[i, :, 2 * D + at : 2 * D + at + 128] = dw.astype(BF)

    def attend_weights(block):
        a_all = a_scr[...].reshape(m, D)
        for f in range(3):
            keep(block + f, t_dot(a_all, dqkv_scr[:, :, f * D : f * D + D].reshape(m, D)))
        keep(block + 3, t_dot(r["v_o"][...].reshape(m, D), dbr_scr[...].reshape(m, D)))

    def close(x, layer, row, out):
        def image(i, _):
            da = dot_t(dqkv_scr[i], r["v_wqkv"][layer])
            dx, by_gain = norm_back(da, x[i].astype(F32), gains[row : row + 1])
            out[i] = gv[i] + dx
            add_gain(row, by_gain)
            return 0

        lax.fori_loop(0, images, image, 0)

    def first_close():
        for name in ("qkv", "o", "p"):
            fetch(name, name + "1")
        need("wqkv")
        close(r["v_x2"], 1, 2, gv)
        need("x1", "wout", "gp", "u", "win")

    gp = r["v_gp"]

    def mlp(i):
        a_scr[i] = (norm_parts(r["v_x1"][i])[0] * gains[1:2]).astype(BF)
        dm = gv[i].astype(BF)
        dbr_scr[i] = dm
        for f in range(0, FF, 512):
            du = dot_t(dm, r["v_wout"][f : f + 512])
            gp[i, :, f : f + 512] = (du * gp[i, :, f : f + 512].astype(F32)).astype(BF)

    def mlp_out_weights():
        dm_all = dbr_scr[...].reshape(m, D)
        for f in range(4):
            keep(4 + f, t_dot(r["v_u"][:, :, f * D : f * D + D].reshape(m, D), dm_all))

    def mlp_in_weights():
        b_all = a_scr[...].reshape(m, D)
        for f in range(4):
            keep(8 + f, t_dot(b_all, gp[:, :, f * D : f * D + D].reshape(m, D)))

    def mlp_close():
        def image(i, _):
            db = dot_t(gp[i], r["v_win"][...])
            dx, by_gain = norm_back(db, r["v_x1"][i], gains[1:2])
            gv[i] = gv[i] + dx
            add_gain(1, by_gain)
            return 0

        lax.fori_loop(0, images, image, 0)
        need("x0", "qkv", "o", "p")

    def last(i):
        attend_image(i, 0, gains[0:1], r["v_x0"])

    def last_close():
        close(r["v_x0"], 0, 0, r["gin_out"])

    def act():
        need("y")
        if linked:
            y_copy.wait()
        for i in range(images):
            x4 = r["v_x3"][i] + r["v_y"][i].astype(F32)
            if linked:
                x4 = x4 + r["y_rx"][i].astype(F32)
            r["act_out"][i] = x4.astype(BF)

    compute = [router] + [functools.partial(first, i) for i in range(images)]
    compute += [lambda: attend_weights(0), first_close] + [functools.partial(mlp, i) for i in range(images)]
    compute += [mlp_out_weights, mlp_in_weights, mlp_close] + [functools.partial(last, i) for i in range(images)]
    compute += [lambda: attend_weights(12), last_close, act]
    if not linked:
        for step in compute:
            step()
        return
    done = 0
    for kind, at, what in ORDER:
        if kind == "run":
            compute[done]()
            done += 1
        elif kind == "d":
            d_copy(at).start()
        elif kind == "y":
            y_copy.start()
        elif kind == "few":
            few.run(at, r["small_out"])
        elif kind == "E":
            experts[at].run(what)
            if what == 1 and turn.index(at) + 2 < len(turn):
                experts[turn[turn.index(at) + 2]].load.start()
        else:
            sums[at].run(what)


def dense_backward(weights, router_t, routes, saved, cot, d, delta, y, sent=None):
    gains, wqkv, wo, win, wout = weights
    x0, x1, x2, x3, qkv1, qkv2, o1, o2, p1, p2, u, gp, c = saved
    images = x0.shape[0]
    linked = sent is not None
    small_rows = 16 if linked else 4 + router_t.shape[0]
    ins = [gains, router_t, routes, wqkv, wo, win, wout, *saved, cot, d, delta, y] + (list(sent) if linked else [])
    outs = [
        jax.ShapeDtypeStruct((images, ROWS, D), BF),
        jax.ShapeDtypeStruct((images, ROWS, D), F32),
        jax.ShapeDtypeStruct((small_rows, D), F32),
    ]
    if not linked:
        outs.append(jax.ShapeDtypeStruct((16, D, D), BF))
    vm = pltpu.VMEM
    loaded = dict(
        c=c, x3=x3, cot=cot, d=d, delta=delta, x2=x2, qkv=qkv1, o=o1, p=p1, wo=wo, wqkv=wqkv, x1=x1, wout=wout,
        gp=gp, u=u, win=win, y=y, x0=x0,
    )
    scratch = [vm(loaded[name].shape, loaded[name].dtype) for name in LOADED]
    scratch += [vm((images, ROWS, D), F32), vm((images, ROWS, D), BF), vm((images, ROWS, D), BF)]
    scratch += [vm((images, ROWS, 3 * D), BF), pltpu.SemaphoreType.DMA((len(LOADED),))]
    params = dict(vmem_limit_bytes=62 << 20)
    if linked:
        eg = sent[-1]
        local, share = eg.shape[0], eg.shape[-2]
        outs.append(jax.ShapeDtypeStruct((local, 2, share, D), F32))
        outs += [jax.ShapeDtypeStruct((2,) * 5 + (rows, D), BF) for rows, _ in GROUPS]
        copies = 2 + images + 4 * local + 15 * len(GROUPS) + len(BITS)
        scratch += [vm(d.shape, BF), vm(delta.shape, F32), vm(y.shape, BF)]
        scratch += [
            vm((2, 2, 2, 2, 2, share, D), BF),
            vm((local, 2, 2, 2, 2, share, D), BF),
            vm((len(BITS), small_rows, D), F32),
            vm((len(BITS), small_rows, D), F32),
            pltpu.SemaphoreType.DMA((2,)),
            pltpu.SemaphoreType.DMA((copies,)),
            pltpu.SemaphoreType.DMA((copies,)),
        ]
        scratch += [vm((2,) * 5 + (rows, D), BF) for rows, _ in GROUPS]
        for rows, order in GROUPS:
            scratch += [vm((2,) * (4 - k) + (rows, D), BF) for k in range(len(order.strip("z")) + 1)]
            if "z" in order:
                scratch.append(vm((3, rows, D), BF))
        scratch += [vm((2,) * (3 - k) + (share, D), BF) for _ in EXPERT_ORDERS for k in range(3)]
        params.update(collective_id=1, has_side_effects=True)
    return pl.pallas_call(
        functools.partial(bwd_kernel, linked),
        out_shape=outs,
        in_specs=[VMEM] * 3 + [pl.BlockSpec(memory_space=pl.ANY)] * (len(ins) - 3),
        out_specs=[VMEM] * len(outs),
        scratch_shapes=scratch,
        compiler_params=pltpu.CompilerParams(**params),
        name="dense_backward",
    )(*ins)


def finish_kernel(n_shared, act, gin, small, eg, *refs):
    shared, refs = refs[:n_shared], refs[n_shared:]
    act_out, gin_out, qkv_out, proj_out, gain_out, mlp_in_out, mlp_out_out, router_out, in_out, out_out = refs[:10]
    v_shared, v_wide, v_gin, v_act, in_sem, out_sem = refs[10:]
    images = act.shape[0]
    blocks = v_wide.shape[0]
    targets = {3: proj_out.at[1], 15: proj_out.at[0]}
    for f in range(3):
        targets[f] = qkv_out.at[1, :, pl.ds(f * D, D)]
        targets[12 + f] = qkv_out.at[0, :, pl.ds(f * D, D)]
    for f in range(4):
        targets[4 + f] = mlp_out_out.at[pl.ds(f * D, D)]
        targets[8 + f] = mlp_in_out.at[:, pl.ds(f * D, D)]
    loads, at = [], 0
    for k, part in enumerate(shared):
        rows = part.shape[0]
        loads.append((at, pltpu.make_async_copy(part, v_shared.at[pl.ds(at, rows)], in_sem.at[k])))
        at += rows
    load_gin = pltpu.make_async_copy(gin, v_gin, in_sem.at[n_shared])
    load_act = pltpu.make_async_copy(act, v_act, in_sem.at[n_shared + 1])
    for _, load in loads:
        load.start()
    load_gin.start()
    load_act.start()

    def store(b):
        return pltpu.make_async_copy(v_wide.at[b], targets[b], out_sem.at[b])

    waited = 0
    for b in range(blocks):
        while waited < n_shared and loads[waited][0] < (b + 1) * D:
            loads[waited][1].wait()
            waited += 1
        v_wide[b] = v_shared[b * D : (b + 1) * D].astype(F32)
        store(b).start()
    gain_out[...] = small[0:4]
    router_out[...] = small[4 : 4 + router_out.shape[0]]
    for e in range(eg.shape[0]):
        in_out[e] = eg[e, 0]
        out_out[e] = eg[e, 1]
    load_gin.wait()
    load_act.wait()
    for i in range(images):
        gin_out[i * PATCHES : (i + 1) * PATCHES] = v_act[i, 0:PATCHES].astype(F32)
    act_out[...] = gin_out[...].astype(BF)
    for i in range(images):
        gin_out[i * PATCHES : (i + 1) * PATCHES] = v_gin[i, 0:PATCHES]
    for b in range(blocks):
        store(b).wait()


def finish(act, gin, shared, small, eg, experts):
    images, local, share = act.shape[0], eg.shape[0], eg.shape[2]
    row_count = images * PATCHES
    blocks = 16
    outs = [
        jax.ShapeDtypeStruct((row_count, D), BF),
        jax.ShapeDtypeStruct((row_count, D), F32),
        jax.ShapeDtypeStruct((2, D, 3 * D), F32),
        jax.ShapeDtypeStruct((2, D, D), F32),
        jax.ShapeDtypeStruct((4, D), F32),
        jax.ShapeDtypeStruct((D, FF), F32),
        jax.ShapeDtypeStruct((FF, D), F32),
        jax.ShapeDtypeStruct((experts, D), F32),
        jax.ShapeDtypeStruct((local, share, D), F32),
        jax.ShapeDtypeStruct((local, share, D), F32),
    ]
    far = pl.BlockSpec(memory_space=pl.ANY)
    return pl.pallas_call(
        functools.partial(finish_kernel, len(shared)),
        out_shape=outs,
        in_specs=[far, far, VMEM, VMEM] + [far] * len(shared),
        out_specs=[VMEM, VMEM, far, far, VMEM, far, far, VMEM, VMEM, VMEM],
        scratch_shapes=[
            pltpu.VMEM((blocks * D, D), BF),
            pltpu.VMEM((blocks, D, D), F32),
            pltpu.VMEM(gin.shape, F32),
            pltpu.VMEM(act.shape, BF),
            pltpu.SemaphoreType.DMA((len(shared) + 2,)),
            pltpu.SemaphoreType.DMA((blocks,)),
        ],
        compiler_params=pltpu.CompilerParams(vmem_limit_bytes=62 << 20),
        name="finish",
    )(act, gin, small, eg, *shared)


def from_peer(array, groups, shift):
    return lax.ppermute(array, "exp", [(i, (i + shift) % groups) for i in range(groups)])


def shards(
    tokens, routes, norm_gains, attn_qkv, attn_out, mlp_in, mlp_out, router, experts_in, experts_out, cotangent
):
    row_count = tokens.shape[0]
    groups = lax.axis_size("exp")
    local = experts_in.shape[0]
    choices = routes.shape[1]
    capacity = 2 * choices * row_count // (local * groups)
    images = row_count // PATCHES
    router_t = router.T
    rep = lax.axis_size("rep")
    known = (rep, groups, local) == (16, 2, 4)
    owners = (2, 2, 2, 2) if known else (rep,)
    routes_t, x0, cot, x1, x2, x3, qkv1, qkv2, o1, o2, p1, p2, u, gp, c, *received = dense_forward(
        tokens, cotangent, routes.T, norm_gains, attn_qkv, attn_out, mlp_in, mlp_out, known
    )

    def of_all(mine, place):
        if known:
            others = [received[place]]
        else:
            others = [from_peer(mine, groups, k) for k in range(1, groups)]
        return [part.reshape(-1, part.shape[-1]) for part in [mine] + others]

    cs, gs, rs = of_all(c, 0), of_all(cot, 1), of_all(routes_t, 2)
    eg, ys, ds, deltas = experts_all(
        cs, gs, rs, router_t, experts_in, experts_out, local * capacity * groups, owners
    )

    weights = (norm_gains, attn_qkv, attn_out, mlp_in, mlp_out)
    saved = (x0, x1, x2, x3, qkv1, qkv2, o1, o2, p1, p2, u, gp, c)
    by_image = (images, ROWS, D)
    experts = router_t.shape[0]
    if known:
        sent = (ds[1].reshape(by_image), deltas[1], ys[1].reshape(by_image), eg)
        act, gin, small, eg, *shared = dense_backward(
            weights, router_t, routes_t, saved, cot, ds[0].reshape(by_image), deltas[0], ys[0].reshape(by_image), sent
        )
        shared = [part.reshape(-1, D) for part in shared]
    else:

        def back(parts):
            total = parts[0].astype(F32)
            for k in range(1, groups):
                total = total + from_peer(parts[k], groups, groups - k).astype(F32)
            return total

        d, delta, y = back(ds).astype(BF), back(deltas), back(ys).astype(BF)
        act, gin, small, shared = dense_backward(
            weights, router_t, routes_t, saved, cot, d.reshape(by_image), delta, y.reshape(by_image)
        )
        eg = lax.psum_scatter(eg, "rep", scatter_dimension=2, tiled=True).reshape(local, 2, FF // rep, D).astype(F32)
        shared, small = lax.psum((shared, small), ("rep", "exp"))
        shared = [shared.reshape(-1, D)]
    outs = list(finish(act, gin, shared, small, eg, experts))
    outs[7] = outs[7].T
    outs[8] = jnp.swapaxes(outs[8], 1, 2)
    return tuple(outs)


def solution(mesh):
    rows = P(("rep", "exp"), None)
    return jax.shard_map(
        shards,
        mesh=mesh,
        in_specs=(rows, rows, P(), P(), P(), P(), P(), P(), P("exp", None, None), P("exp", None, None), rows),
        out_specs=(rows, rows, P(), P(), P(), P(), P(), P(), P("exp", None, "rep"), P("exp", "rep", None)),
        check_vma=False,
    )
```

```python
import functools
import math

import jax
import jax.numpy as jnp
from jax import lax
from jax.experimental import pallas as pl
from jax.experimental.pallas import tpu as pltpu
from jax.sharding import PartitionSpec as P

F32 = jnp.float32
BF = jnp.bfloat16
HEADS = 6
PATCHES = 197
ROWS = 208
EPS = 1e-6
TILE = 256
D = 384
FF = 1536
IMAGES_AT_ONCE = 1
VMEM = pl.BlockSpec(memory_space=pltpu.VMEM)


def dot(a, b):
    return lax.dot_general(a, b, (((1,), (0,)), ((), ())), preferred_element_type=F32)


def dot_t(a, b):
    return lax.dot_general(a, b, (((1,), (1,)), ((), ())), preferred_element_type=F32)


def t_dot(a, b):
    return lax.dot_general(a, b, (((0,), (0,)), ((), ())), preferred_element_type=F32)


def norm_parts(x):
    centred = x - jnp.mean(x, axis=-1, keepdims=True)
    rstd = lax.rsqrt(jnp.mean(centred * centred, axis=-1, keepdims=True) + EPS)
    return centred * rstd, rstd


def norm_back(grad, x, gain):
    xh, rstd = norm_parts(x)
    dxh = grad * gain
    inner = dxh - jnp.mean(dxh, axis=-1, keepdims=True)
    return rstd * (inner - xh * jnp.mean(dxh * xh, axis=-1, keepdims=True)), grad * xh


def gelu_parts(h):
    phi = 0.5 + 0.5 * lax.erf(0.7071067811865476 * h)
    e = jnp.exp2(h * h * -0.7213475204444817)
    return h * phi, phi + h * (0.3989422804014327 * e)


def lane_low(rows):
    return lax.broadcasted_iota(jnp.int32, (rows, 128), 1) < 64


MESH = pl.DeviceIdType.MESH
BITS = "cyxhl"


class Place:
    def __init__(self):
        r = lax.axis_index("rep")
        y = lax.axis_index("exp")
        self.bit = {"c": r % 2, "y": y, "x": (r // 2) % 2, "h": r // 8, "l": (r // 4) % 2}
        stride = {"c": 1, "x": 2, "l": 4, "h": 8}
        self.partner = {b: (r + stride[b] * (1 - 2 * self.bit[b]), y) for b in stride}
        self.partner["y"] = (r, 1 - y)
        self.others = []
        for k in range(1, 4):
            z = (r // 4 + k) % 4
            self.others.append(({"h": z // 2, "l": z % 2}, (z * 4 + r % 4, y)))

    def greet(self, partners):
        for partner in partners:
            pl.semaphore_signal(pltpu.get_barrier_semaphore(), inc=1, device_id=partner, device_id_type=MESH)

    def meet(self, partners):
        pl.semaphore_wait(pltpu.get_barrier_semaphore(), len(partners))


class Links:
    def __init__(self, send, recv):
        self.send, self.recv, self.used = send, recv, 0

    def reserve(self, count):
        first = self.used
        self.used += count
        return first

    def copy(self, at, src, dst, device):
        return pltpu.make_async_remote_copy(
            src_ref=src, dst_ref=dst, send_sem=self.send.at[at], recv_sem=self.recv.at[at],
            device_id=device, device_id_type=MESH,
        )

    def start(self, at, src, dst, device):
        copy = self.copy(at, src, dst, device)
        copy.start()
        return copy


def fwd_kernel(linked, *refs):
    weights = ["wqkv", "wo", "win", "wout"]
    names = ["tokens", "cot", "routes", "gains"] + ["far_" + name for name in weights]
    names += ["routes_out", "x0", "cot_out", "x1", "x2", "x3", "qkv1", "qkv2", "o1", "o2", "p1", "p2", "u", "gp", "c"]
    if linked:
        names += ["c_rx", "cot_rx", "routes_rx"]
    names += ["wide"] + weights + ["sem"]
    if linked:
        names += ["c_scr", "send", "recv"]
    r = dict(zip(names, refs, strict=True))
    gains = r["gains"]
    ib = r["x1"].shape[0]
    m = ib * ROWS
    images = r["x0"].shape[0]
    step = pl.program_id(0)
    lo = lane_low(ROWS)
    valid = lax.broadcasted_iota(jnp.int32, (ROWS, ROWS), 1) < PATCHES
    real = lax.broadcasted_iota(jnp.int32, (ROWS, D), 0) < PATCHES
    if linked:
        place = Place()
        links = Links(r["send"], r["recv"])

        def exchange(at, src, dst):
            return links.copy(at, src, dst, place.partner["y"])

        early = [exchange(0, r["cot_out"], r["cot_rx"]), exchange(1, r["routes_out"], r["routes_rx"])]

        def c_copy(image):
            return exchange(2 + image, r["c_scr"].at[image], r["c_rx"].at[image])

    @pl.when(step == 0)
    def _():
        if linked:
            place.greet([place.partner["y"]])
        loads = [pltpu.make_async_copy(r["far_" + w], r[w], r["sem"].at[k]) for k, w in enumerate(weights)]
        for load in loads:
            load.start()
        wide = r["wide"]
        slots = r["routes_out"]
        slots[...] = jnp.full(slots.shape, -1, jnp.int32)
        for i in range(images):
            slots[0:2, i * ROWS : i * ROWS + PATCHES] = r["routes"][:, i * PATCHES : (i + 1) * PATCHES]
        for source, target in (("cot", "cot_out"), ("tokens", "x0")):
            wide[0 : images * PATCHES] = r[source][...].astype(F32)
            for i in range(images):
                rows = wide[i * PATCHES : i * PATCHES + ROWS]
                r[target][i] = jnp.where(real, rows, 0.0).astype(BF)
            if linked and source == "cot":
                place.meet([place.partner["y"]])
                for copy in early:
                    copy.start()
        for load in loads:
            load.wait()

    def attend_image(i, qkv_ref, o_ref, p_ref):
        for pair in range(HEADS // 2):
            at = 128 * pair
            q = qkv_ref[i, :, at : at + 128] * BF(0.125)
            k = qkv_ref[i, :, D + at : D + at + 128]
            w = qkv_ref[i, :, 2 * D + at : 2 * D + at + 128]
            mixed = []
            for h in range(2):
                qm = jnp.where(lo if h == 0 else ~lo, q, BF(0))
                s = jnp.where(valid, dot_t(qm, k), -1e30)
                s = jnp.exp(s - jnp.max(s, axis=-1, keepdims=True))
                p = (s * (1.0 / jnp.sum(s, axis=-1, keepdims=True))).astype(BF)
                p_ref[i, 2 * pair + h] = p
                mixed.append(dot(p, w))
            o_ref[i, :, at : at + 128] = jnp.where(lo, mixed[0], mixed[1]).astype(BF)

    def project(x, layer, gain, qkv_ref):
        a = (norm_parts(x)[0] * gain).astype(BF)
        qkv_ref[...] = dot(a, r["wqkv"][layer]).astype(BF).reshape(ib, ROWS, 3 * D)

    x0 = r["x0"][pl.ds(step * ib, ib)].astype(F32).reshape(m, D)
    project(x0, 0, gains[0:1], r["qkv1"])
    for i in range(ib):
        attend_image(i, r["qkv1"], r["o1"], r["p1"])
    x1 = x0 + dot(r["o1"][...].reshape(m, D), r["wo"][0])
    r["x1"][...] = x1.reshape(ib, ROWS, D)
    b = (norm_parts(x1)[0] * gains[1:2]).astype(BF)
    x2 = x1
    for f in range(0, FF, 512):
        u, gp = gelu_parts(dot(b, r["win"][:, f : f + 512]))
        u = u.astype(BF)
        r["u"][:, :, f : f + 512] = u.reshape(ib, ROWS, 512)
        r["gp"][:, :, f : f + 512] = gp.astype(BF).reshape(ib, ROWS, 512)
        x2 = x2 + dot(u, r["wout"][f : f + 512])
    r["x2"][...] = x2.reshape(ib, ROWS, D)
    project(x2, 1, gains[2:3], r["qkv2"])

    def last(i, _):
        attend_image(i, r["qkv2"], r["o2"], r["p2"])
        x3 = r["x2"][i] + dot(r["o2"][i], r["wo"][1])
        r["x3"][i] = x3
        c = (norm_parts(x3)[0] * gains[3:4]).astype(BF)
        r["c"][i] = c
        if linked:
            r["c_scr"][step * ib + i] = c
            c_copy(step * ib + i).start()
        return 0

    lax.fori_loop(0, ib, last, 0)

    if linked:

        @pl.when(step == pl.num_programs(0) - 1)
        def _():
            for copy in early + [c_copy(i) for i in range(images)]:
                copy.wait()


def dense_forward(tokens, cot, routes, gains, wqkv, wo, win, wout, linked):
    n = tokens.shape[0] // PATCHES
    ib = IMAGES_AT_ONCE if n % IMAGES_AT_ONCE == 0 else 1

    def out(*shape, dtype=BF):
        return jax.ShapeDtypeStruct((n,) + shape, dtype)

    def block(shape):
        return pl.BlockSpec((ib,) + tuple(shape[1:]), lambda i: (i,) + (0,) * (len(shape) - 1))

    whole = pl.BlockSpec((n, ROWS, D), lambda i: (0, 0, 0))
    routes_shape = jax.ShapeDtypeStruct((8, n * ROWS), jnp.int32)
    outs = [routes_shape] + [out(ROWS, D)] * 2 + [out(ROWS, D, dtype=F32)] * 3 + [out(ROWS, 3 * D)] * 2 + [out(ROWS, D)] * 2
    outs += [out(HEADS, ROWS, ROWS)] * 2 + [out(ROWS, FF)] * 2 + [out(ROWS, D)]
    out_specs = [pl.BlockSpec(routes_shape.shape, lambda i: (0, 0)), whole, whole] + [block(o.shape) for o in outs[3:]]
    scratch = [pltpu.VMEM(((n - 1) * PATCHES + ROWS, D), F32)]
    scratch += [pltpu.VMEM(w.shape, BF) for w in (wqkv, wo, win, wout)] + [pltpu.SemaphoreType.DMA((4,))]
    params = dict(vmem_limit_bytes=62 << 20)
    if linked:
        outs += [out(ROWS, D)] * 2 + [routes_shape]
        out_specs += [pl.BlockSpec(memory_space=pl.ANY)] * 3
        copies = pltpu.SemaphoreType.DMA((2 + n,))
        scratch += [pltpu.VMEM((n, ROWS, D), BF), copies, copies]
        params.update(collective_id=2, has_side_effects=True)
    return pl.pallas_call(
        functools.partial(fwd_kernel, linked),
        grid=(n // ib,),
        out_shape=outs,
        in_specs=[VMEM] * 4 + [pl.BlockSpec(memory_space=pl.ANY)] * 4,
        out_specs=out_specs,
        scratch_shapes=scratch,
        compiler_params=pltpu.CompilerParams(**params),
        name="dense_forward",
    )(tokens, cot, routes, gains, wqkv, wo, win, wout)


def gate_rows(router_t, c, routes):
    logits = dot_t(router_t, c)
    expert = lax.broadcasted_iota(jnp.int32, logits.shape, 0)
    first, second = expert == routes[0:1], expert == routes[1:2]
    diff = jnp.sum(jnp.where(first, logits, 0.0) - jnp.where(second, logits, 0.0), axis=0, keepdims=True)
    return 1.0 / (1.0 + jnp.exp(-diff)), 1.0 / (1.0 + jnp.exp(diff)), first, second


def experts_kernel(groups, local, exp_axis, *refs):
    c_refs, g_refs, r_refs = refs[:groups], refs[groups : 2 * groups], refs[2 * groups : 3 * groups]
    router_t, win, wout = refs[3 * groups : 3 * groups + 3]
    outs = refs[3 * groups + 3 :]
    eg_ref, y_refs, d_refs, delta_refs = outs[0], outs[1 : groups + 1], outs[groups + 1 : 2 * groups + 1], outs[2 * groups + 1 : 3 * groups + 1]
    ci, cols, place, xg, slots, dy_scr, u_scr, gp_scr, stack, back, staged, count_v, count, plan, sem, load_sem, out_sem = outs[3 * groups + 1 :]
    n_tok = c_refs[0].shape[0]
    total = groups * n_tok
    images = total // ROWS
    step = pl.program_id(0)
    first_expert = lax.axis_index(exp_axis) * local

    def window(e, i):
        begin = plan[e * (images + 1) + i]
        return begin, pl.multiple_of(begin // 16 * 16, 16)

    def windows(i):
        most = jnp.int32(1)
        for e in range(local):
            at = window(e, i)[1]
            most = jnp.maximum(most, (plan[e * (images + 1) + i + 1] - at + 127) // 128)
        return most

    @pl.when(step == 0)
    def _():
        loads = []
        for k, (sources, first) in enumerate(((c_refs, 0), (g_refs, D + 128))):
            for s in range(groups):
                target = ci.at[pl.ds(s * n_tok, n_tok), pl.ds(first, D)]
                loads.append(pltpu.make_async_copy(sources[s], target, load_sem.at[k * groups + s]))
                loads[-1].start()
        for load in loads:
            load.wait()
        routes = jnp.concatenate([r[0:2] for r in r_refs], axis=1)
        g0, g1, _, _ = gate_rows(router_t[...], ci[:, 0:D], routes)
        expert_row = lax.broadcasted_iota(jnp.int32, (8, total), 0)
        mine, inside = first_expert + expert_row, expert_row < local
        is0, is1 = (mine == routes[0:1]) & inside, (mine == routes[1:2]) & inside
        member = jnp.where(is0 | is1, 1.0, 0.0)
        lane = lax.broadcasted_iota(jnp.int32, (8, total), 1)
        of_image = lax.broadcasted_iota(jnp.int32, (total, 128), 0) // ROWS
        of_image = jnp.where(of_image == lax.broadcasted_iota(jnp.int32, (total, 128), 1), 1.0, 0.0)
        count_v[...] = dot(member.astype(BF), of_image.astype(BF)).astype(jnp.int32)
        to_scalars = pltpu.make_async_copy(count_v, count, sem)
        to_scalars.start()
        upto = member
        shift = 1
        while shift < total:
            upto = upto + jnp.where(lane >= shift, pltpu.roll(upto, shift, 1), 0.0)
            shift *= 2
        to_scalars.wait()
        begin = jnp.int32(0)
        starts = []
        for e in range(local):
            starts.append(begin.astype(F32))
            plan[local * (images + 1) + 2 * e] = begin
            first = begin
            for i in range(images):
                plan[e * (images + 1) + i] = begin
                begin = begin + count[e, i]
            plan[e * (images + 1) + images] = begin
            plan[local * (images + 1) + 2 * e + 1] = begin - first
            begin = first + (begin - first + 127) // 128 * 128 + 256
        start = jnp.zeros((8, total), F32)
        for e in range(local):
            start = jnp.where(expert_row == e, starts[e], start)
        slot = start + jnp.where(member > 0, upto, 0.0)
        slot0 = jnp.sum(jnp.where(is0, slot, 0.0), axis=0, keepdims=True) - 1.0
        slot1 = jnp.sum(jnp.where(is1, slot, 0.0), axis=0, keepdims=True) - 1.0
        slot = jnp.where(member > 0, slot - 1.0, -1.0)
        for i in range(images):
            place[i] = slot[:, i * ROWS : (i + 1) * ROWS]
        gates = jnp.where(is0, g0, jnp.where(is1, g1, 0.0))
        sign = jnp.where(is0, 1.0, jnp.where(is1, -1.0, 0.0))
        slot_rows = jnp.where(expert_row == 0, slot0, jnp.where(expert_row == 1, slot1, 0.0))
        stacked = jnp.concatenate([gates, sign, slot_rows, jnp.zeros((104, total), F32)], axis=0)
        lane128 = lax.broadcasted_iota(jnp.int32, (128, 128), 1)
        for at in range(0, total, 128):
            col = stacked[:, at : at + 128].T
            cols[at : at + 128] = col
            low = col - col.astype(BF).astype(F32)
            info = jnp.where(lane128 < 16, col, jnp.where(lane128 < 24, pltpu.roll(low, 16, 1), 0.0))
            ci[at : at + 128, D : D + 128] = info.astype(BF)

        row = lax.broadcasted_iota(jnp.int32, (128, ROWS), 0)
        head = lax.broadcasted_iota(jnp.int32, (16, 2 * D + 128), 0)

        def gather(i, _):
            rows = ci[pl.ds(pl.multiple_of(i * ROWS, 16), ROWS)]

            def part(w, _):
                picks = []
                for e in range(local):
                    at = window(e, i)[1] + 128 * w
                    picks.append(jnp.where(place[i, e : e + 1] == (at + row).astype(F32), 1.0, 0.0).astype(BF))
                found = dot(jnp.concatenate(picks, axis=0), rows).astype(BF)
                for e in range(local):
                    begin, at = window(e, i)
                    at = pl.multiple_of(at + 128 * w, 16)
                    old = xg[pl.ds(at, 16)]
                    new = found[e * 128 : e * 128 + 16]
                    xg[pl.ds(at, 16)] = jnp.where(at + head < begin, old, new)
                    xg[pl.ds(pl.multiple_of(at + 16, 16), 112)] = found[e * 128 + 16 : e * 128 + 128]
                return 0

            return lax.fori_loop(0, windows(i), part, 0)

        lax.fori_loop(0, images, gather, 0)
        for e in range(local):
            end, at = window(e, images)
            xg[pl.ds(at, 16)] = jnp.where(at + head < end, xg[pl.ds(at, 16)], jnp.zeros(head.shape, BF))
            xg[pl.ds(pl.multiple_of(at + 16, 16), 240)] = jnp.zeros((240, 2 * D + 128), BF)

    begin, n = plan[local * (images + 1) + 2 * step], plan[local * (images + 1) + 2 * step + 1]

    def tile(row, size):
        at = pl.multiple_of(begin + row, 16)
        here = pl.ds(pl.multiple_of(row, TILE // 4), size)
        lane = lax.broadcasted_iota(jnp.int32, (size, 128), 1)
        x = xg[pl.ds(at, size), 0:D]
        info = xg[pl.ds(at, size), D : D + 128].astype(F32)
        g4r = xg[pl.ds(at, size), D + 128 :].astype(F32)
        gate = jnp.sum(jnp.where((lane == step) | (lane == step + 16), info, 0.0), axis=-1, keepdims=True)
        sign = jnp.sum(jnp.where(lane == step + 8, info, 0.0), axis=-1, keepdims=True)
        dy = (gate * g4r).astype(BF)
        dy_scr[here] = dy
        for f in range(0, FF, 512):
            u, gp = gelu_parts(dot(x, win[0, :, f : f + 512]))
            u_scr[here, f : f + 512] = u.astype(BF)
            gp_scr[here, f : f + 512] = gp.astype(BF)
        ey = dot(u_scr[here], wout[0]).astype(BF).astype(F32)
        dg = sign * jnp.sum(g4r * ey, axis=-1, keepdims=True)
        for f in range(0, FF, 512):
            du = dot_t(dy, wout[0, f : f + 512])
            gp_scr[here, f : f + 512] = (du * gp_scr[here, f : f + 512].astype(F32)).astype(BF)
        dcp = dot_t(gp_scr[here], win[0])
        slots[pl.ds(at, size), 0:D] = (gate * ey).astype(BF)
        slots[pl.ds(at, size), D : 2 * D] = dcp.astype(BF)
        low = dg - dg.astype(BF).astype(F32)
        slots[pl.ds(at, size), 2 * D :] = jnp.where(lane == 0, dg, jnp.where(lane == 1, low, 0.0)).astype(BF)

    whole = (n + TILE // 4 - 1) // TILE

    def full_tile(j, _):
        tile(j * TILE, TILE)
        return 0

    lax.fori_loop(0, whole, full_tile, 0)

    for size in range(TILE // 4, TILE, TILE // 4):

        @pl.when((n > whole * TILE + size - TILE // 4) & (n <= whole * TILE + size))
        def _(size=size):
            tile(whole * TILE, size)
            rest = pl.ds(pl.multiple_of(whole * TILE + size, TILE // 4), TILE - size)
            for scratch in (dy_scr, u_scr, gp_scr):
                scratch[rest] = jnp.zeros((TILE - size,) + scratch.shape[1:], BF)

    after = pl.multiple_of(begin + (n + TILE // 4 - 1) // (TILE // 4) * (TILE // 4), 16)
    slots[pl.ds(after, 256)] = jnp.zeros((256, 2 * D + 128), BF)

    rounded = (n + TILE - 1) // TILE

    @pl.when(rounded == 0)
    def _():
        eg_ref[...] = jnp.zeros_like(eg_ref)

    for tiles in range(1, u_scr.shape[0] // TILE + 1):

        @pl.when(rounded == tiles)
        def _(depth=tiles * TILE):
            x = xg[pl.ds(pl.multiple_of(begin, 16), depth), 0:D]
            dy = dy_scr[0:depth]
            for f in range(0, FF, D):
                eg_ref[0, 0, f : f + D] = t_dot(gp_scr[0:depth, f : f + D], x).astype(BF)
                eg_ref[0, 1, f : f + D] = t_dot(u_scr[0:depth, f : f + D], dy).astype(BF)

    @pl.when(step == local - 1)
    def _():
        lane = lax.broadcasted_iota(jnp.int32, (ROWS, 128), 1)

        def out_copies(s, i, slot):
            rows = pl.ds(pl.multiple_of(i * ROWS, 16), ROWS)
            return [
                pltpu.make_async_copy(staged.at[slot, k], target.at[rows], out_sem.at[slot, k])
                for k, target in enumerate((y_refs[s], d_refs[s]))
            ]

        def restore(s, i):
            image = s * (n_tok // ROWS) + i
            at_rows = pl.multiple_of(image * ROWS, 16)
            slot0, slot1 = cols[pl.ds(at_rows, ROWS), 16:17], cols[pl.ds(at_rows, ROWS), 17:18]

            def part(w):
                picks = []
                for e in range(local):
                    at = pl.multiple_of(window(e, image)[1] + 128 * w, 16)
                    stack[e * 128 : (e + 1) * 128] = slots[pl.ds(at, 128)]
                    slot = (at + lane).astype(F32)
                    picks.append(jnp.where((slot0 == slot) | (slot1 == slot), 1.0, 0.0).astype(BF))
                return dot(jnp.concatenate(picks, axis=1), stack[...])

            back[...] = part(0)

            def more(w, _):
                back[...] += part(w)
                return 0

            lax.fori_loop(1, windows(image), more, 0)
            slot = lax.rem(image, 2)

            @pl.when(image >= 2)
            def _():
                for copy in out_copies(s, i, slot):
                    copy.wait()

            staged[slot, 0] = back[:, 0:D].astype(BF)
            staged[slot, 1] = back[:, D : 2 * D].astype(BF)
            for copy in out_copies(s, i, slot):
                copy.start()
            cols[pl.ds(at_rows, ROWS)] = back[:, 2 * D :]

        for s in range(groups):

            def one(i, _, s=s):
                restore(s, i)
                return 0

            lax.fori_loop(0, n_tok // ROWS, one, 0)
        for slot in range(2):
            for copy in out_copies(groups - 1, 0, slot):
                copy.wait()
        for at in range(0, total, 128):
            place_t = cols[at : at + 128].T[0:8]
            s, left = divmod(at, n_tok)
            here = min(128, n_tok - left)
            delta_refs[s][:, left : left + here] = place_t[:, 0:here]
            if here < 128:
                delta_refs[s + 1][:, 0 : 128 - here] = place_t[:, here:]


def experts_all(cs, gs, rs, router_t, win, wout, slots_most, owners):
    groups = len(cs)
    local = win.shape[0]
    n_tok = cs[0].shape[0]
    total = groups * n_tok
    images = total // ROWS
    room = -(-(slots_most + local * 384 + TILE) // 128) * 128
    width = 2 * D + 128
    deepest = -(-slots_most // local // TILE) * TILE

    def full(shape):
        return pl.BlockSpec(tuple(shape), lambda i: (0,) * len(shape))

    outs = [jax.ShapeDtypeStruct((local, 2, FF, D), BF)]
    outs += [jax.ShapeDtypeStruct((n_tok, D), BF)] * (2 * groups)
    outs += [jax.ShapeDtypeStruct((8, n_tok), F32)] * groups
    vm = pltpu.VMEM
    result = pl.pallas_call(
        functools.partial(experts_kernel, groups, local, "exp"),
        grid=(local,),
        out_shape=outs,
        in_specs=[pl.BlockSpec(memory_space=pl.ANY)] * (2 * groups)
        + [VMEM] * (groups + 1)
        + [pl.BlockSpec((1, D, FF), lambda i: (i, 0, 0)), pl.BlockSpec((1, FF, D), lambda i: (i, 0, 0))],
        out_specs=[pl.BlockSpec((1, 2, FF, D), lambda i: (i, 0, 0, 0))]
        + [pl.BlockSpec(memory_space=pl.ANY)] * (2 * groups)
        + [full(o.shape) for o in outs[2 * groups + 1 :]],
        scratch_shapes=[
            vm((total, width), BF),
            vm((total, 128), F32),
            vm((images, 8, ROWS), F32),
            vm((room, width), BF),
            vm((room, width), BF),
            vm((deepest, D), BF),
            vm((deepest, FF), BF),
            vm((deepest, FF), BF),
            vm((local * 128, width), BF),
            vm((ROWS, width), F32),
            vm((2, 2, ROWS, D), BF),
            vm((8, 128), jnp.int32),
            pltpu.SMEM((8, 128), jnp.int32),
            pltpu.SMEM((local * (images + 3),), jnp.int32),
            pltpu.SemaphoreType.DMA(()),
            pltpu.SemaphoreType.DMA((2 * groups,)),
            pltpu.SemaphoreType.DMA((2, 2)),
        ],
        compiler_params=pltpu.CompilerParams(vmem_limit_bytes=62 << 20),
        name="experts",
    )(*cs, *gs, *rs, router_t, win, wout)
    eg = result[0].reshape((local, 2) + owners + (FF // math.prod(owners), D))
    return eg, result[1 : groups + 1], result[groups + 1 : 2 * groups + 1], result[2 * groups + 1 :]


class Halving:
    def __init__(self, place, links, total, dims, order, received, lead=()):
        self.p, self.links, self.total, self.dims, self.order = place, links, total, dims, order
        self.received, self.lead = received, lead
        self.first = links.reserve(len(order) + 2 * order.count("z"))

    def where(self, fixed):
        return (slice(None),) * len(self.lead) + tuple(fixed.get(b, slice(None)) for b in self.dims)

    def copies(self, k):
        b = self.order[k]
        fixed = {q: self.p.bit[q] for q in self.order[:k]}
        if b == "z":
            return [
                self.links.copy(self.first + k + n, self.total.at[self.where({**fixed, **bits})], self.received[k].at[n], device)
                for n, (bits, device) in enumerate(self.p.others)
            ]
        fixed[b] = 1 - self.p.bit[b]
        return [self.links.copy(self.first + k, self.total.at[self.where(fixed)], self.received[k], self.p.partner[b])]

    def add(self, fixed, other, other_dims):
        free = [b for b in self.dims if b not in fixed]
        sizes = list(self.lead) + [2] * len(free)

        def block(i, _):
            at = []
            for size in reversed(sizes):
                at.insert(0, i % size)
                i = i // size
            full = dict(fixed, **dict(zip(free, at[len(self.lead) :])))
            mine = self.total.at[tuple(at[: len(self.lead)]) + tuple(full[b] for b in self.dims)]
            term = other.at[tuple(at[: len(self.lead)]) + tuple(full[b] for b in other_dims)]
            mine[...] = (mine[...].astype(F32) + term[...].astype(F32)).astype(BF)
            return 0

        lax.fori_loop(0, math.prod(sizes), block, 0)

    def step(self, k, other=None):
        fixed = {q: self.p.bit[q] for q in self.order[:k] if q != "z"}
        other_dims = [b for b in self.dims if b not in fixed]
        if k:
            for copy in self.copies(k - 1):
                copy.wait()
            other = self.received[k - 1]
        if k == len(self.order) and self.order[-1] == "z":
            mine = self.own()
            total = mine[...].astype(F32)
            for n in range(len(self.p.others)):
                total = total + other[n].astype(F32)
            mine[...] = total.astype(BF)
        elif k < len(self.order) and self.order[k] != "z":
            b = self.order[k]
            self.add(dict(fixed, **{b: 1 - self.p.bit[b]}), other, other_dims)
            self.copies(k)[0].start()
            self.add(dict(fixed, **{b: self.p.bit[b]}), other, other_dims)
        else:
            self.add(fixed, other, other_dims)
            if k < len(self.order):
                for copy in self.copies(k):
                    copy.start()

    def own(self):
        return self.total.at[self.where(self.p.bit)]


class ExpertSum:
    def __init__(self, place, links, j, slot, eg, own, part, received, order, out, local_sem):
        self.p, self.links, self.out = place, links, out.at[j]
        self.given = eg.at[j]
        self.mine = own.at[slot]
        self.load = pltpu.make_async_copy(self.given.at[:, :, :, :, place.bit["c"]], self.mine, local_sem.at[slot])
        self.core = links.copy(
            links.reserve(1), self.given.at[:, :, :, :, 1 - place.bit["c"]], part.at[j], place.partner["c"]
        )
        self.halving = Halving(place, links, part.at[j], "hlx", order, received, lead=(2,))

    def run(self, k):
        if k == 0:
            self.core.start()
            return
        if k == 1:
            self.load.wait()
            self.core.wait()
        self.halving.step(k - 1, self.mine)
        if k == 4:
            self.out[...] = self.halving.own()[...].astype(F32)


class SharedSum:
    def __init__(self, place, links, src, core_rx, received, order, out):
        self.p, self.links, self.order, self.out, self.core_rx = place, links, order, out, core_rx
        self.core = links.copy(links.reserve(1), src.at[1 - place.bit["c"]], core_rx, place.partner["c"])
        self.halving = Halving(place, links, src.at[place.bit["c"]], "yxhl", order, received)
        self.first = links.reserve(len(order) + 3)

    def back(self, k):
        known = "c" + self.order[: len(self.order) - k] if k <= len(self.order) else ""
        bits = known.replace("z", "hl")
        mine = self.out.at[tuple(self.p.bit[b] if b in bits else slice(None) for b in BITS)]
        if known[-1] == "z":
            return [self.links.copy(self.first + n, mine, mine, device) for n, (_, device) in enumerate(self.p.others)]
        return [self.links.copy(self.first + 2 + k, mine, mine, self.p.partner[known[-1]])]

    def run(self, k):
        n = len(self.order)
        if k == 0:
            self.core.start()
        elif k <= n:
            if k == 1:
                self.core.wait()
            self.halving.step(k - 1, self.core_rx)
        elif k == n + 1:
            self.halving.step(n)
            self.out[tuple(self.p.bit[b] for b in BITS)] = self.halving.own()[...]
            for copy in self.back(0):
                copy.start()
        else:
            for copy in self.back(k - n - 2):
                copy.wait()
            if k <= 2 * n + 1:
                for copy in self.back(k - n - 1):
                    copy.start()


class SmallSum:
    def __init__(self, place, links, src, rx):
        self.p, self.links, self.src, self.rx = place, links, src, rx
        self.first = links.reserve(len(BITS))

    def copy(self, k):
        return self.links.copy(self.first + k, self.src.at[k], self.rx.at[k], self.p.partner[BITS[k]])

    def run(self, k, out):
        if k:
            self.copy(k - 1).wait()
            total = self.src[k - 1] + self.rx[k - 1]
            if k == len(BITS):
                out[...] = total
                return
            self.src[k] = total
        self.copy(k).start()


GROUPS = ((48, "yxz"), (48, "xyz"), (48, "yxz"), (32, "yxz"), (16, "yxz"))
GROUP_ROWS = (0, 1536, 3072, 4608, 5632)
EXPERT_ORDERS = ("lhx", "xlh", "xlh", "xlh")

ORDER = (
    ("E", 3, 0), ("E", 0, 0), ("d", 0, 0), ("E", 1, 0), ("E", 2, 0), ("E", 3, 1), ("d", 1, 0), ("run", 0, 0),
    ("d", 2, 0), ("E", 0, 1), ("run", 1, 0), ("d", 3, 0), ("E", 1, 1), ("E", 2, 1), ("y", 0, 0), ("run", 2, 0),
    ("run", 3, 0), ("E", 3, 2), ("run", 4, 0), ("run", 5, 0), ("run", 6, 0), ("S", 0, 0), ("run", 7, 0),
    ("run", 8, 0), ("run", 9, 0), ("E", 0, 2), ("S", 0, 1), ("run", 10, 0), ("E", 1, 2), ("run", 11, 0),
    ("run", 12, 0), ("run", 13, 0), ("S", 1, 0), ("S", 2, 0), ("run", 14, 0), ("S", 0, 2), ("run", 15, 0),
    ("S", 2, 1), ("E", 3, 3), ("run", 16, 0), ("S", 1, 1), ("S", 0, 3), ("run", 17, 0), ("run", 18, 0), ("S", 4, 0),
    ("S", 3, 0), ("S", 2, 2), ("run", 19, 0), ("S", 4, 1), ("S", 1, 2), ("few", 0, 0), ("S", 0, 4), ("S", 3, 1),
    ("S", 2, 3), ("S", 4, 2), ("S", 0, 5), ("S", 4, 3), ("S", 1, 3), ("S", 3, 2), ("S", 2, 4), ("S", 0, 6),
    ("S", 3, 3), ("S", 1, 4), ("E", 3, 4), ("few", 1, 0), ("E", 0, 3), ("S", 3, 4), ("S", 4, 4), ("S", 2, 5),
    ("E", 2, 2), ("few", 2, 0), ("E", 1, 3), ("S", 1, 5), ("S", 3, 5), ("S", 2, 6), ("S", 4, 5), ("E", 0, 4),
    ("few", 3, 0), ("S", 1, 6), ("run", 20, 0), ("S", 3, 6), ("S", 4, 6), ("E", 2, 3), ("S", 1, 7), ("few", 4, 0),
    ("S", 2, 7), ("E", 1, 4), ("S", 3, 7), ("S", 0, 7), ("S", 1, 8), ("S", 4, 7), ("S", 3, 8), ("S", 2, 8),
    ("S", 0, 8), ("E", 2, 4), ("S", 4, 8), ("few", 5, 0),
)

LOADED = ("c", "x3", "cot", "d", "delta", "x2", "qkv", "o", "p", "wo", "wqkv", "x1", "wout", "gp", "u", "win", "y", "x0")
EARLY = 10


def bwd_kernel(linked, *refs):
    names = ["gains", "router_t", "routes", "wqkv", "wo", "win", "wout", "x0", "x1", "x2", "x3", "qkv1", "qkv2"]
    names += ["o1", "o2", "p1", "p2", "u", "gp", "c", "cot", "d", "delta", "y"]
    if linked:
        names += ["d_send", "delta_send", "y_send", "eg"]
    names += ["act_out", "gin_out", "small_out"]
    if linked:
        names += ["eg_out"] + ["out" + str(g) for g in range(len(GROUPS))]
    else:
        names += ["shared_out"]
    names += ["v_" + n for n in LOADED] + ["gv", "a_scr", "dbr_scr", "dqkv_scr", "sem"]
    names += ["v_act", "v_gin", "leave_sem"]
    if linked:
        names += ["v_eg"] + ["v_out" + str(g) for g in range(len(GROUPS))]
    if linked:
        names += ["d_rx", "delta_rx", "y_rx", "own", "part", "small_src", "small_rx", "eg_sem", "send", "recv"]
        names += ["src" + str(g) for g in range(len(GROUPS))]
        names += ["rx" + str(g) + str(k) for g, (_, order) in enumerate(GROUPS) for k in range(len(order) + 1)]
        names += ["erx" + str(j) + str(k) for j in range(len(EXPERT_ORDERS)) for k in range(3)]
    r = dict(zip(names, refs, strict=True))
    gains, gv, a_scr, dbr_scr, dqkv_scr = (r[n] for n in ("gains", "gv", "a_scr", "dbr_scr", "dqkv_scr"))
    images = gv.shape[0]
    m = images * ROWS
    lo = lane_low(ROWS)

    second = {"qkv": "qkv2", "o": "o2", "p": "p2"}
    copies = {}

    def fetch(name, source):
        copies[name] = pltpu.make_async_copy(r[source], r["v_" + name], r["sem"].at[LOADED.index(name)])
        copies[name].start()

    def need(*wanted):
        for name in wanted:
            copies[name].wait()

    leaving = []

    def leave(source, target):
        leaving.append(pltpu.make_async_copy(source, target, r["leave_sem"].at[len(leaving)]))
        leaving[-1].start()

    if linked:
        place = Place()
        links = Links(r["send"], r["recv"])
        partners = [place.partner[b] for b in "cyx"] + [device for _, device in place.others]
        place.greet(partners)
        place.meet(partners)
        beside = place.partner["y"]
        delta_copy = links.copy(links.reserve(1), r["delta_send"], r["delta_rx"], beside)
        delta_copy.start()
        d_first = links.reserve(images)

        def d_copy(i):
            return links.copy(d_first + i, r["d_send"].at[i], r["d_rx"].at[i], beside)

        turn = [at for kind, at, what in ORDER if (kind, what) == ("E", 1)]
        experts = [
            ExpertSum(
                place, links, j, turn.index(j) % 2, r["eg"], r["own"], r["part"], [r["erx" + str(j) + str(k)] for k in range(3)],
                order, r["v_eg"], r["eg_sem"],
            )
            for j, order in enumerate(EXPERT_ORDERS)
        ]
        experts[turn[0]].load.start()
        experts[turn[1]].load.start()
        y_copy = links.copy(links.reserve(1), r["y_send"], r["y_rx"], beside)
        sums = []
        for g, (_, order) in enumerate(GROUPS):
            rx = [r["rx" + str(g) + str(k)] for k in range(len(order) + 1)]
            sums.append(SharedSum(place, links, r["src" + str(g)], rx[0], rx[1:], order, r["v_out" + str(g)]))
        few = SmallSum(place, links, r["small_src"], r["small_rx"])
        small = r["small_src"].at[0]
        small[...] = jnp.zeros(small.shape, F32)
    else:
        small = r["small_out"]
    for name in LOADED[:EARLY]:
        fetch(name, second.get(name, name))

    def keep(block, value):
        value = value.astype(BF)
        if not linked:
            r["shared_out"][block] = value
            return
        row, end = block * D, block * D + D
        for g, (share, _) in enumerate(GROUPS):
            base, cell = GROUP_ROWS[g], 4 * share
            for q in range(8):
                at = base + q * cell
                if row <= at and at + cell <= end:
                    part = value[at - row : at - row + cell]
                    r["src" + str(g)][q // 4, q // 2 % 2, q % 2] = part.reshape(2, 2, share, D)

    def router():
        need("c", "delta")
        c_all = r["v_c"][...].reshape(m, D)
        g0, g1, first, other = gate_rows(r["router_t"][...], c_all, r["routes"][...])
        delta = r["v_delta"][0:1] + r["v_delta"][1:2]
        if linked:
            delta_copy.wait()
            delta = delta + (r["delta_rx"][0:1] + r["delta_rx"][1:2])
        dl = g0 * g1 * delta
        dlog = jnp.where(first, dl, jnp.where(other, -dl, 0.0)).astype(BF)
        small[4 : 4 + dlog.shape[0]] = dot(dlog, c_all)
        small[0:4] = jnp.zeros((4, D), F32)
        gv[...] = t_dot(dlog, r["router_t"][...]).reshape(images, ROWS, D)
        need("x3", "cot", "d")

    def add_gain(row, by_gain):
        small[row : row + 1] += jnp.sum(by_gain, axis=0, keepdims=True)

    def first(i):
        dc = gv[i] + r["v_d"][i].astype(F32)
        if linked:
            d_copy(i).wait()
            dc = dc + r["d_rx"][i].astype(F32)
        dx, by_gain = norm_back(dc, r["v_x3"][i], gains[3:4])
        gv[i] = r["v_cot"][i].astype(F32) + dx
        add_gain(3, by_gain)
        if i == 0:
            need("x2", "qkv", "o", "p", "wo")
            for name in LOADED[EARLY:]:
                fetch(name, name)
        attend_image(i, 1, gains[2:3], r["v_x2"])

    def attend_image(i, layer, gain, x):
        qkv, o, p = r["v_qkv"], r["v_o"], r["v_p"]
        a_scr[i] = (norm_parts(x[i].astype(F32))[0] * gain).astype(BF)
        dbr = gv[i].astype(BF)
        dbr_scr[i] = dbr
        do = dot_t(dbr, r["v_wo"][layer]).astype(BF)
        dod = do.astype(F32) * o[i].astype(F32)
        for pair in range(HEADS // 2):
            at = 128 * pair
            q = qkv[i, :, at : at + 128] * BF(0.125)
            k = qkv[i, :, D + at : D + at + 128]
            w = qkv[i, :, 2 * D + at : 2 * D + at + 128]
            dqs, dk, dw = [], 0.0, 0.0
            for h in range(2):
                mask = lo if h == 0 else ~lo
                dom = jnp.where(mask, do[:, at : at + 128], BF(0))
                inner = jnp.sum(jnp.where(mask, dod[:, at : at + 128], 0.0), axis=-1, keepdims=True)
                ph = p[i, 2 * pair + h]
                ds = (ph.astype(F32) * (dot_t(dom, w) - inner)).astype(BF)
                dw = dw + t_dot(ph, dom)
                dqs.append(dot(ds, k))
                dk = dk + t_dot(ds, jnp.where(mask, q, BF(0)))
            dqkv_scr[i, :, at : at + 128] = (jnp.where(lo, dqs[0], dqs[1]) * 0.125).astype(BF)
            dqkv_scr[i, :, D + at : D + at + 128] = dk.astype(BF)
            dqkv_scr[i, :, 2 * D + at : 2 * D + at + 128] = dw.astype(BF)

    def attend_weights(block):
        a_all = a_scr[...].reshape(m, D)
        for f in range(3):
            keep(block + f, t_dot(a_all, dqkv_scr[:, :, f * D : f * D + D].reshape(m, D)))
        keep(block + 3, t_dot(r["v_o"][...].reshape(m, D), dbr_scr[...].reshape(m, D)))

    def close(x, layer, row, out):
        def image(i, _):
            da = dot_t(dqkv_scr[i], r["v_wqkv"][layer])
            dx, by_gain = norm_back(da, x[i].astype(F32), gains[row : row + 1])
            out[i] = gv[i] + dx
            add_gain(row, by_gain)
            return 0

        lax.fori_loop(0, images, image, 0)

    def first_close():
        for name in ("qkv", "o", "p"):
            fetch(name, name + "1")
        need("wqkv")
        close(r["v_x2"], 1, 2, gv)
        need("x1", "wout", "gp", "u", "win")

    gp = r["v_gp"]

    def mlp(i):
        a_scr[i] = (norm_parts(r["v_x1"][i])[0] * gains[1:2]).astype(BF)
        dm = gv[i].astype(BF)
        dbr_scr[i] = dm
        for f in range(0, FF, 512):
            du = dot_t(dm, r["v_wout"][f : f + 512])
            gp[i, :, f : f + 512] = (du * gp[i, :, f : f + 512].astype(F32)).astype(BF)

    def mlp_out_weights():
        dm_all = dbr_scr[...].reshape(m, D)
        for f in range(4):
            keep(4 + f, t_dot(r["v_u"][:, :, f * D : f * D + D].reshape(m, D), dm_all))

    def mlp_in_weights():
        b_all = a_scr[...].reshape(m, D)
        for f in range(4):
            keep(8 + f, t_dot(b_all, gp[:, :, f * D : f * D + D].reshape(m, D)))

    def mlp_close():
        def image(i, _):
            db = dot_t(gp[i], r["v_win"][...])
            dx, by_gain = norm_back(db, r["v_x1"][i], gains[1:2])
            gv[i] = gv[i] + dx
            add_gain(1, by_gain)
            return 0

        lax.fori_loop(0, images, image, 0)
        need("x0", "qkv", "o", "p")

    def last(i):
        attend_image(i, 0, gains[0:1], r["v_x0"])

    def last_close():
        close(r["v_x0"], 0, 0, r["v_gin"])
        leave(r["v_gin"], r["gin_out"])

    def act():
        need("y")
        if linked:
            y_copy.wait()
        for i in range(images):
            x4 = r["v_x3"][i] + r["v_y"][i].astype(F32)
            if linked:
                x4 = x4 + r["y_rx"][i].astype(F32)
            r["v_act"][i] = x4.astype(BF)
        leave(r["v_act"], r["act_out"])

    compute = [router] + [functools.partial(first, i) for i in range(images)]
    compute += [lambda: attend_weights(0), first_close] + [functools.partial(mlp, i) for i in range(images)]
    compute += [mlp_out_weights, mlp_in_weights, mlp_close] + [functools.partial(last, i) for i in range(images)]
    compute += [lambda: attend_weights(12), last_close, act]
    if not linked:
        for step in compute:
            step()
        for copy in leaving:
            copy.wait()
        return
    done = 0
    for kind, at, what in ORDER:
        if kind == "run":
            compute[done]()
            done += 1
        elif kind == "d":
            d_copy(at).start()
        elif kind == "y":
            y_copy.start()
        elif kind == "few":
            few.run(at, r["small_out"])
        elif kind == "E":
            experts[at].run(what)
            if what == 4:
                leave(r["v_eg"].at[at], r["eg_out"].at[at])
            if what == 1 and turn.index(at) + 2 < len(turn):
                experts[turn[turn.index(at) + 2]].load.start()
        else:
            sums[at].run(what)
            if what == 2 * len(GROUPS[at][1]) + 2:
                leave(r["v_out" + str(at)], r["out" + str(at)])
    for copy in leaving:
        copy.wait()


def dense_backward(weights, router_t, routes, saved, cot, d, delta, y, sent=None):
    gains, wqkv, wo, win, wout = weights
    x0, x1, x2, x3, qkv1, qkv2, o1, o2, p1, p2, u, gp, c = saved
    images = x0.shape[0]
    linked = sent is not None
    small_rows = 16 if linked else 4 + router_t.shape[0]
    ins = [gains, router_t, routes, wqkv, wo, win, wout, *saved, cot, d, delta, y] + (list(sent) if linked else [])
    outs = [
        jax.ShapeDtypeStruct((images, ROWS, D), BF),
        jax.ShapeDtypeStruct((images, ROWS, D), F32),
        jax.ShapeDtypeStruct((small_rows, D), F32),
    ]
    if not linked:
        outs.append(jax.ShapeDtypeStruct((16, D, D), BF))
    vm = pltpu.VMEM
    loaded = dict(
        c=c, x3=x3, cot=cot, d=d, delta=delta, x2=x2, qkv=qkv1, o=o1, p=p1, wo=wo, wqkv=wqkv, x1=x1, wout=wout,
        gp=gp, u=u, win=win, y=y, x0=x0,
    )
    scratch = [vm(loaded[name].shape, loaded[name].dtype) for name in LOADED]
    scratch += [vm((images, ROWS, D), F32), vm((images, ROWS, D), BF), vm((images, ROWS, D), BF)]
    scratch += [vm((images, ROWS, 3 * D), BF), pltpu.SemaphoreType.DMA((len(LOADED),))]
    leavers = 2 + (sent[-1].shape[0] + len(GROUPS) if linked else 0)
    scratch += [vm((images, ROWS, D), BF), vm((images, ROWS, D), F32), pltpu.SemaphoreType.DMA((leavers,))]
    params = dict(vmem_limit_bytes=62 << 20)
    if linked:
        eg = sent[-1]
        local, share = eg.shape[0], eg.shape[-2]
        outs.append(jax.ShapeDtypeStruct((local, 2, share, D), F32))
        outs += [jax.ShapeDtypeStruct((2,) * 5 + (rows, D), BF) for rows, _ in GROUPS]
        copies = 2 + images + 4 * local + 15 * len(GROUPS) + len(BITS)
        scratch += [vm((local, 2, share, D), F32)] + [vm((2,) * 5 + (rows, D), BF) for rows, _ in GROUPS]
        scratch += [vm(d.shape, BF), vm(delta.shape, F32), vm(y.shape, BF)]
        scratch += [
            vm((2, 2, 2, 2, 2, share, D), BF),
            vm((local, 2, 2, 2, 2, share, D), BF),
            vm((len(BITS), small_rows, D), F32),
            vm((len(BITS), small_rows, D), F32),
            pltpu.SemaphoreType.DMA((2,)),
            pltpu.SemaphoreType.DMA((copies,)),
            pltpu.SemaphoreType.DMA((copies,)),
        ]
        scratch += [vm((2,) * 5 + (rows, D), BF) for rows, _ in GROUPS]
        for rows, order in GROUPS:
            scratch += [vm((2,) * (4 - k) + (rows, D), BF) for k in range(len(order.strip("z")) + 1)]
            if "z" in order:
                scratch.append(vm((3, rows, D), BF))
        scratch += [vm((2,) * (3 - k) + (share, D), BF) for _ in EXPERT_ORDERS for k in range(3)]
        params.update(collective_id=1, has_side_effects=True)
    far = pl.BlockSpec(memory_space=pl.ANY)
    out_specs = [far, far, VMEM] + [far if linked else VMEM] * (len(outs) - 3)
    return pl.pallas_call(
        functools.partial(bwd_kernel, linked),
        out_shape=outs,
        in_specs=[VMEM] * 3 + [pl.BlockSpec(memory_space=pl.ANY)] * (len(ins) - 3),
        out_specs=out_specs,
        scratch_shapes=scratch,
        compiler_params=pltpu.CompilerParams(**params),
        name="dense_backward",
    )(*ins)


def finish_kernel(n_shared, act, gin, small, eg, *refs):
    shared, refs = refs[:n_shared], refs[n_shared:]
    act_out, gin_out, qkv_out, proj_out, gain_out, mlp_in_out, mlp_out_out, router_out, in_out, out_out = refs[:10]
    v_shared, v_wide, v_gin, v_act, in_sem, out_sem = refs[10:]
    images = act.shape[0]
    blocks = v_wide.shape[0]
    targets = {3: proj_out.at[1], 15: proj_out.at[0]}
    for f in range(3):
        targets[f] = qkv_out.at[1, :, pl.ds(f * D, D)]
        targets[12 + f] = qkv_out.at[0, :, pl.ds(f * D, D)]
    for f in range(4):
        targets[4 + f] = mlp_out_out.at[pl.ds(f * D, D)]
        targets[8 + f] = mlp_in_out.at[:, pl.ds(f * D, D)]
    loads, at = [], 0
    for k, part in enumerate(shared):
        rows = part.shape[0]
        loads.append((at, pltpu.make_async_copy(part, v_shared.at[pl.ds(at, rows)], in_sem.at[k])))
        at += rows
    load_gin = pltpu.make_async_copy(gin, v_gin, in_sem.at[n_shared])
    load_act = pltpu.make_async_copy(act, v_act, in_sem.at[n_shared + 1])
    for _, load in loads:
        load.start()
    load_gin.start()
    load_act.start()

    def store(b):
        return pltpu.make_async_copy(v_wide.at[b], targets[b], out_sem.at[b])

    waited = 0
    for b in range(blocks):
        while waited < n_shared and loads[waited][0] < (b + 1) * D:
            loads[waited][1].wait()
            waited += 1
        v_wide[b] = v_shared[b * D : (b + 1) * D].astype(F32)
        store(b).start()
    gain_out[...] = small[0:4]
    router_out[...] = small[4 : 4 + router_out.shape[0]]
    for e in range(eg.shape[0]):
        in_out[e] = eg[e, 0]
        out_out[e] = eg[e, 1]
    load_gin.wait()
    load_act.wait()
    for i in range(images):
        gin_out[i * PATCHES : (i + 1) * PATCHES] = v_act[i, 0:PATCHES].astype(F32)
    act_out[...] = gin_out[...].astype(BF)
    for i in range(images):
        gin_out[i * PATCHES : (i + 1) * PATCHES] = v_gin[i, 0:PATCHES]
    for b in range(blocks):
        store(b).wait()


def finish(act, gin, shared, small, eg, experts):
    images, local, share = act.shape[0], eg.shape[0], eg.shape[2]
    row_count = images * PATCHES
    blocks = 16
    outs = [
        jax.ShapeDtypeStruct((row_count, D), BF),
        jax.ShapeDtypeStruct((row_count, D), F32),
        jax.ShapeDtypeStruct((2, D, 3 * D), F32),
        jax.ShapeDtypeStruct((2, D, D), F32),
        jax.ShapeDtypeStruct((4, D), F32),
        jax.ShapeDtypeStruct((D, FF), F32),
        jax.ShapeDtypeStruct((FF, D), F32),
        jax.ShapeDtypeStruct((experts, D), F32),
        jax.ShapeDtypeStruct((local, share, D), F32),
        jax.ShapeDtypeStruct((local, share, D), F32),
    ]
    far = pl.BlockSpec(memory_space=pl.ANY)
    return pl.pallas_call(
        functools.partial(finish_kernel, len(shared)),
        out_shape=outs,
        in_specs=[far, far, VMEM, VMEM] + [far] * len(shared),
        out_specs=[VMEM, VMEM, far, far, VMEM, far, far, VMEM, VMEM, VMEM],
        scratch_shapes=[
            pltpu.VMEM((blocks * D, D), BF),
            pltpu.VMEM((blocks, D, D), F32),
            pltpu.VMEM(gin.shape, F32),
            pltpu.VMEM(act.shape, BF),
            pltpu.SemaphoreType.DMA((len(shared) + 2,)),
            pltpu.SemaphoreType.DMA((blocks,)),
        ],
        compiler_params=pltpu.CompilerParams(vmem_limit_bytes=62 << 20),
        name="finish",
    )(act, gin, small, eg, *shared)


def from_peer(array, groups, shift):
    return lax.ppermute(array, "exp", [(i, (i + shift) % groups) for i in range(groups)])


def shards(
    tokens, routes, norm_gains, attn_qkv, attn_out, mlp_in, mlp_out, router, experts_in, experts_out, cotangent
):
    row_count = tokens.shape[0]
    groups = lax.axis_size("exp")
    local = experts_in.shape[0]
    choices = routes.shape[1]
    capacity = 2 * choices * row_count // (local * groups)
    images = row_count // PATCHES
    router_t = router.T
    rep = lax.axis_size("rep")
    known = (rep, groups, local) == (16, 2, 4)
    owners = (2, 2, 2, 2) if known else (rep,)
    routes_t, x0, cot, x1, x2, x3, qkv1, qkv2, o1, o2, p1, p2, u, gp, c, *received = dense_forward(
        tokens, cotangent, routes.T, norm_gains, attn_qkv, attn_out, mlp_in, mlp_out, known
    )

    def of_all(mine, place):
        if known:
            others = [received[place]]
        else:
            others = [from_peer(mine, groups, k) for k in range(1, groups)]
        return [part.reshape(-1, part.shape[-1]) for part in [mine] + others]

    cs, gs, rs = of_all(c, 0), of_all(cot, 1), of_all(routes_t, 2)
    eg, ys, ds, deltas = experts_all(
        cs, gs, rs, router_t, experts_in, experts_out, local * capacity * groups, owners
    )

    weights = (norm_gains, attn_qkv, attn_out, mlp_in, mlp_out)
    saved = (x0, x1, x2, x3, qkv1, qkv2, o1, o2, p1, p2, u, gp, c)
    by_image = (images, ROWS, D)
    experts = router_t.shape[0]
    if known:
        sent = (ds[1].reshape(by_image), deltas[1], ys[1].reshape(by_image), eg)
        act, gin, small, eg, *shared = dense_backward(
            weights, router_t, routes_t, saved, cot, ds[0].reshape(by_image), deltas[0], ys[0].reshape(by_image), sent
        )
        shared = [part.reshape(-1, D) for part in shared]
    else:

        def back(parts):
            total = parts[0].astype(F32)
            for k in range(1, groups):
                total = total + from_peer(parts[k], groups, groups - k).astype(F32)
            return total

        d, delta, y = back(ds).astype(BF), back(deltas), back(ys).astype(BF)
        act, gin, small, shared = dense_backward(
            weights, router_t, routes_t, saved, cot, d.reshape(by_image), delta, y.reshape(by_image)
        )
        eg = lax.psum_scatter(eg, "rep", scatter_dimension=2, tiled=True).reshape(local, 2, FF // rep, D).astype(F32)
        shared, small = lax.psum((shared, small), ("rep", "exp"))
        shared = [shared.reshape(-1, D)]
    outs = list(finish(act, gin, shared, small, eg, experts))
    outs[7] = outs[7].T
    outs[8] = jnp.swapaxes(outs[8], 1, 2)
    return tuple(outs)


def solution(mesh):
    rows = P(("rep", "exp"), None)
    return jax.shard_map(
        shards,
        mesh=mesh,
        in_specs=(rows, rows, P(), P(), P(), P(), P(), P(), P("exp", None, None), P("exp", None, None), rows),
        out_specs=(rows, rows, P(), P(), P(), P(), P(), P(), P("exp", None, "rep"), P("exp", "rep", None)),
        check_vma=False,
    )
```

```python
import functools
import math

import jax
import jax.numpy as jnp
from jax import lax
from jax.experimental import pallas as pl
from jax.experimental.pallas import tpu as pltpu
from jax.sharding import PartitionSpec as P

F32 = jnp.float32
BF = jnp.bfloat16
HEADS = 6
PATCHES = 197
ROWS = 208
EPS = 1e-6
TILE = 256
D = 384
FF = 1536
IMAGES_AT_ONCE = 1
VMEM = pl.BlockSpec(memory_space=pltpu.VMEM)


def dot(a, b):
    return lax.dot_general(a, b, (((1,), (0,)), ((), ())), preferred_element_type=F32)


def dot_t(a, b):
    return lax.dot_general(a, b, (((1,), (1,)), ((), ())), preferred_element_type=F32)


def t_dot(a, b):
    return lax.dot_general(a, b, (((0,), (0,)), ((), ())), preferred_element_type=F32)


def norm_parts(x):
    centred = x - jnp.mean(x, axis=-1, keepdims=True)
    rstd = lax.rsqrt(jnp.mean(centred * centred, axis=-1, keepdims=True) + EPS)
    return centred * rstd, rstd


def norm_back(grad, x, gain):
    xh, rstd = norm_parts(x)
    dxh = grad * gain
    inner = dxh - jnp.mean(dxh, axis=-1, keepdims=True)
    return rstd * (inner - xh * jnp.mean(dxh * xh, axis=-1, keepdims=True)), grad * xh


def gelu_parts(h):
    phi = 0.5 + 0.5 * lax.erf(0.7071067811865476 * h)
    e = jnp.exp2(h * h * -0.7213475204444817)
    return h * phi, phi + h * (0.3989422804014327 * e)


def lane_low(rows):
    return lax.broadcasted_iota(jnp.int32, (rows, 128), 1) < 64


MESH = pl.DeviceIdType.MESH
BITS = "cyxhl"


class Place:
    def __init__(self):
        r = lax.axis_index("rep")
        y = lax.axis_index("exp")
        self.bit = {"c": r % 2, "y": y, "x": (r // 2) % 2, "h": r // 8, "l": (r // 4) % 2}
        stride = {"c": 1, "x": 2, "l": 4, "h": 8}
        self.partner = {b: (r + stride[b] * (1 - 2 * self.bit[b]), y) for b in stride}
        self.partner["y"] = (r, 1 - y)
        self.others = []
        for k in range(1, 4):
            z = (r // 4 + k) % 4
            self.others.append(({"h": z // 2, "l": z % 2}, (z * 4 + r % 4, y)))

    def greet(self, partners):
        for partner in partners:
            pl.semaphore_signal(pltpu.get_barrier_semaphore(), inc=1, device_id=partner, device_id_type=MESH)

    def meet(self, partners):
        pl.semaphore_wait(pltpu.get_barrier_semaphore(), len(partners))


class Links:
    def __init__(self, send, recv):
        self.send, self.recv, self.used = send, recv, 0

    def reserve(self, count):
        first = self.used
        self.used += count
        return first

    def copy(self, at, src, dst, device):
        return pltpu.make_async_remote_copy(
            src_ref=src, dst_ref=dst, send_sem=self.send.at[at], recv_sem=self.recv.at[at],
            device_id=device, device_id_type=MESH,
        )

    def start(self, at, src, dst, device):
        copy = self.copy(at, src, dst, device)
        copy.start()
        return copy


def fwd_kernel(linked, *refs):
    weights = ["wqkv", "wo", "win", "wout"]
    names = ["tokens", "cot", "routes", "gains"] + ["far_" + name for name in weights]
    names += ["routes_out", "x0", "cot_out", "x1", "x2", "x3", "qkv1", "qkv2", "o1", "o2", "p1", "p2", "u", "gp", "c"]
    if linked:
        names += ["c_rx", "cot_rx", "routes_rx"]
    names += ["wide"] + weights + ["sem"]
    if linked:
        names += ["c_scr", "send", "recv"]
    r = dict(zip(names, refs, strict=True))
    gains = r["gains"]
    ib = r["x1"].shape[0]
    m = ib * ROWS
    images = r["x0"].shape[0]
    step = pl.program_id(0)
    lo = lane_low(ROWS)
    valid = lax.broadcasted_iota(jnp.int32, (ROWS, ROWS), 1) < PATCHES
    real = lax.broadcasted_iota(jnp.int32, (ROWS, D), 0) < PATCHES
    if linked:
        place = Place()
        links = Links(r["send"], r["recv"])

        def exchange(at, src, dst):
            return links.copy(at, src, dst, place.partner["y"])

        early = [exchange(0, r["cot_out"], r["cot_rx"]), exchange(1, r["routes_out"], r["routes_rx"])]

        def c_copy(image):
            return exchange(2 + image, r["c_scr"].at[image], r["c_rx"].at[image])

    @pl.when(step == 0)
    def _():
        if linked:
            place.greet([place.partner["y"]])
        loads = [pltpu.make_async_copy(r["far_" + w], r[w], r["sem"].at[k]) for k, w in enumerate(weights)]
        for load in loads:
            load.start()
        wide = r["wide"]
        slots = r["routes_out"]
        slots[...] = jnp.full(slots.shape, -1, jnp.int32)
        for i in range(images):
            slots[0:2, i * ROWS : i * ROWS + PATCHES] = r["routes"][:, i * PATCHES : (i + 1) * PATCHES]
        for source, target in (("cot", "cot_out"), ("tokens", "x0")):
            wide[0 : images * PATCHES] = r[source][...].astype(F32)
            for i in range(images):
                rows = wide[i * PATCHES : i * PATCHES + ROWS]
                r[target][i] = jnp.where(real, rows, 0.0).astype(BF)
            if linked and source == "cot":
                place.meet([place.partner["y"]])
                for copy in early:
                    copy.start()
        for load in loads:
            load.wait()

    def attend_image(i, qkv_ref, o_ref, p_ref):
        for pair in range(HEADS // 2):
            at = 128 * pair
            q = qkv_ref[i, :, at : at + 128] * BF(0.125)
            k = qkv_ref[i, :, D + at : D + at + 128]
            w = qkv_ref[i, :, 2 * D + at : 2 * D + at + 128]
            mixed = []
            for h in range(2):
                qm = jnp.where(lo if h == 0 else ~lo, q, BF(0))
                s = jnp.where(valid, dot_t(qm, k), -1e30)
                s = jnp.exp(s - jnp.max(s, axis=-1, keepdims=True))
                p = (s * (1.0 / jnp.sum(s, axis=-1, keepdims=True))).astype(BF)
                p_ref[i, 2 * pair + h] = p
                mixed.append(dot(p, w))
            o_ref[i, :, at : at + 128] = jnp.where(lo, mixed[0], mixed[1]).astype(BF)

    def project(x, layer, gain, qkv_ref):
        a = (norm_parts(x)[0] * gain).astype(BF)
        qkv_ref[...] = dot(a, r["wqkv"][layer]).astype(BF).reshape(ib, ROWS, 3 * D)

    x0 = r["x0"][pl.ds(step * ib, ib)].astype(F32).reshape(m, D)
    project(x0, 0, gains[0:1], r["qkv1"])
    for i in range(ib):
        attend_image(i, r["qkv1"], r["o1"], r["p1"])
    x1 = x0 + dot(r["o1"][...].reshape(m, D), r["wo"][0])
    r["x1"][...] = x1.reshape(ib, ROWS, D)
    b = (norm_parts(x1)[0] * gains[1:2]).astype(BF)
    x2 = x1
    for f in range(0, FF, 512):
        u, gp = gelu_parts(dot(b, r["win"][:, f : f + 512]))
        u = u.astype(BF)
        r["u"][:, :, f : f + 512] = u.reshape(ib, ROWS, 512)
        r["gp"][:, :, f : f + 512] = gp.astype(BF).reshape(ib, ROWS, 512)
        x2 = x2 + dot(u, r["wout"][f : f + 512])
    r["x2"][...] = x2.reshape(ib, ROWS, D)
    project(x2, 1, gains[2:3], r["qkv2"])

    def last(i, _):
        attend_image(i, r["qkv2"], r["o2"], r["p2"])
        x3 = r["x2"][i] + dot(r["o2"][i], r["wo"][1])
        r["x3"][i] = x3
        c = (norm_parts(x3)[0] * gains[3:4]).astype(BF)
        r["c"][i] = c
        if linked:
            r["c_scr"][step * ib + i] = c
            c_copy(step * ib + i).start()
        return 0

    lax.fori_loop(0, ib, last, 0)

    if linked:

        @pl.when(step == pl.num_programs(0) - 1)
        def _():
            for copy in early + [c_copy(i) for i in range(images)]:
                copy.wait()


def dense_forward(tokens, cot, routes, gains, wqkv, wo, win, wout, linked):
    n = tokens.shape[0] // PATCHES
    ib = IMAGES_AT_ONCE if n % IMAGES_AT_ONCE == 0 else 1

    def out(*shape, dtype=BF):
        return jax.ShapeDtypeStruct((n,) + shape, dtype)

    def block(shape):
        return pl.BlockSpec((ib,) + tuple(shape[1:]), lambda i: (i,) + (0,) * (len(shape) - 1))

    whole = pl.BlockSpec((n, ROWS, D), lambda i: (0, 0, 0))
    routes_shape = jax.ShapeDtypeStruct((8, n * ROWS), jnp.int32)
    outs = [routes_shape] + [out(ROWS, D)] * 2 + [out(ROWS, D, dtype=F32)] * 3 + [out(ROWS, 3 * D)] * 2 + [out(ROWS, D)] * 2
    outs += [out(HEADS, ROWS, ROWS)] * 2 + [out(ROWS, FF)] * 2 + [out(ROWS, D)]
    out_specs = [pl.BlockSpec(routes_shape.shape, lambda i: (0, 0)), whole, whole] + [block(o.shape) for o in outs[3:]]
    scratch = [pltpu.VMEM(((n - 1) * PATCHES + ROWS, D), F32)]
    scratch += [pltpu.VMEM(w.shape, BF) for w in (wqkv, wo, win, wout)] + [pltpu.SemaphoreType.DMA((4,))]
    params = dict(vmem_limit_bytes=62 << 20)
    if linked:
        outs += [out(ROWS, D)] * 2 + [routes_shape]
        out_specs += [pl.BlockSpec(memory_space=pl.ANY)] * 3
        copies = pltpu.SemaphoreType.DMA((2 + n,))
        scratch += [pltpu.VMEM((n, ROWS, D), BF), copies, copies]
        params.update(collective_id=2, has_side_effects=True)
    return pl.pallas_call(
        functools.partial(fwd_kernel, linked),
        grid=(n // ib,),
        out_shape=outs,
        in_specs=[VMEM] * 4 + [pl.BlockSpec(memory_space=pl.ANY)] * 4,
        out_specs=out_specs,
        scratch_shapes=scratch,
        compiler_params=pltpu.CompilerParams(**params),
        name="dense_forward",
    )(tokens, cot, routes, gains, wqkv, wo, win, wout)


def gate_rows(router_t, c, routes):
    logits = dot_t(router_t, c)
    expert = lax.broadcasted_iota(jnp.int32, logits.shape, 0)
    first, second = expert == routes[0:1], expert == routes[1:2]
    diff = jnp.sum(jnp.where(first, logits, 0.0) - jnp.where(second, logits, 0.0), axis=0, keepdims=True)
    return 1.0 / (1.0 + jnp.exp(-diff)), 1.0 / (1.0 + jnp.exp(diff)), first, second


def experts_kernel(groups, local, exp_axis, *refs):
    c_refs, g_refs, r_refs = refs[:groups], refs[groups : 2 * groups], refs[2 * groups : 3 * groups]
    router_t, win, wout = refs[3 * groups : 3 * groups + 3]
    outs = refs[3 * groups + 3 :]
    eg_ref, y_refs, d_refs, delta_refs = outs[0], outs[1 : groups + 1], outs[groups + 1 : 2 * groups + 1], outs[2 * groups + 1 : 3 * groups + 1]
    ci, cols, place, xg, slots, dy_scr, u_scr, gp_scr, stack, back, staged, count_v, count, plan, sem, load_sem, out_sem = outs[3 * groups + 1 :]
    n_tok = c_refs[0].shape[0]
    total = groups * n_tok
    images = total // ROWS
    step = pl.program_id(0)
    first_expert = lax.axis_index(exp_axis) * local

    def window(e, i):
        begin = plan[e * (images + 1) + i]
        return begin, pl.multiple_of(begin // 16 * 16, 16)

    def windows(i):
        most = jnp.int32(1)
        for e in range(local):
            at = window(e, i)[1]
            most = jnp.maximum(most, (plan[e * (images + 1) + i + 1] - at + 127) // 128)
        return most

    @pl.when(step == 0)
    def _():
        loads = []
        for k, (sources, first) in enumerate(((c_refs, 0), (g_refs, D + 128))):
            for s in range(groups):
                target = ci.at[pl.ds(s * n_tok, n_tok), pl.ds(first, D)]
                loads.append(pltpu.make_async_copy(sources[s], target, load_sem.at[k * groups + s]))
                loads[-1].start()
        for load in loads[:groups]:
            load.wait()
        routes = jnp.concatenate([r[0:2] for r in r_refs], axis=1)
        g0, g1, _, _ = gate_rows(router_t[...], ci[:, 0:D], routes)
        expert_row = lax.broadcasted_iota(jnp.int32, (8, total), 0)
        mine, inside = first_expert + expert_row, expert_row < local
        is0, is1 = (mine == routes[0:1]) & inside, (mine == routes[1:2]) & inside
        member = jnp.where(is0 | is1, 1.0, 0.0)
        lane = lax.broadcasted_iota(jnp.int32, (8, total), 1)
        of_image = lax.broadcasted_iota(jnp.int32, (total, 128), 0) // ROWS
        of_image = jnp.where(of_image == lax.broadcasted_iota(jnp.int32, (total, 128), 1), 1.0, 0.0)
        count_v[...] = dot(member.astype(BF), of_image.astype(BF)).astype(jnp.int32)
        to_scalars = pltpu.make_async_copy(count_v, count, sem)
        to_scalars.start()
        upto = member
        shift = 1
        while shift < total:
            upto = upto + jnp.where(lane >= shift, pltpu.roll(upto, shift, 1), 0.0)
            shift *= 2
        to_scalars.wait()
        begin = jnp.int32(0)
        starts = []
        for e in range(local):
            starts.append(begin.astype(F32))
            plan[local * (images + 1) + 2 * e] = begin
            first = begin
            for i in range(images):
                plan[e * (images + 1) + i] = begin
                begin = begin + count[e, i]
            plan[e * (images + 1) + images] = begin
            plan[local * (images + 1) + 2 * e + 1] = begin - first
            begin = first + (begin - first + 127) // 128 * 128 + 256
        start = jnp.zeros((8, total), F32)
        for e in range(local):
            start = jnp.where(expert_row == e, starts[e], start)
        slot = start + jnp.where(member > 0, upto, 0.0)
        slot0 = jnp.sum(jnp.where(is0, slot, 0.0), axis=0, keepdims=True) - 1.0
        slot1 = jnp.sum(jnp.where(is1, slot, 0.0), axis=0, keepdims=True) - 1.0
        slot = jnp.where(member > 0, slot - 1.0, -1.0)
        for i in range(images):
            place[i] = slot[:, i * ROWS : (i + 1) * ROWS]
        gates = jnp.where(is0, g0, jnp.where(is1, g1, 0.0))
        sign = jnp.where(is0, 1.0, jnp.where(is1, -1.0, 0.0))
        slot_rows = jnp.where(expert_row == 0, slot0, jnp.where(expert_row == 1, slot1, 0.0))
        stacked = jnp.concatenate([gates, sign, slot_rows, jnp.zeros((104, total), F32)], axis=0)
        lane128 = lax.broadcasted_iota(jnp.int32, (128, 128), 1)
        for at in range(0, total, 128):
            col = stacked[:, at : at + 128].T
            cols[at : at + 128] = col
            low = col - col.astype(BF).astype(F32)
            info = jnp.where(lane128 < 16, col, jnp.where(lane128 < 24, pltpu.roll(low, 16, 1), 0.0))
            ci[at : at + 128, D : D + 128] = info.astype(BF)

        row = lax.broadcasted_iota(jnp.int32, (128, ROWS), 0)
        head = lax.broadcasted_iota(jnp.int32, (16, 2 * D + 128), 0)

        def gather(i, _):
            rows = ci[pl.ds(pl.multiple_of(i * ROWS, 16), ROWS)]

            def part(w, _):
                picks = []
                for e in range(local):
                    at = window(e, i)[1] + 128 * w
                    picks.append(jnp.where(place[i, e : e + 1] == (at + row).astype(F32), 1.0, 0.0).astype(BF))
                found = dot(jnp.concatenate(picks, axis=0), rows).astype(BF)
                for e in range(local):
                    begin, at = window(e, i)
                    at = pl.multiple_of(at + 128 * w, 16)
                    old = xg[pl.ds(at, 16)]
                    new = found[e * 128 : e * 128 + 16]
                    xg[pl.ds(at, 16)] = jnp.where(at + head < begin, old, new)
                    xg[pl.ds(pl.multiple_of(at + 16, 16), 112)] = found[e * 128 + 16 : e * 128 + 128]
                return 0

            return lax.fori_loop(0, windows(i), part, 0)

        for load in loads[groups:]:
            load.wait()
        lax.fori_loop(0, images, gather, 0)
        for e in range(local):
            end, at = window(e, images)
            xg[pl.ds(at, 16)] = jnp.where(at + head < end, xg[pl.ds(at, 16)], jnp.zeros(head.shape, BF))
            xg[pl.ds(pl.multiple_of(at + 16, 16), 240)] = jnp.zeros((240, 2 * D + 128), BF)

    begin, n = plan[local * (images + 1) + 2 * step], plan[local * (images + 1) + 2 * step + 1]

    def tile(row, size):
        at = pl.multiple_of(begin + row, 16)
        here = pl.ds(pl.multiple_of(row, TILE // 4), size)
        lane = lax.broadcasted_iota(jnp.int32, (size, 128), 1)
        x = xg[pl.ds(at, size), 0:D]
        info = xg[pl.ds(at, size), D : D + 128].astype(F32)
        g4r = xg[pl.ds(at, size), D + 128 :].astype(F32)
        gate = jnp.sum(jnp.where((lane == step) | (lane == step + 16), info, 0.0), axis=-1, keepdims=True)
        sign = jnp.sum(jnp.where(lane == step + 8, info, 0.0), axis=-1, keepdims=True)
        dy = (gate * g4r).astype(BF)
        dy_scr[here] = dy
        for f in range(0, FF, 512):
            u, gp = gelu_parts(dot(x, win[0, :, f : f + 512]))
            u_scr[here, f : f + 512] = u.astype(BF)
            gp_scr[here, f : f + 512] = gp.astype(BF)
        ey = dot(u_scr[here], wout[0]).astype(BF).astype(F32)
        dg = sign * jnp.sum(g4r * ey, axis=-1, keepdims=True)
        for f in range(0, FF, 512):
            du = dot_t(dy, wout[0, f : f + 512])
            gp_scr[here, f : f + 512] = (du * gp_scr[here, f : f + 512].astype(F32)).astype(BF)
        dcp = dot_t(gp_scr[here], win[0])
        slots[pl.ds(at, size), 0:D] = (gate * ey).astype(BF)
        slots[pl.ds(at, size), D : 2 * D] = dcp.astype(BF)
        low = dg - dg.astype(BF).astype(F32)
        slots[pl.ds(at, size), 2 * D :] = jnp.where(lane == 0, dg, jnp.where(lane == 1, low, 0.0)).astype(BF)

    whole = (n + TILE // 4 - 1) // TILE

    def full_tile(j, _):
        tile(j * TILE, TILE)
        return 0

    lax.fori_loop(0, whole, full_tile, 0)

    for size in range(TILE // 4, TILE, TILE // 4):

        @pl.when((n > whole * TILE + size - TILE // 4) & (n <= whole * TILE + size))
        def _(size=size):
            tile(whole * TILE, size)
            rest = pl.ds(pl.multiple_of(whole * TILE + size, TILE // 4), TILE - size)
            for scratch in (dy_scr, u_scr, gp_scr):
                scratch[rest] = jnp.zeros((TILE - size,) + scratch.shape[1:], BF)

    after = pl.multiple_of(begin + (n + TILE // 4 - 1) // (TILE // 4) * (TILE // 4), 16)
    slots[pl.ds(after, 256)] = jnp.zeros((256, 2 * D + 128), BF)

    rounded = (n + TILE - 1) // TILE

    @pl.when(rounded == 0)
    def _():
        eg_ref[...] = jnp.zeros_like(eg_ref)

    for tiles in range(1, u_scr.shape[0] // TILE + 1):

        @pl.when(rounded == tiles)
        def _(depth=tiles * TILE):
            x = xg[pl.ds(pl.multiple_of(begin, 16), depth), 0:D]
            dy = dy_scr[0:depth]
            for f in range(0, FF, D):
                eg_ref[0, 0, f : f + D] = t_dot(gp_scr[0:depth, f : f + D], x).astype(BF)
                eg_ref[0, 1, f : f + D] = t_dot(u_scr[0:depth, f : f + D], dy).astype(BF)

    @pl.when(step == local - 1)
    def _():
        lane = lax.broadcasted_iota(jnp.int32, (ROWS, 128), 1)

        def out_copies(s, i, slot):
            rows = pl.ds(pl.multiple_of(i * ROWS, 16), ROWS)
            return [
                pltpu.make_async_copy(staged.at[slot, k], target.at[rows], out_sem.at[slot, k])
                for k, target in enumerate((y_refs[s], d_refs[s]))
            ]

        def restore(s, i):
            image = s * (n_tok // ROWS) + i
            at_rows = pl.multiple_of(image * ROWS, 16)
            slot0, slot1 = cols[pl.ds(at_rows, ROWS), 16:17], cols[pl.ds(at_rows, ROWS), 17:18]

            def part(w):
                picks = []
                for e in range(local):
                    at = pl.multiple_of(window(e, image)[1] + 128 * w, 16)
                    stack[e * 128 : (e + 1) * 128] = slots[pl.ds(at, 128)]
                    slot = (at + lane).astype(F32)
                    picks.append(jnp.where((slot0 == slot) | (slot1 == slot), 1.0, 0.0).astype(BF))
                return dot(jnp.concatenate(picks, axis=1), stack[...])

            back[...] = part(0)

            def more(w, _):
                back[...] += part(w)
                return 0

            lax.fori_loop(1, windows(image), more, 0)
            slot = lax.rem(image, 2)

            @pl.when(image >= 2)
            def _():
                for copy in out_copies(s, i, slot):
                    copy.wait()

            staged[slot, 0] = back[:, 0:D].astype(BF)
            staged[slot, 1] = back[:, D : 2 * D].astype(BF)
            for copy in out_copies(s, i, slot):
                copy.start()
            cols[pl.ds(at_rows, ROWS)] = back[:, 2 * D :]

        for s in range(groups):

            def one(i, _, s=s):
                restore(s, i)
                return 0

            lax.fori_loop(0, n_tok // ROWS, one, 0)
        for slot in range(2):
            for copy in out_copies(groups - 1, 0, slot):
                copy.wait()
        for at in range(0, total, 128):
            place_t = cols[at : at + 128].T[0:8]
            s, left = divmod(at, n_tok)
            here = min(128, n_tok - left)
            delta_refs[s][:, left : left + here] = place_t[:, 0:here]
            if here < 128:
                delta_refs[s + 1][:, 0 : 128 - here] = place_t[:, here:]


def experts_all(cs, gs, rs, router_t, win, wout, slots_most, owners):
    groups = len(cs)
    local = win.shape[0]
    n_tok = cs[0].shape[0]
    total = groups * n_tok
    images = total // ROWS
    room = -(-(slots_most + local * 384 + TILE) // 128) * 128
    width = 2 * D + 128
    deepest = -(-slots_most // local // TILE) * TILE

    def full(shape):
        return pl.BlockSpec(tuple(shape), lambda i: (0,) * len(shape))

    outs = [jax.ShapeDtypeStruct((local, 2, FF, D), BF)]
    outs += [jax.ShapeDtypeStruct((n_tok, D), BF)] * (2 * groups)
    outs += [jax.ShapeDtypeStruct((8, n_tok), F32)] * groups
    vm = pltpu.VMEM
    result = pl.pallas_call(
        functools.partial(experts_kernel, groups, local, "exp"),
        grid=(local,),
        out_shape=outs,
        in_specs=[pl.BlockSpec(memory_space=pl.ANY)] * (2 * groups)
        + [VMEM] * (groups + 1)
        + [pl.BlockSpec((1, D, FF), lambda i: (i, 0, 0)), pl.BlockSpec((1, FF, D), lambda i: (i, 0, 0))],
        out_specs=[pl.BlockSpec((1, 2, FF, D), lambda i: (i, 0, 0, 0))]
        + [pl.BlockSpec(memory_space=pl.ANY)] * (2 * groups)
        + [full(o.shape) for o in outs[2 * groups + 1 :]],
        scratch_shapes=[
            vm((total, width), BF),
            vm((total, 128), F32),
            vm((images, 8, ROWS), F32),
            vm((room, width), BF),
            vm((room, width), BF),
            vm((deepest, D), BF),
            vm((deepest, FF), BF),
            vm((deepest, FF), BF),
            vm((local * 128, width), BF),
            vm((ROWS, width), F32),
            vm((2, 2, ROWS, D), BF),
            vm((8, 128), jnp.int32),
            pltpu.SMEM((8, 128), jnp.int32),
            pltpu.SMEM((local * (images + 3),), jnp.int32),
            pltpu.SemaphoreType.DMA(()),
            pltpu.SemaphoreType.DMA((2 * groups,)),
            pltpu.SemaphoreType.DMA((2, 2)),
        ],
        compiler_params=pltpu.CompilerParams(vmem_limit_bytes=62 << 20),
        name="experts",
    )(*cs, *gs, *rs, router_t, win, wout)
    eg = result[0].reshape((local, 2) + owners + (FF // math.prod(owners), D))
    return eg, result[1 : groups + 1], result[groups + 1 : 2 * groups + 1], result[2 * groups + 1 :]


class Halving:
    def __init__(self, place, links, total, dims, order, received, lead=()):
        self.p, self.links, self.total, self.dims, self.order = place, links, total, dims, order
        self.received, self.lead = received, lead
        self.first = links.reserve(len(order) + 2 * order.count("z"))

    def where(self, fixed):
        return (slice(None),) * len(self.lead) + tuple(fixed.get(b, slice(None)) for b in self.dims)

    def copies(self, k):
        b = self.order[k]
        fixed = {q: self.p.bit[q] for q in self.order[:k]}
        if b == "z":
            return [
                self.links.copy(self.first + k + n, self.total.at[self.where({**fixed, **bits})], self.received[k].at[n], device)
                for n, (bits, device) in enumerate(self.p.others)
            ]
        fixed[b] = 1 - self.p.bit[b]
        return [self.links.copy(self.first + k, self.total.at[self.where(fixed)], self.received[k], self.p.partner[b])]

    def add(self, fixed, other, other_dims):
        free = [b for b in self.dims if b not in fixed]
        sizes = list(self.lead) + [2] * len(free)

        def block(i, _):
            at = []
            for size in reversed(sizes):
                at.insert(0, i % size)
                i = i // size
            full = dict(fixed, **dict(zip(free, at[len(self.lead) :])))
            mine = self.total.at[tuple(at[: len(self.lead)]) + tuple(full[b] for b in self.dims)]
            term = other.at[tuple(at[: len(self.lead)]) + tuple(full[b] for b in other_dims)]
            mine[...] = (mine[...].astype(F32) + term[...].astype(F32)).astype(BF)
            return 0

        lax.fori_loop(0, math.prod(sizes), block, 0)

    def step(self, k, other=None):
        fixed = {q: self.p.bit[q] for q in self.order[:k] if q != "z"}
        other_dims = [b for b in self.dims if b not in fixed]
        if k:
            for copy in self.copies(k - 1):
                copy.wait()
            other = self.received[k - 1]
        if k == len(self.order) and self.order[-1] == "z":
            mine = self.own()
            total = mine[...].astype(F32)
            for n in range(len(self.p.others)):
                total = total + other[n].astype(F32)
            mine[...] = total.astype(BF)
        elif k < len(self.order) and self.order[k] != "z":
            b = self.order[k]
            self.add(dict(fixed, **{b: 1 - self.p.bit[b]}), other, other_dims)
            self.copies(k)[0].start()
            self.add(dict(fixed, **{b: self.p.bit[b]}), other, other_dims)
        else:
            self.add(fixed, other, other_dims)
            if k < len(self.order):
                for copy in self.copies(k):
                    copy.start()

    def own(self):
        return self.total.at[self.where(self.p.bit)]


class ExpertSum:
    def __init__(self, place, links, j, slot, eg, own, part, received, order, out, local_sem):
        self.p, self.links, self.out = place, links, out.at[j]
        self.given = eg.at[j]
        self.mine = own.at[slot]
        self.load = pltpu.make_async_copy(self.given.at[:, :, :, :, place.bit["c"]], self.mine, local_sem.at[slot])
        self.core = links.copy(
            links.reserve(1), self.given.at[:, :, :, :, 1 - place.bit["c"]], part.at[j], place.partner["c"]
        )
        self.halving = Halving(place, links, part.at[j], "hlx", order, received, lead=(2,))

    def run(self, k):
        if k == 0:
            self.core.start()
            return
        if k == 1:
            self.load.wait()
            self.core.wait()
        self.halving.step(k - 1, self.mine)
        if k == 4:
            self.out[...] = self.halving.own()[...].astype(F32)


class SharedSum:
    def __init__(self, place, links, src, core_rx, received, order, out):
        self.p, self.links, self.order, self.out, self.core_rx = place, links, order, out, core_rx
        self.core = links.copy(links.reserve(1), src.at[1 - place.bit["c"]], core_rx, place.partner["c"])
        self.halving = Halving(place, links, src.at[place.bit["c"]], "yxhl", order, received)
        self.first = links.reserve(len(order) + 3)

    def back(self, k):
        known = "c" + self.order[: len(self.order) - k] if k <= len(self.order) else ""
        bits = known.replace("z", "hl")
        mine = self.out.at[tuple(self.p.bit[b] if b in bits else slice(None) for b in BITS)]
        if known[-1] == "z":
            return [self.links.copy(self.first + n, mine, mine, device) for n, (_, device) in enumerate(self.p.others)]
        return [self.links.copy(self.first + 2 + k, mine, mine, self.p.partner[known[-1]])]

    def run(self, k):
        n = len(self.order)
        if k == 0:
            self.core.start()
        elif k <= n:
            if k == 1:
                self.core.wait()
            self.halving.step(k - 1, self.core_rx)
        elif k == n + 1:
            self.halving.step(n)
            self.out[tuple(self.p.bit[b] for b in BITS)] = self.halving.own()[...]
            for copy in self.back(0):
                copy.start()
        else:
            for copy in self.back(k - n - 2):
                copy.wait()
            if k <= 2 * n + 1:
                for copy in self.back(k - n - 1):
                    copy.start()


class SmallSum:
    def __init__(self, place, links, src, rx):
        self.p, self.links, self.src, self.rx = place, links, src, rx
        self.first = links.reserve(len(BITS))

    def copy(self, k):
        return self.links.copy(self.first + k, self.src.at[k], self.rx.at[k], self.p.partner[BITS[k]])

    def run(self, k, out):
        if k:
            self.copy(k - 1).wait()
            total = self.src[k - 1] + self.rx[k - 1]
            if k == len(BITS):
                out[...] = total
                return
            self.src[k] = total
        self.copy(k).start()


GROUPS = ((48, "yxz"), (48, "xyz"), (48, "yxz"), (32, "yxz"), (16, "yxz"))
GROUP_ROWS = (0, 1536, 3072, 4608, 5632)
EXPERT_ORDERS = ("lhx", "xlh", "xlh", "xlh")

ORDER = (
    ("E", 3, 0), ("E", 0, 0), ("d", 0, 0), ("E", 1, 0), ("E", 2, 0), ("E", 3, 1), ("d", 1, 0), ("run", 0, 0),
    ("d", 2, 0), ("E", 0, 1), ("run", 1, 0), ("d", 3, 0), ("E", 1, 1), ("E", 2, 1), ("y", 0, 0), ("run", 2, 0),
    ("run", 3, 0), ("E", 3, 2), ("run", 4, 0), ("run", 5, 0), ("run", 6, 0), ("S", 0, 0), ("run", 7, 0),
    ("run", 8, 0), ("run", 9, 0), ("E", 0, 2), ("S", 0, 1), ("run", 10, 0), ("E", 1, 2), ("run", 11, 0),
    ("run", 12, 0), ("run", 13, 0), ("S", 1, 0), ("S", 2, 0), ("run", 14, 0), ("S", 0, 2), ("run", 15, 0),
    ("S", 2, 1), ("E", 3, 3), ("run", 16, 0), ("S", 1, 1), ("S", 0, 3), ("run", 17, 0), ("run", 18, 0), ("S", 4, 0),
    ("S", 3, 0), ("S", 2, 2), ("run", 19, 0), ("S", 4, 1), ("S", 1, 2), ("few", 0, 0), ("S", 0, 4), ("S", 3, 1),
    ("S", 2, 3), ("S", 4, 2), ("S", 0, 5), ("S", 4, 3), ("S", 1, 3), ("S", 3, 2), ("S", 2, 4), ("S", 0, 6),
    ("S", 3, 3), ("S", 1, 4), ("E", 3, 4), ("few", 1, 0), ("E", 0, 3), ("S", 3, 4), ("S", 4, 4), ("S", 2, 5),
    ("E", 2, 2), ("few", 2, 0), ("E", 1, 3), ("S", 1, 5), ("S", 3, 5), ("S", 2, 6), ("S", 4, 5), ("E", 0, 4),
    ("few", 3, 0), ("S", 1, 6), ("run", 20, 0), ("S", 3, 6), ("S", 4, 6), ("E", 2, 3), ("S", 1, 7), ("few", 4, 0),
    ("S", 2, 7), ("E", 1, 4), ("S", 3, 7), ("S", 0, 7), ("S", 1, 8), ("S", 4, 7), ("S", 3, 8), ("S", 2, 8),
    ("S", 0, 8), ("E", 2, 4), ("S", 4, 8), ("few", 5, 0),
)

LOADED = ("c", "x3", "cot", "d", "delta", "x2", "qkv", "o", "p", "wo", "wqkv", "x1", "wout", "gp", "u", "win", "y", "x0")
EARLY = 10


def bwd_kernel(linked, *refs):
    names = ["gains", "router_t", "routes", "wqkv", "wo", "win", "wout", "x0", "x1", "x2", "x3", "qkv1", "qkv2"]
    names += ["o1", "o2", "p1", "p2", "u", "gp", "c", "cot", "d", "delta", "y"]
    if linked:
        names += ["d_send", "delta_send", "y_send", "eg"]
    names += ["act_out", "gin_out", "small_out"]
    if linked:
        names += ["eg_out"] + ["out" + str(g) for g in range(len(GROUPS))]
    else:
        names += ["shared_out"]
    names += ["v_" + n for n in LOADED] + ["gv", "a_scr", "dbr_scr", "dqkv_scr", "sem"]
    names += ["v_act", "v_gin", "leave_sem"]
    if linked:
        names += ["v_eg"] + ["v_out" + str(g) for g in range(len(GROUPS))]
    if linked:
        names += ["d_rx", "delta_rx", "y_rx", "own", "part", "small_src", "small_rx", "eg_sem", "send", "recv"]
        names += ["src" + str(g) for g in range(len(GROUPS))]
        names += ["rx" + str(g) + str(k) for g, (_, order) in enumerate(GROUPS) for k in range(len(order) + 1)]
        names += ["erx" + str(j) + str(k) for j in range(len(EXPERT_ORDERS)) for k in range(3)]
    r = dict(zip(names, refs, strict=True))
    gains, gv, a_scr, dbr_scr, dqkv_scr = (r[n] for n in ("gains", "gv", "a_scr", "dbr_scr", "dqkv_scr"))
    images = gv.shape[0]
    m = images * ROWS
    lo = lane_low(ROWS)

    second = {"qkv": "qkv2", "o": "o2", "p": "p2"}
    copies = {}

    def fetch(name, source):
        copies[name] = pltpu.make_async_copy(r[source], r["v_" + name], r["sem"].at[LOADED.index(name)])
        copies[name].start()

    def need(*wanted):
        for name in wanted:
            copies[name].wait()

    leaving = []

    def leave(source, target):
        leaving.append(pltpu.make_async_copy(source, target, r["leave_sem"].at[len(leaving)]))
        leaving[-1].start()

    if linked:
        place = Place()
        links = Links(r["send"], r["recv"])
        partners = [place.partner[b] for b in "cyx"] + [device for _, device in place.others]
        place.greet(partners)
        place.meet(partners)
        beside = place.partner["y"]
        delta_copy = links.copy(links.reserve(1), r["delta_send"], r["delta_rx"], beside)
        delta_copy.start()
        d_first = links.reserve(images)

        def d_copy(i):
            return links.copy(d_first + i, r["d_send"].at[i], r["d_rx"].at[i], beside)

        turn = [at for kind, at, what in ORDER if (kind, what) == ("E", 1)]
        experts = [
            ExpertSum(
                place, links, j, turn.index(j) % 2, r["eg"], r["own"], r["part"], [r["erx" + str(j) + str(k)] for k in range(3)],
                order, r["v_eg"], r["eg_sem"],
            )
            for j, order in enumerate(EXPERT_ORDERS)
        ]
        experts[turn[0]].load.start()
        experts[turn[1]].load.start()
        y_copy = links.copy(links.reserve(1), r["y_send"], r["y_rx"], beside)
        sums = []
        for g, (_, order) in enumerate(GROUPS):
            rx = [r["rx" + str(g) + str(k)] for k in range(len(order) + 1)]
            sums.append(SharedSum(place, links, r["src" + str(g)], rx[0], rx[1:], order, r["v_out" + str(g)]))
        few = SmallSum(place, links, r["small_src"], r["small_rx"])
        small = r["small_src"].at[0]
        small[...] = jnp.zeros(small.shape, F32)
    else:
        small = r["small_out"]
    for name in LOADED[:EARLY]:
        fetch(name, second.get(name, name))

    def keep(block, value):
        value = value.astype(BF)
        if not linked:
            r["shared_out"][block] = value
            return
        row, end = block * D, block * D + D
        for g, (share, _) in enumerate(GROUPS):
            base, cell = GROUP_ROWS[g], 4 * share
            for q in range(8):
                at = base + q * cell
                if row <= at and at + cell <= end:
                    part = value[at - row : at - row + cell]
                    r["src" + str(g)][q // 4, q // 2 % 2, q % 2] = part.reshape(2, 2, share, D)

    def router():
        need("c", "delta")
        c_all = r["v_c"][...].reshape(m, D)
        g0, g1, first, other = gate_rows(r["router_t"][...], c_all, r["routes"][...])
        delta = r["v_delta"][0:1] + r["v_delta"][1:2]
        if linked:
            delta_copy.wait()
            delta = delta + (r["delta_rx"][0:1] + r["delta_rx"][1:2])
        dl = g0 * g1 * delta
        dlog = jnp.where(first, dl, jnp.where(other, -dl, 0.0)).astype(BF)
        small[4 : 4 + dlog.shape[0]] = dot(dlog, c_all)
        small[0:4] = jnp.zeros((4, D), F32)
        gv[...] = t_dot(dlog, r["router_t"][...]).reshape(images, ROWS, D)
        need("x3", "cot", "d")

    def add_gain(row, by_gain):
        small[row : row + 1] += jnp.sum(by_gain, axis=0, keepdims=True)

    def first(i):
        dc = gv[i] + r["v_d"][i].astype(F32)
        if linked:
            d_copy(i).wait()
            dc = dc + r["d_rx"][i].astype(F32)
        dx, by_gain = norm_back(dc, r["v_x3"][i], gains[3:4])
        gv[i] = r["v_cot"][i].astype(F32) + dx
        add_gain(3, by_gain)
        if i == 0:
            need("x2", "qkv", "o", "p", "wo")
            for name in LOADED[EARLY:]:
                fetch(name, name)
        attend_image(i, 1, gains[2:3], r["v_x2"])

    def attend_image(i, layer, gain, x):
        qkv, o, p = r["v_qkv"], r["v_o"], r["v_p"]
        a_scr[i] = (norm_parts(x[i].astype(F32))[0] * gain).astype(BF)
        dbr = gv[i].astype(BF)
        dbr_scr[i] = dbr
        do = dot_t(dbr, r["v_wo"][layer]).astype(BF)
        dod = do.astype(F32) * o[i].astype(F32)
        for pair in range(HEADS // 2):
            at = 128 * pair
            q = qkv[i, :, at : at + 128] * BF(0.125)
            k = qkv[i, :, D + at : D + at + 128]
            w = qkv[i, :, 2 * D + at : 2 * D + at + 128]
            dqs, dk, dw = [], 0.0, 0.0
            for h in range(2):
                mask = lo if h == 0 else ~lo
                dom = jnp.where(mask, do[:, at : at + 128], BF(0))
                inner = jnp.sum(jnp.where(mask, dod[:, at : at + 128], 0.0), axis=-1, keepdims=True)
                ph = p[i, 2 * pair + h]
                ds = (ph.astype(F32) * (dot_t(dom, w) - inner)).astype(BF)
                dw = dw + t_dot(ph, dom)
                dqs.append(dot(ds, k))
                dk = dk + t_dot(ds, jnp.where(mask, q, BF(0)))
            dqkv_scr[i, :, at : at + 128] = (jnp.where(lo, dqs[0], dqs[1]) * 0.125).astype(BF)
            dqkv_scr[i, :, D + at : D + at + 128] = dk.astype(BF)
            dqkv_scr[i, :, 2 * D + at : 2 * D + at + 128] = dw.astype(BF)

    def attend_weights(block):
        a_all = a_scr[...].reshape(m, D)
        for f in range(3):
            keep(block + f, t_dot(a_all, dqkv_scr[:, :, f * D : f * D + D].reshape(m, D)))
        keep(block + 3, t_dot(r["v_o"][...].reshape(m, D), dbr_scr[...].reshape(m, D)))

    def close(x, layer, row, out):
        def image(i, _):
            da = dot_t(dqkv_scr[i], r["v_wqkv"][layer])
            dx, by_gain = norm_back(da, x[i].astype(F32), gains[row : row + 1])
            out[i] = gv[i] + dx
            add_gain(row, by_gain)
            return 0

        lax.fori_loop(0, images, image, 0)

    def first_close():
        for name in ("qkv", "o", "p"):
            fetch(name, name + "1")
        need("wqkv")
        close(r["v_x2"], 1, 2, gv)
        need("x1", "wout", "gp", "u", "win")

    gp = r["v_gp"]

    def mlp(i):
        a_scr[i] = (norm_parts(r["v_x1"][i])[0] * gains[1:2]).astype(BF)
        dm = gv[i].astype(BF)
        dbr_scr[i] = dm
        for f in range(0, FF, 512):
            du = dot_t(dm, r["v_wout"][f : f + 512])
            gp[i, :, f : f + 512] = (du * gp[i, :, f : f + 512].astype(F32)).astype(BF)

    def mlp_out_weights():
        dm_all = dbr_scr[...].reshape(m, D)
        for f in range(4):
            keep(4 + f, t_dot(r["v_u"][:, :, f * D : f * D + D].reshape(m, D), dm_all))

    def mlp_in_weights():
        b_all = a_scr[...].reshape(m, D)
        for f in range(4):
            keep(8 + f, t_dot(b_all, gp[:, :, f * D : f * D + D].reshape(m, D)))

    def mlp_close():
        def image(i, _):
            db = dot_t(gp[i], r["v_win"][...])
            dx, by_gain = norm_back(db, r["v_x1"][i], gains[1:2])
            gv[i] = gv[i] + dx
            add_gain(1, by_gain)
            return 0

        lax.fori_loop(0, images, image, 0)
        need("x0", "qkv", "o", "p")

    def last(i):
        attend_image(i, 0, gains[0:1], r["v_x0"])

    def last_close():
        close(r["v_x0"], 0, 0, r["v_gin"])
        leave(r["v_gin"], r["gin_out"])

    def act():
        need("y")
        if linked:
            y_copy.wait()
        for i in range(images):
            x4 = r["v_x3"][i] + r["v_y"][i].astype(F32)
            if linked:
                x4 = x4 + r["y_rx"][i].astype(F32)
            r["v_act"][i] = x4.astype(BF)
        leave(r["v_act"], r["act_out"])

    compute = [router] + [functools.partial(first, i) for i in range(images)]
    compute += [lambda: attend_weights(0), first_close] + [functools.partial(mlp, i) for i in range(images)]
    compute += [mlp_out_weights, mlp_in_weights, mlp_close] + [functools.partial(last, i) for i in range(images)]
    compute += [lambda: attend_weights(12), last_close, act]
    if not linked:
        for step in compute:
            step()
        for copy in leaving:
            copy.wait()
        return
    done = 0
    for kind, at, what in ORDER:
        if kind == "run":
            compute[done]()
            done += 1
        elif kind == "d":
            d_copy(at).start()
        elif kind == "y":
            y_copy.start()
        elif kind == "few":
            few.run(at, r["small_out"])
        elif kind == "E":
            experts[at].run(what)
            if what == 4:
                leave(r["v_eg"].at[at], r["eg_out"].at[at])
            if what == 1 and turn.index(at) + 2 < len(turn):
                experts[turn[turn.index(at) + 2]].load.start()
        else:
            sums[at].run(what)
            if what == 2 * len(GROUPS[at][1]) + 2:
                leave(r["v_out" + str(at)], r["out" + str(at)])
    for copy in leaving:
        copy.wait()


def dense_backward(weights, router_t, routes, saved, cot, d, delta, y, sent=None):
    gains, wqkv, wo, win, wout = weights
    x0, x1, x2, x3, qkv1, qkv2, o1, o2, p1, p2, u, gp, c = saved
    images = x0.shape[0]
    linked = sent is not None
    small_rows = 16 if linked else 4 + router_t.shape[0]
    ins = [gains, router_t, routes, wqkv, wo, win, wout, *saved, cot, d, delta, y] + (list(sent) if linked else [])
    outs = [
        jax.ShapeDtypeStruct((images, ROWS, D), BF),
        jax.ShapeDtypeStruct((images, ROWS, D), F32),
        jax.ShapeDtypeStruct((small_rows, D), F32),
    ]
    if not linked:
        outs.append(jax.ShapeDtypeStruct((16, D, D), BF))
    vm = pltpu.VMEM
    loaded = dict(
        c=c, x3=x3, cot=cot, d=d, delta=delta, x2=x2, qkv=qkv1, o=o1, p=p1, wo=wo, wqkv=wqkv, x1=x1, wout=wout,
        gp=gp, u=u, win=win, y=y, x0=x0,
    )
    scratch = [vm(loaded[name].shape, loaded[name].dtype) for name in LOADED]
    scratch += [vm((images, ROWS, D), F32), vm((images, ROWS, D), BF), vm((images, ROWS, D), BF)]
    scratch += [vm((images, ROWS, 3 * D), BF), pltpu.SemaphoreType.DMA((len(LOADED),))]
    leavers = 2 + (sent[-1].shape[0] + len(GROUPS) if linked else 0)
    scratch += [vm((images, ROWS, D), BF), vm((images, ROWS, D), F32), pltpu.SemaphoreType.DMA((leavers,))]
    params = dict(vmem_limit_bytes=62 << 20)
    if linked:
        eg = sent[-1]
        local, share = eg.shape[0], eg.shape[-2]
        outs.append(jax.ShapeDtypeStruct((local, 2, share, D), F32))
        outs += [jax.ShapeDtypeStruct((2,) * 5 + (rows, D), BF) for rows, _ in GROUPS]
        copies = 2 + images + 4 * local + 15 * len(GROUPS) + len(BITS)
        scratch += [vm((local, 2, share, D), F32)] + [vm((2,) * 5 + (rows, D), BF) for rows, _ in GROUPS]
        scratch += [vm(d.shape, BF), vm(delta.shape, F32), vm(y.shape, BF)]
        scratch += [
            vm((2, 2, 2, 2, 2, share, D), BF),
            vm((local, 2, 2, 2, 2, share, D), BF),
            vm((len(BITS), small_rows, D), F32),
            vm((len(BITS), small_rows, D), F32),
            pltpu.SemaphoreType.DMA((2,)),
            pltpu.SemaphoreType.DMA((copies,)),
            pltpu.SemaphoreType.DMA((copies,)),
        ]
        scratch += [vm((2,) * 5 + (rows, D), BF) for rows, _ in GROUPS]
        for rows, order in GROUPS:
            scratch += [vm((2,) * (4 - k) + (rows, D), BF) for k in range(len(order.strip("z")) + 1)]
            if "z" in order:
                scratch.append(vm((3, rows, D), BF))
        scratch += [vm((2,) * (3 - k) + (share, D), BF) for _ in EXPERT_ORDERS for k in range(3)]
        params.update(collective_id=1, has_side_effects=True)
    far = pl.BlockSpec(memory_space=pl.ANY)
    out_specs = [far, far, VMEM] + [far if linked else VMEM] * (len(outs) - 3)
    return pl.pallas_call(
        functools.partial(bwd_kernel, linked),
        out_shape=outs,
        in_specs=[VMEM] * 3 + [pl.BlockSpec(memory_space=pl.ANY)] * (len(ins) - 3),
        out_specs=out_specs,
        scratch_shapes=scratch,
        compiler_params=pltpu.CompilerParams(**params),
        name="dense_backward",
    )(*ins)


def finish_kernel(n_shared, act, gin, small, eg, *refs):
    shared, refs = refs[:n_shared], refs[n_shared:]
    act_out, gin_out, qkv_out, proj_out, gain_out, mlp_in_out, mlp_out_out, router_out, in_out, out_out = refs[:10]
    v_shared, v_qkv, v_proj, v_mlp_in, v_mlp_out, v_gin, v_act, in_sem, out_sem = refs[10:]
    images = act.shape[0]
    blocks = v_shared.shape[0] // D
    targets = {3: v_proj.at[1], 15: v_proj.at[0]}
    for f in range(3):
        targets[f] = v_qkv.at[1, :, pl.ds(f * D, D)]
        targets[12 + f] = v_qkv.at[0, :, pl.ds(f * D, D)]
    for f in range(4):
        targets[4 + f] = v_mlp_out.at[pl.ds(f * D, D)]
        targets[8 + f] = v_mlp_in.at[:, pl.ds(f * D, D)]
    wholes = {2: (v_qkv.at[1], qkv_out.at[1]), 7: (v_mlp_out, mlp_out_out), 11: (v_mlp_in, mlp_in_out)}
    wholes.update({14: (v_qkv.at[0], qkv_out.at[0]), 15: (v_proj, proj_out)})
    stores = {}
    for k, (b, (source, target)) in enumerate(wholes.items()):
        stores[b] = pltpu.make_async_copy(source, target, out_sem.at[k])
    loads, at = [], 0
    for k, part in enumerate(shared):
        rows = part.shape[0]
        loads.append((at, pltpu.make_async_copy(part, v_shared.at[pl.ds(at, rows)], in_sem.at[k])))
        at += rows
    load_gin = pltpu.make_async_copy(gin, v_gin, in_sem.at[n_shared])
    load_act = pltpu.make_async_copy(act, v_act, in_sem.at[n_shared + 1])
    for _, load in loads:
        load.start()
    load_gin.start()
    load_act.start()

    waited = 0
    for b in range(blocks):
        while waited < n_shared and loads[waited][0] < (b + 1) * D:
            loads[waited][1].wait()
            waited += 1
        targets[b][...] = v_shared[b * D : (b + 1) * D].astype(F32)
        if b in stores:
            stores[b].start()
    gain_out[...] = small[0:4]
    router_out[...] = small[4 : 4 + router_out.shape[0]]
    for e in range(eg.shape[0]):
        in_out[e] = eg[e, 0]
        out_out[e] = eg[e, 1]
    load_gin.wait()
    load_act.wait()
    for i in range(images):
        gin_out[i * PATCHES : (i + 1) * PATCHES] = v_act[i, 0:PATCHES].astype(F32)
    act_out[...] = gin_out[...].astype(BF)
    for i in range(images):
        gin_out[i * PATCHES : (i + 1) * PATCHES] = v_gin[i, 0:PATCHES]
    for store in stores.values():
        store.wait()


def finish(act, gin, shared, small, eg, experts):
    images, local, share = act.shape[0], eg.shape[0], eg.shape[2]
    row_count = images * PATCHES
    blocks = 16
    outs = [
        jax.ShapeDtypeStruct((row_count, D), BF),
        jax.ShapeDtypeStruct((row_count, D), F32),
        jax.ShapeDtypeStruct((2, D, 3 * D), F32),
        jax.ShapeDtypeStruct((2, D, D), F32),
        jax.ShapeDtypeStruct((4, D), F32),
        jax.ShapeDtypeStruct((D, FF), F32),
        jax.ShapeDtypeStruct((FF, D), F32),
        jax.ShapeDtypeStruct((experts, D), F32),
        jax.ShapeDtypeStruct((local, share, D), F32),
        jax.ShapeDtypeStruct((local, share, D), F32),
    ]
    far = pl.BlockSpec(memory_space=pl.ANY)
    return pl.pallas_call(
        functools.partial(finish_kernel, len(shared)),
        out_shape=outs,
        in_specs=[far, far, VMEM, VMEM] + [far] * len(shared),
        out_specs=[VMEM, VMEM, far, far, VMEM, far, far, VMEM, VMEM, VMEM],
        scratch_shapes=[
            pltpu.VMEM((blocks * D, D), BF),
            pltpu.VMEM((2, D, 3 * D), F32),
            pltpu.VMEM((2, D, D), F32),
            pltpu.VMEM((D, FF), F32),
            pltpu.VMEM((FF, D), F32),
            pltpu.VMEM(gin.shape, F32),
            pltpu.VMEM(act.shape, BF),
            pltpu.SemaphoreType.DMA((len(shared) + 2,)),
            pltpu.SemaphoreType.DMA((5,)),
        ],
        compiler_params=pltpu.CompilerParams(vmem_limit_bytes=62 << 20),
        name="finish",
    )(act, gin, small, eg, *shared)


def from_peer(array, groups, shift):
    return lax.ppermute(array, "exp", [(i, (i + shift) % groups) for i in range(groups)])


def shards(
    tokens, routes, norm_gains, attn_qkv, attn_out, mlp_in, mlp_out, router, experts_in, experts_out, cotangent
):
    row_count = tokens.shape[0]
    groups = lax.axis_size("exp")
    local = experts_in.shape[0]
    choices = routes.shape[1]
    capacity = 2 * choices * row_count // (local * groups)
    images = row_count // PATCHES
    router_t = router.T
    rep = lax.axis_size("rep")
    known = (rep, groups, local) == (16, 2, 4)
    owners = (2, 2, 2, 2) if known else (rep,)
    routes_t, x0, cot, x1, x2, x3, qkv1, qkv2, o1, o2, p1, p2, u, gp, c, *received = dense_forward(
        tokens, cotangent, routes.T, norm_gains, attn_qkv, attn_out, mlp_in, mlp_out, known
    )

    def of_all(mine, place):
        if known:
            others = [received[place]]
        else:
            others = [from_peer(mine, groups, k) for k in range(1, groups)]
        return [part.reshape(-1, part.shape[-1]) for part in [mine] + others]

    cs, gs, rs = of_all(c, 0), of_all(cot, 1), of_all(routes_t, 2)
    eg, ys, ds, deltas = experts_all(
        cs, gs, rs, router_t, experts_in, experts_out, local * capacity * groups, owners
    )

    weights = (norm_gains, attn_qkv, attn_out, mlp_in, mlp_out)
    saved = (x0, x1, x2, x3, qkv1, qkv2, o1, o2, p1, p2, u, gp, c)
    by_image = (images, ROWS, D)
    experts = router_t.shape[0]
    if known:
        sent = (ds[1].reshape(by_image), deltas[1], ys[1].reshape(by_image), eg)
        act, gin, small, eg, *shared = dense_backward(
            weights, router_t, routes_t, saved, cot, ds[0].reshape(by_image), deltas[0], ys[0].reshape(by_image), sent
        )
        shared = [part.reshape(-1, D) for part in shared]
    else:

        def back(parts):
            total = parts[0].astype(F32)
            for k in range(1, groups):
                total = total + from_peer(parts[k], groups, groups - k).astype(F32)
            return total

        d, delta, y = back(ds).astype(BF), back(deltas), back(ys).astype(BF)
        act, gin, small, shared = dense_backward(
            weights, router_t, routes_t, saved, cot, d.reshape(by_image), delta, y.reshape(by_image)
        )
        eg = lax.psum_scatter(eg, "rep", scatter_dimension=2, tiled=True).reshape(local, 2, FF // rep, D).astype(F32)
        shared, small = lax.psum((shared, small), ("rep", "exp"))
        shared = [shared.reshape(-1, D)]
    outs = list(finish(act, gin, shared, small, eg, experts))
    outs[7] = outs[7].T
    outs[8] = jnp.swapaxes(outs[8], 1, 2)
    return tuple(outs)


def solution(mesh):
    rows = P(("rep", "exp"), None)
    return jax.shard_map(
        shards,
        mesh=mesh,
        in_specs=(rows, rows, P(), P(), P(), P(), P(), P(), P("exp", None, None), P("exp", None, None), rows),
        out_specs=(rows, rows, P(), P(), P(), P(), P(), P(), P("exp", None, "rep"), P("exp", "rep", None)),
        check_vma=False,
    )
```
